32 devices in a mesh: dp: 8 (over z, y), fsdp: 4 (over x, core).
Axes of the slice: x: 2, y: 2, z: 4, core: 2. Of those that a mesh axis runs over, the one named last changes fastest.
Arguments:
- tokens: bfloat16 [32768, 512], P(('dp', 'fsdp')), may hold values from -6 to 6
- memory: bfloat16 [32768, 512], P(('dp', 'fsdp')), may hold values from -6 to 6
- token_seg: int32 [32, 1024], P(('dp', 'fsdp')), may hold values from 0 to 7, never falling along the last dimension, each value on 1 to 512 neighbouring positions
- token_pad: int32 [32, 1024], P(('dp', 'fsdp')), may hold values 0 or 1
- memory_seg: int32 [32, 1024], P(('dp', 'fsdp')), may hold values from 0 to 7, as said below
- memory_pad: int32 [32, 1024], P(('dp', 'fsdp')), may hold values from 0 to 1, as said below
- out_grad: bfloat16 [32768, 512], P(('dp', 'fsdp')), may hold values from -6 to 6
- self_q_w: bfloat16 [512, 512], P(('dp', 'fsdp')), may hold values from -0.25 to 0.25
- self_q_b: bfloat16 [512], P(('dp', 'fsdp')), may hold values from -1.75 to 1.75
- self_k_w: bfloat16 [512, 512], P(('dp', 'fsdp')), may hold values from -0.25 to 0.25
- self_v_w: bfloat16 [512, 512], P(('dp', 'fsdp')), may hold values from -0.25 to 0.25
- self_v_b: bfloat16 [512], P(('dp', 'fsdp')), may hold values from -1.75 to 1.75
- self_o_w: bfloat16 [512, 512], P(('dp', 'fsdp')), may hold values from -0.75 to 0.75
- self_o_b: bfloat16 [512], P(('dp', 'fsdp')), may hold values from -1.75 to 1.75
- norm1_gain: bfloat16 [512], P(('dp', 'fsdp')), may hold values from 0.25 to 1.75
- norm1_bias: bfloat16 [512], P(('dp', 'fsdp')), may hold values from -1.75 to 1.75
- cross_q_w: bfloat16 [512, 512], P(('dp', 'fsdp')), may hold values from -0.25 to 0.25
- cross_q_b: bfloat16 [512], P(('dp', 'fsdp')), may hold values from -1.75 to 1.75
- cross_k_w: bfloat16 [512, 512], P(('dp', 'fsdp')), may hold values from -0.25 to 0.25
- cross_v_w: bfloat16 [512, 512], P(('dp', 'fsdp')), may hold values from -0.25 to 0.25
- cross_v_b: bfloat16 [512], P(('dp', 'fsdp')), may hold values from -1.75 to 1.75
- cross_o_w: bfloat16 [512, 512], P(('dp', 'fsdp')), may hold values from -0.75 to 0.75
- cross_o_b: bfloat16 [512], P(('dp', 'fsdp')), may hold values from -1.75 to 1.75
- norm2_gain: bfloat16 [512], P(('dp', 'fsdp')), may hold values from 0.25 to 1.75
- norm2_bias: bfloat16 [512], P(('dp', 'fsdp')), may hold values from -1.75 to 1.75
- ffn_in_w: bfloat16 [512, 2048], P(('dp', 'fsdp')), may hold values from -0.25 to 0.25
- ffn_in_b: bfloat16 [2048], P(('dp', 'fsdp')), may hold values from -1.75 to 1.75
- ffn_out_w: bfloat16 [2048, 512], P(('dp', 'fsdp')), may hold values from -0.125 to 0.125
- ffn_out_b: bfloat16 [512], P(('dp', 'fsdp')), may hold values from -1.75 to 1.75
- norm3_gain: bfloat16 [512], P(('dp', 'fsdp')), may hold values from 0.25 to 1.75
- norm3_bias: bfloat16 [512], P(('dp', 'fsdp')), may hold values from -1.75 to 1.75
Outputs:
- layer_out: bfloat16 [32768, 512], P(('dp', 'fsdp'))
- tokens_grad: bfloat16 [32768, 512], P(('dp', 'fsdp'))
- memory_grad: bfloat16 [32768, 512], P(('dp', 'fsdp'))
- grad_self_q_w: float32 [512, 512], P(('dp', 'fsdp'))
- grad_self_q_b: float32 [512], P(('dp', 'fsdp'))
- grad_self_k_w: float32 [512, 512], P(('dp', 'fsdp'))
- grad_self_v_w: float32 [512, 512], P(('dp', 'fsdp'))
- grad_self_v_b: float32 [512], P(('dp', 'fsdp'))
- grad_self_o_w: float32 [512, 512], P(('dp', 'fsdp'))
- grad_self_o_b: float32 [512], P(('dp', 'fsdp'))
- grad_norm1_gain: float32 [512], P(('dp', 'fsdp'))
- grad_norm1_bias: float32 [512], P(('dp', 'fsdp'))
- grad_cross_q_w: float32 [512, 512], P(('dp', 'fsdp'))
- grad_cross_q_b: float32 [512], P(('dp', 'fsdp'))
- grad_cross_k_w: float32 [512, 512], P(('dp', 'fsdp'))
- grad_cross_v_w: float32 [512, 512], P(('dp', 'fsdp'))
- grad_cross_v_b: float32 [512], P(('dp', 'fsdp'))
- grad_cross_o_w: float32 [512, 512], P(('dp', 'fsdp'))
- grad_cross_o_b: float32 [512], P(('dp', 'fsdp'))
- grad_norm2_gain: float32 [512], P(('dp', 'fsdp'))
- grad_norm2_bias: float32 [512], P(('dp', 'fsdp'))
- grad_ffn_in_w: float32 [512, 2048], P(('dp', 'fsdp'))
- grad_ffn_in_b: float32 [2048], P(('dp', 'fsdp'))
- grad_ffn_out_w: float32 [2048, 512], P(('dp', 'fsdp'))
- grad_ffn_out_b: float32 [512], P(('dp', 'fsdp'))
- grad_norm3_gain: float32 [512], P(('dp', 'fsdp'))
- grad_norm3_bias: float32 [512], P(('dp', 'fsdp'))
The draws below stay inside these ranges and needn't reach their ends.
Inputs may be any that keep to these rules, and one draw needn't show every extreme that they name: `memory_seg`: in each row the memory ids never fall and every id of 0 to 7 occurs. `memory_pad`: the first memory position of each document is never padding.
All inputs are finite; a program needn't handle non-finite values. No bound on the sum of `token_pad` on one device may be relied on, other than what follows from the above.
Results may differ from the reference program's by a relative error of at most 0.02.
Values may be sent and summed in bfloat16 or wider, within the bound.
A program may use at most 192 MiB of HBM per device.

```python
import math
import jax
import jax.numpy as jnp
import numpy as np
from jax import lax

D = 512
HEADS = 8
HEAD_DIM = 64
FF = 2048
LEN = 1024
MEM_LEN = 1024
DOCS = 8
ROWS = 32
TOKENS = 32768
MEMS = 32768


def memory_layout(key):
    positions = jnp.arange(MEM_LEN)

    def per_row(row_key):
        cut_points = jax.random.permutation(row_key, MEM_LEN - 1)[:DOCS - 1] + 1
        return jnp.sum((cut_points[None, :] <= positions[:, None]).astype(jnp.int32), axis=1).astype(jnp.int32)
    row_keys = jax.random.split(key, ROWS)
    return jax.vmap(per_row)(row_keys)


def draw_memory_seg(key, part):
    segment_ids = memory_layout(key)
    return segment_ids


def draw_memory_pad(key, part):
    segment_ids = memory_layout(key)
    key = jax.random.fold_in(key, 17)
    random_bits = jax.random.randint(key, (ROWS, MEM_LEN), 0, 8)
    doc_start = jnp.concatenate([jnp.ones((ROWS, 1), bool), segment_ids[:, 1:] != segment_ids[:, :-1]], axis=1)
    return jnp.where((random_bits == 0) & ~doc_start, 1, 0).astype(jnp.int32)


def set_ends(values, rng, least, largest):
    shape = values.shape
    index_at = [jax.random.randint(jax.random.fold_in(rng, axis), (), 0, shape[axis]) for axis in range(len(shape))]
    values = values.at[tuple(index_at)].set(least)
    longest = shape.index(max(shape))
    index_at[longest] = (index_at[longest] + 1) % shape[longest]
    return values.at[tuple(index_at)].set(largest)


def shard_levels(stream_key, shape, shards, low, high):
    loudness, own = 1.0, jax.random.fold_in(stream_key, 6)
    for position, shards_of in shards:
        steps = jnp.exp(jax.random.uniform(jax.random.fold_in(own, position), (shards_of,), jnp.float32, low / len(shards), high / len(shards)))
        loudness = loudness * jnp.repeat(steps, shape[position] // shards_of).reshape([-1 if axis == position else 1 for axis in range(len(shape))])
    return loudness


def split_up(amount, total, most, slope):
    loads = [(1 << 20) // math.isqrt(standing ** slope) + 1 for standing in range(2, amount + 1)]
    spare, counts = total - most - (amount - 1), [1] * (amount - 1)
    while spare > 0:
        candidates = [i for i in range(amount - 1) if counts[i] < most]
        mass, remaining = sum([loads[i] for i in candidates]), spare
        for i in candidates:
            addition = min(most - counts[i], max(1, remaining * loads[i] // mass), spare)
            counts[i] = counts[i] + addition
            spare = spare - addition
    return np.array([most] + counts)


def ragged_sizes(rng, count, total, reach, skew):
    if count == 2:
        one = jax.random.randint(rng, (), max(1, total - reach), min(reach, total - 1) + 1)
        return jnp.stack([one, total - one])
    sizes = jnp.asarray(split_up(count, total, reach, skew), jnp.int32)
    twos = (count - 1) // 2
    source_of, sink = sizes[1:1 + 2 * twos:2], sizes[2:2 + 2 * twos:2]
    room = jnp.minimum(source_of - 1, reach - sink)
    shifted = jax.random.randint(jax.random.fold_in(rng, 1), (twos,), 0, 1 << 20) % (room + 1)
    sizes = sizes.at[1:1 + 2 * twos:2].set(source_of - shifted).at[2:2 + 2 * twos:2].set(sink + shifted)
    return sizes[jax.random.permutation(jax.random.fold_in(rng, 2), count)]


def normal_values(rng, extent, deviation, reach, cuts=(), kind=jnp.bfloat16):
    values = jax.random.normal(rng, extent, jnp.float32) * deviation
    if len(cuts) > 0:
        values = shard_levels(rng, extent, cuts, -0.22, 0.18) * values
    return jnp.clip(values, min=-reach, max=reach).astype(kind)


def setup_inputs(seed: int = 0) -> dict:
    key_of = jax.random.split(jax.random.key(seed), 32)
    tokens = normal_values(key_of[0], (TOKENS, D), 1.0, 6.0, ((0, 32),))
    memory = normal_values(key_of[1], (MEMS, D), 1.0, 6.0, ((0, 32),))
    token_seg = jax.vmap(lambda own: jnp.searchsorted(jnp.cumsum(ragged_sizes(own, DOCS, LEN, LEN // 2, 1)), jnp.arange(LEN), side="right"))(jax.random.split(key_of[2], ROWS)).reshape((ROWS, LEN)).astype(jnp.int32)
    token_pad = set_ends((jax.random.randint(key_of[3], (ROWS, LEN), 0, 8) < 1).astype(jnp.int32), jax.random.fold_in(key_of[3], 1), 0, 1)
    memory_seg = draw_memory_seg(jax.random.fold_in(key_of[31], 71), 0)
    memory_pad = draw_memory_pad(jax.random.fold_in(key_of[31], 71), 0)
    out_grad = normal_values(key_of[6], (TOKENS, D), 1.0, 6.0, ((0, 32),))
    self_q_w = normal_values(key_of[7], (D, D), D ** -0.5, 0.25, ((0, 32),))
    self_q_b = normal_values(key_of[8], (D,), 0.3, 1.75, ((0, 32),))
    self_k_w = normal_values(key_of[9], (D, D), D ** -0.5, 0.25, ((0, 32),))
    self_v_w = normal_values(key_of[10], (D, D), D ** -0.5, 0.25, ((0, 32),))
    self_v_b = normal_values(key_of[11], (D,), 0.3, 1.75, ((0, 32),))
    self_o_w = normal_values(key_of[12], (D, D), (D // 8) ** -0.5, 0.75, ((0, 32),))
    self_o_b = normal_values(key_of[13], (D,), 0.3, 1.75, ((0, 32),))
    norm1_gain = jnp.clip(1.0 + 0.15 * jax.random.normal(key_of[14], (D,), jnp.float32), 0.25, 1.75).astype(jnp.bfloat16)
    norm1_bias = normal_values(key_of[15], (D,), 0.3, 1.75, ((0, 32),))
    cross_q_w = normal_values(key_of[16], (D, D), D ** -0.5, 0.25, ((0, 32),))
    cross_q_b = normal_values(key_of[17], (D,), 0.3, 1.75, ((0, 32),))
    cross_k_w = normal_values(key_of[18], (D, D), D ** -0.5, 0.25, ((0, 32),))
    cross_v_w = normal_values(key_of[19], (D, D), D ** -0.5, 0.25, ((0, 32),))
    cross_v_b = normal_values(key_of[20], (D,), 0.3, 1.75, ((0, 32),))
    cross_o_w = normal_values(key_of[21], (D, D), (D // 8) ** -0.5, 0.75, ((0, 32),))
    cross_o_b = normal_values(key_of[22], (D,), 0.3, 1.75, ((0, 32),))
    norm2_gain = jnp.clip(1.0 + 0.15 * jax.random.normal(key_of[23], (D,), jnp.float32), 0.25, 1.75).astype(jnp.bfloat16)
    norm2_bias = normal_values(key_of[24], (D,), 0.3, 1.75, ((0, 32),))
    ffn_in_w = normal_values(key_of[25], (D, FF), D ** -0.5, 0.25, ((0, 32),))
    ffn_in_b = normal_values(key_of[26], (FF,), 0.3, 1.75, ((0, 32),))
    ffn_out_w = normal_values(key_of[27], (FF, D), FF ** -0.5, 0.125, ((0, 32),))
    ffn_out_b = normal_values(key_of[28], (D,), 0.3, 1.75, ((0, 32),))
    norm3_gain = jnp.clip(1.0 + 0.15 * jax.random.normal(key_of[29], (D,), jnp.float32), 0.25, 1.75).astype(jnp.bfloat16)
    norm3_bias = normal_values(key_of[30], (D,), 0.3, 1.75, ((0, 32),))
    return {"tokens": tokens, "memory": memory, "token_seg": token_seg, "token_pad": token_pad, "memory_seg": memory_seg, "memory_pad": memory_pad, "out_grad": out_grad, "self_q_w": self_q_w, "self_q_b": self_q_b, "self_k_w": self_k_w, "self_v_w": self_v_w, "self_v_b": self_v_b, "self_o_w": self_o_w, "self_o_b": self_o_b, "norm1_gain": norm1_gain, "norm1_bias": norm1_bias, "cross_q_w": cross_q_w, "cross_q_b": cross_q_b, "cross_k_w": cross_k_w, "cross_v_w": cross_v_w, "cross_v_b": cross_v_b, "cross_o_w": cross_o_w, "cross_o_b": cross_o_b, "norm2_gain": norm2_gain, "norm2_bias": norm2_bias, "ffn_in_w": ffn_in_w, "ffn_in_b": ffn_in_b, "ffn_out_w": ffn_out_w, "ffn_out_b": ffn_out_b, "norm3_gain": norm3_gain, "norm3_bias": norm3_bias}


EPSILON = 1e-05
MASKED = -1e+30

@jax.custom_vjp
def low(v):
    return lax.optimization_barrier(v.astype(jnp.bfloat16)).astype(jnp.float32)

@jax.custom_vjp
def low_back(v):
    return v

def low_keep(v):
    return (low(v), None)

def low_pass(kept, grad):
    return (grad,)

def back_keep(v):
    return (v, None)

def back_low(kept, grad):
    return (low(grad),)
low.defvjp(low_keep, low_pass)
low_back.defvjp(back_keep, back_low)

def matmul(left, right):
    return jnp.dot(left, right, precision=lax.Precision.HIGHEST, preferred_element_type=jnp.float32)

def layer_norm(values_in, gain_vec, shift_vec):
    center = values_in - lax.optimization_barrier(jnp.mean(values_in, axis=-1, keepdims=True))
    spread = lax.optimization_barrier(jnp.mean(center * center, axis=-1, keepdims=True))
    return center * lax.rsqrt(spread + EPSILON) * gain_vec + shift_vec

def attend(query_rows, key_rows, value_rows, query_seg, key_seg, key_pad, causal):
    length = query_rows.shape[0]
    block_size = min(512, length)
    block_count = length // block_size
    score_scale = HEAD_DIM ** (-0.5)
    key_pos = jnp.arange(key_rows.shape[0])

    def per_block(pieces):
        block_q, block_seg, block_pos = pieces
        same_doc = block_seg[:, None] == key_seg[None, :]
        open_keys = key_pad[None, :] == 0
        if causal:
            allowed_keys = same_doc & (key_pos[None, :] <= block_pos[:, None]) & (open_keys | (key_pos[None, :] == block_pos[:, None]))
        else:
            allowed_keys = same_doc & open_keys
        raw_scores = low_back(jnp.einsum('qhd,khd->hqk', block_q, key_rows, precision=lax.Precision.HIGHEST) * score_scale)
        prob_rows = jax.nn.softmax(jnp.where(allowed_keys[None], raw_scores, MASKED), axis=-1)
        return jnp.einsum('hqk,khd->qhd', low(prob_rows), value_rows, precision=lax.Precision.HIGHEST)
    attended = lax.map(jax.checkpoint(per_block), (query_rows.reshape(block_count, block_size, HEADS, HEAD_DIM), query_seg.reshape(block_count, block_size), jnp.arange(length).reshape(block_count, block_size)))
    return attended.reshape(length, HEADS * HEAD_DIM)

def split_heads(array_in):
    return array_in.reshape(array_in.shape[0], HEADS, HEAD_DIM)

def attention_block(weight_set, inputs, source, residual, query_seg, key_seg, key_pad, causal):
    query_w, query_b, key_w, value_w, value_b, output_w, output_b, norm_gain, norm_shift = weight_set
    query_rows = low_back(low(matmul(inputs, query_w) + query_b))
    key_rows = low_back(low(matmul(source, key_w)))
    value_rows = low_back(low(matmul(source, value_w) + value_b))
    attended = attend(split_heads(query_rows), split_heads(key_rows), split_heads(value_rows), query_seg, key_seg, key_pad, causal)
    attended = low_back(low(attended))
    summed = residual + low_back(matmul(attended, output_w)) + output_b
    return layer_norm(summed, norm_gain, norm_shift)

def row_forward(params, row_in, row_mem, row_seg, row_pad, mem_seg, mem_pad):
    first_norm = attention_block(params[0:9], row_in, row_in, row_in, row_seg, row_seg, row_pad, True)
    second_norm = attention_block(params[9:18], low(first_norm), row_mem, first_norm, row_seg, mem_seg, mem_pad, False)
    in_w, in_b, out_w, out_b, norm_gain, norm_shift = params[18:24]
    hidden = low_back(matmul(low(second_norm), in_w) + in_b)
    active = low(jax.nn.gelu(hidden, approximate=False))
    summed = second_norm + low_back(matmul(active, out_w)) + out_b
    return layer_norm(summed, norm_gain, norm_shift)

def reference(tokens, memory, token_seg, token_pad, memory_seg, memory_pad, out_grad, self_q_w, self_q_b, self_k_w, self_v_w, self_v_b, self_o_w, self_o_b, norm1_gain, norm1_bias, cross_q_w, cross_q_b, cross_k_w, cross_v_w, cross_v_b, cross_o_w, cross_o_b, norm2_gain, norm2_bias, ffn_in_w, ffn_in_b, ffn_out_w, ffn_out_b, norm3_gain, norm3_bias):
    raw_params = (self_q_w, self_q_b, self_k_w, self_v_w, self_v_b, self_o_w, self_o_b, norm1_gain, norm1_bias, cross_q_w, cross_q_b, cross_k_w, cross_v_w, cross_v_b, cross_o_w, cross_o_b, norm2_gain, norm2_bias, ffn_in_w, ffn_in_b, ffn_out_w, ffn_out_b, norm3_gain, norm3_bias)
    params = jax.tree.map(lambda leaf: leaf.astype(jnp.float32), raw_params)
    rows_in = tokens.astype(jnp.float32).reshape(ROWS, LEN, D)
    rows_mem = memory.astype(jnp.float32).reshape(ROWS, MEM_LEN, D)

    def forward(params, rows_in, rows_mem):

        def per_row(state_in, pieces):
            return (state_in, row_forward(params, pieces[0], pieces[1], pieces[2], pieces[3], pieces[4], pieces[5]))
        _, layer_rows = lax.scan(per_row, jnp.zeros((), jnp.float32), (rows_in, rows_mem, token_seg, token_pad, memory_seg, memory_pad))
        return layer_rows
    layer_rows, pullback = jax.vjp(forward, params, rows_in, rows_mem)
    grad_params, grad_rows, grad_mem = pullback(out_grad.astype(jnp.float32).reshape(ROWS, LEN, D))
    return (layer_rows.reshape(TOKENS, D).astype(jnp.bfloat16), grad_rows.reshape(TOKENS, D).astype(jnp.bfloat16), grad_mem.reshape(MEMS, D).astype(jnp.bfloat16), grad_params[0], grad_params[1], grad_params[2], grad_params[3], grad_params[4], grad_params[5], grad_params[6], grad_params[7], grad_params[8], grad_params[9], grad_params[10], grad_params[11], grad_params[12], grad_params[13], grad_params[14], grad_params[15], grad_params[16], grad_params[17], grad_params[18], grad_params[19], grad_params[20], grad_params[21], grad_params[22], grad_params[23])
```

```python
from functools import partial

import jax
import jax.numpy as jnp
from jax import lax
from jax.experimental import pallas as pl
from jax.experimental.pallas import tpu as pltpu
from jax.sharding import PartitionSpec as P

HEADS = 8
EPSILON = 1e-05
MASKED = -1e30
AXES = ("dp", "fsdp")
MESH = pl.DeviceIdType.MESH
BF16 = jnp.bfloat16
F32 = jnp.float32
BLOCK = 256
VMEM_LIMIT = 58 << 20

(SELF_Q_B, SELF_V_B, SELF_O_B, NORM1_G, NORM1_B, CROSS_Q_B, CROSS_V_B, CROSS_O_B,
 NORM2_G, NORM2_B, FFN_OUT_B, NORM3_G, NORM3_B) = range(13)
FFN_IN_B = 15

BITS = ("zh", "zl", "y", "x", "c")
ORDERS = {
    "A": ("zh", "zl", "x", "y", "c"),
    "B": ("zh", "zl", "y", "x", "c"),
    "C": ("x", "zh", "zl", "y", "c"),
    "D": ("y", "zh", "zl", "x", "c"),
}
UNIT_ORDERS = "CDACDBCDACDBCDAB"
LAG = 4
UNITS = 16


def dot(left, right):
    return jnp.dot(left, right, preferred_element_type=F32)


def dot_nt(left, right):
    return lax.dot_general(left, right, (((1,), (1,)), ((), ())), preferred_element_type=F32)


def dot_tn(left, right):
    return lax.dot_general(left, right, (((0,), (0,)), ((), ())), preferred_element_type=F32)


def rows_at(index, size):
    return pl.ds(pl.multiple_of(index * size, size), size)


def loop(low, high, body):
    def step(index, carry):
        body(index)
        return carry

    lax.fori_loop(low, high, step, 0)


def whole(shape):
    return pl.BlockSpec(memory_space=pltpu.VMEM)


def any_space():
    return pl.BlockSpec(memory_space=pl.ANY)


def place():
    d = lax.axis_index("dp")
    f = lax.axis_index("fsdp")
    return d, f, {"zh": d // 4, "zl": (d // 2) % 2, "y": d % 2, "x": f // 2, "c": f % 2}


def flip(value, mask):
    return value + mask - 2 * mask * ((value // mask) % 2)


def partner(bit, d, f):
    return {
        "zh": (flip(d, 4), f),
        "zl": (flip(d, 2), f),
        "y": (flip(d, 1), f),
        "x": (d, flip(f, 2)),
        "c": (d, flip(f, 1)),
    }[bit]


def greet(d, f):
    barrier = pltpu.get_barrier_semaphore()
    for bit in BITS:
        pl.semaphore_signal(barrier, inc=1, device_id=partner(bit, d, f), device_id_type=MESH)
    pl.semaphore_wait(barrier, len(BITS))


def spread_vectors(packed, vec_ref, in_b_ref):
    flat = packed.reshape(512, 128)
    lane = lax.broadcasted_iota(jnp.int32, (128, 512), 0)
    column = lax.broadcasted_iota(jnp.int32, (128, 512), 1)
    pick = jnp.where((lane == column % 16) & (lane < 16), 1.0, 0.0).astype(BF16)
    spread = dot(flat, pick)
    row = lax.broadcasted_iota(jnp.int32, (512, 512), 0)
    col = lax.broadcasted_iota(jnp.int32, (512, 512), 1)
    kept = jnp.where(row // 16 == col // 16, spread, 0.0)
    vec_ref[...] = jnp.sum(kept.reshape(32, 16, 512), axis=0)
    device = lax.broadcasted_iota(jnp.int32, (32, 512), 0)
    source = lax.broadcasted_iota(jnp.int32, (32, 512), 1)
    choose = jnp.where(source == device * 16 + FFN_IN_B, 1.0, 0.0).astype(BF16)
    own = dot(choose, flat).astype(BF16)
    lane = lax.broadcasted_iota(jnp.int32, (128, 2048), 0)
    column = lax.broadcasted_iota(jnp.int32, (128, 2048), 1)
    pick = jnp.where((lane == column % 64) & (lane < 64), 1.0, 0.0).astype(BF16)
    spread = dot(own, pick)
    row = lax.broadcasted_iota(jnp.int32, (32, 2048), 0)
    col = lax.broadcasted_iota(jnp.int32, (32, 2048), 1)
    in_b_ref[...] = jnp.sum(jnp.where(row == col // 64, spread, 0.0), axis=0, keepdims=True)


def project(x_ref, weight, bias, out_ref, out_t_ref, scale=None):
    count = x_ref.shape[0] // BLOCK

    def body(i):
        rows = rows_at(i, BLOCK)
        value = dot(x_ref[rows, :], weight)
        if bias is not None:
            value = value + bias
        value = value.astype(BF16)
        if scale is not None:
            value = value * scale
        out_ref[rows, :] = value
        if out_t_ref is not None:
            out_t_ref[:, rows] = value.T

    loop(0, count, body)


PROJECTED = 9


def project_unit(unit, x_ref, m_ref, weight, vec_ref, outs):
    q, k, kt, v, vt, ck, ckt, cv, cvt = outs
    if unit == 0:
        project(x_ref, weight, vec_ref[SELF_Q_B : SELF_Q_B + 1, :], q, None, 0.125)
    if unit == 1:
        project(x_ref, weight, None, k, kt)
    if unit == 2:
        project(x_ref, weight, vec_ref[SELF_V_B : SELF_V_B + 1, :], v, vt)
    if unit == 5:
        project(m_ref, weight, None, ck, ckt)
    if unit == 6:
        project(m_ref, weight, vec_ref[CROSS_V_B : CROSS_V_B + 1, :], cv, cvt)


def gather_kernel(*refs):
    x_ref, m_ref, packed = refs[:3]
    shards = refs[3:13]
    o_s, o_c, o_i, o_o, vec_out, in_b_out = refs[13:19]
    outs = refs[19 : 19 + PROJECTED]
    rest = refs[19 + PROJECTED :]
    b_s, b_c, b_i, b_o, b_v = rest[:5]
    held = rest[5 : 5 + PROJECTED]
    send, recv, keep, done = rest[5 + PROJECTED :]
    d, f, me = place()
    own = tuple(me[bit] for bit in BITS)
    for i in range(4):
        b_s[own + (slice(None), slice(512 * i, 512 * i + 512))] = shards[i][...]
        b_c[own + (slice(None), slice(512 * i, 512 * i + 512))] = shards[4 + i][...]
    b_i[own] = shards[8][...]
    b_o[own] = shards[9][...]
    b_v[own] = packed[...]
    greet(d, f)

    buffers = [b_s] * 4 + [b_c] * 4 + [b_i] * 4 + [b_o] * 4 + [b_v]
    targets = [o_s] * 4 + [o_c] * 4 + [o_i] * 4 + [o_o] * 4

    def part(u, index):
        if u == UNITS:
            return index
        if buffers[u] is b_o:
            return index + (slice(16 * (u % 4), 16 * (u % 4) + 16), slice(None))
        return index + (slice(None), slice(512 * (u % 4), 512 * (u % 4) + 512))

    def copy(u, s):
        order = ORDERS["A" if u == UNITS else UNIT_ORDERS[u]]
        have = order[:s]
        index = part(u, tuple(slice(None) if bit in have else me[bit] for bit in BITS))
        return pltpu.make_async_remote_copy(
            src_ref=buffers[u].at[index],
            dst_ref=buffers[u].at[index],
            send_sem=send.at[u, s],
            recv_sem=recv.at[u, s],
            device_id=partner(order[s], d, f),
            device_id_type=MESH,
        )

    def put(u):
        index = part(u, (slice(None),) * 5)
        return pltpu.make_async_copy(buffers[u].at[index], targets[u].at[index], keep.at[u])

    def finished(u):
        if u == UNITS:
            spread_vectors(b_v[...].reshape(32, 16, 128), vec_out, in_b_out)
            return
        put(u).start()
        if u in (0, 1, 2, 5, 6):
            weight = buffers[u][part(u, (slice(None),) * 5)].reshape(512, 512)
            project_unit(u, x_ref, m_ref, weight, vec_out, held)

    steps = [(-2 + LAG * s, -s, UNITS, s) for s in range(6)]
    steps += [(u + LAG * s, -s, u, s) for u in range(UNITS) for s in range(6)]
    for _, _, u, s in sorted(steps):
        if s > 0:
            copy(u, s - 1).wait_recv()
        if s < 5:
            copy(u, s).start()
        else:
            finished(u)
    results = [
        pltpu.make_async_copy(held[i], outs[i], done.at[i]) for i in range(PROJECTED)
    ]
    for result in results:
        result.start()
    for u in range(UNITS + 1):
        for s in range(5):
            copy(u, s).wait_send()
        if u < UNITS:
            put(u).wait()
    for result in results:
        result.wait()


def gather(tokens, memory, packed, shards):
    rows, width = tokens.shape
    bits = (2,) * 5
    weights = [bits + (16, 2048)] * 3 + [bits + (64, 512)]
    straight, turned = (rows, width), (width, rows)
    projected = [straight, straight, turned, straight, turned, straight, turned, straight, turned]
    shapes = [jax.ShapeDtypeStruct(s, BF16) for s in weights]
    shapes += [jax.ShapeDtypeStruct((16, 512), F32), jax.ShapeDtypeStruct((1, 2048), F32)]
    shapes += [jax.ShapeDtypeStruct(s, BF16) for s in projected]
    result = pl.pallas_call(
        gather_kernel,
        out_shape=shapes,
        in_specs=[whole(None)] * 13,
        out_specs=[any_space()] * 4 + [whole(None)] * 2 + [any_space()] * PROJECTED,
        scratch_shapes=[pltpu.VMEM(s, BF16) for s in weights]
        + [pltpu.VMEM(bits + (16, 128), BF16)]
        + [pltpu.VMEM(s, BF16) for s in projected]
        + [
            pltpu.SemaphoreType.DMA((UNITS + 1, 5)),
            pltpu.SemaphoreType.DMA((UNITS + 1, 5)),
            pltpu.SemaphoreType.DMA((UNITS,)),
            pltpu.SemaphoreType.DMA((PROJECTED,)),
        ],
        compiler_params=pltpu.CompilerParams(
            collective_id=1, has_side_effects=True, vmem_limit_bytes=VMEM_LIMIT
        ),
        name="gather_project",
    )(tokens, memory, packed, *shards)
    w_s, w_c, w_i = (w.reshape(512, 2048) for w in result[:3])
    return w_s, w_c, w_i, result[3].reshape(2048, 512), result[4], result[5], result[6:]


def project_kernel(*refs):
    x_ref, m_ref, vec_ref, w_s, w_c = refs[:5]
    outs = refs[5:]
    for unit in (0, 1, 2, 5, 6):
        source = w_s if unit < 4 else w_c
        weight = source[:, 512 * (unit % 4) : 512 * (unit % 4) + 512]
        project_unit(unit, x_ref, m_ref, weight, vec_ref, outs)


def project_only(tokens, memory, vec, w_s, w_c):
    rows, width = tokens.shape
    straight, turned = (rows, width), (width, rows)
    projected = [straight, straight, turned, straight, turned, straight, turned, straight, turned]
    return pl.pallas_call(
        project_kernel,
        out_shape=[jax.ShapeDtypeStruct(s, BF16) for s in projected],
        in_specs=[whole(None)] * 5,
        out_specs=[whole(None)] * PROJECTED,
        compiler_params=pltpu.CompilerParams(vmem_limit_bytes=VMEM_LIMIT),
        name="project",
    )(tokens, memory, vec, w_s, w_c)


def lower_bound(seg_ref, value):
    last = seg_ref.shape[1] - 1

    def step(_, carry):
        low, high = carry
        middle = jnp.minimum((low + high) // 2, last)
        below = seg_ref[0, middle] < value
        return (jnp.where(below, middle + 1, low), jnp.where(below, high, middle))

    steps = (last + 1).bit_length()
    return lax.fori_loop(0, steps, step, (jnp.int32(0), jnp.int32(last + 1)))[0]


def key_blocks(query_seg, key_seg, block, causal):
    first = query_seg[0, block * BLOCK]
    low = lower_bound(key_seg, first) // BLOCK
    if causal:
        return low, block + 1
    last = query_seg[0, block * BLOCK + BLOCK - 1]
    high = (lower_bound(key_seg, last + 1) + BLOCK - 1) // BLOCK
    return low, high


def key_columns(seg_ref, pad_ref, column_ref):
    open_seg = jnp.where(pad_ref[...] == 0, seg_ref[...], -1).astype(F32)
    for i in range(seg_ref.shape[1] // 128):
        piece = jnp.broadcast_to(open_seg[:, 128 * i : 128 * i + 128], (128, 128)).T
        column_ref[128 * i : 128 * i + 128, :] = piece


def mask_block(bias_ref, column_ref, seg_ref, qb, kb, causal):
    query = seg_ref[:, rows_at(qb, BLOCK)].astype(F32)
    column = column_ref[rows_at(kb, BLOCK), :]
    allowed = jnp.concatenate([column] * (BLOCK // 128), axis=1) == query
    if causal:
        key_pos = kb * BLOCK + lax.broadcasted_iota(jnp.int32, (BLOCK, BLOCK), 0)
        query_pos = qb * BLOCK + lax.broadcasted_iota(jnp.int32, (BLOCK, BLOCK), 1)
        allowed = (allowed & (key_pos < query_pos)) | (key_pos == query_pos)
    bias_ref[...] = jnp.where(allowed, 0.0, MASKED)


def own_lanes(value, head):
    lane = lax.broadcasted_iota(jnp.int32, value.shape, 1)
    return jnp.where(lane // 64 == head, value, jnp.zeros_like(value))


def attend(q_ref, k_ref, vt_ref, seg_ref, column_ref, seg_s, key_seg_s, causal, out_ref, lse_ref,
           bias_ref, acc_ref, top_ref, sum_ref):
    def query_block(qb):
        rows = rows_at(qb, BLOCK)
        acc_ref[...] = jnp.zeros_like(acc_ref)
        top_ref[...] = jnp.full_like(top_ref, MASKED)
        sum_ref[...] = jnp.zeros_like(sum_ref)
        low, high = key_blocks(seg_s, key_seg_s, qb, causal)

        def key_block(kb):
            keys = rows_at(kb, BLOCK)
            mask_block(bias_ref, column_ref, seg_ref, qb, kb, causal)
            for slab in range(2):
                lanes = slice(256 * slab, 256 * slab + 256)
                key = k_ref[keys, lanes]
                query = q_ref[rows, lanes]
                for h in range(4):
                    head = 4 * slab + h
                    mine = slice(head, head + 1)
                    part = slice(64 * head, 64 * head + 64)
                    scores = dot_nt(key, own_lanes(query, h)) + bias_ref[...]
                    top = top_ref[mine, :]
                    new_top = jnp.maximum(top, jnp.max(scores, axis=0, keepdims=True))
                    prob = jnp.exp(scores - new_top)
                    fade = jnp.exp(top - new_top)
                    top_ref[mine, :] = new_top
                    sum_ref[mine, :] = sum_ref[mine, :] * fade + jnp.sum(prob, axis=0, keepdims=True)
                    acc_ref[part, :] = acc_ref[part, :] * fade + dot(vt_ref[part, keys], prob.astype(BF16))

        loop(low, high, key_block)
        total = sum_ref[...]
        lse_ref[:, rows] = top_ref[...] + jnp.log(total)
        scale = 1.0 / total
        for head in range(HEADS):
            part = slice(64 * head, 64 * head + 64)
            acc_ref[part, :] = acc_ref[part, :] * scale[head : head + 1, :]
        out_ref[rows, :] = acc_ref[...].astype(BF16).T

    loop(0, q_ref.shape[0] // BLOCK, query_block)


def attend_back(q_ref, k_ref, kt_ref, v_ref, g_ref, lse_ref, delta_ref, seg_ref, column_ref, seg_s,
                key_seg_s, causal, bias_ref, dqt_ref, dk_ref, dv_ref):
    dk_ref[...] = jnp.zeros_like(dk_ref)
    dv_ref[...] = jnp.zeros_like(dv_ref)
    dqt_ref[...] = jnp.zeros_like(dqt_ref)

    def query_block(qb):
        rows = rows_at(qb, BLOCK)
        low, high = key_blocks(seg_s, key_seg_s, qb, causal)

        def key_block(kb):
            keys = rows_at(kb, BLOCK)
            mask_block(bias_ref, column_ref, seg_ref, qb, kb, causal)
            for slab in range(2):
                lanes = slice(256 * slab, 256 * slab + 256)
                key = k_ref[keys, lanes]
                value = v_ref[keys, lanes]
                dk = dk_ref[keys, lanes]
                dv = dv_ref[keys, lanes]
                for h in range(4):
                    head = 4 * slab + h
                    mine = slice(head, head + 1)
                    part = slice(64 * head, 64 * head + 64)
                    query = own_lanes(q_ref[rows, lanes], h)
                    grad = own_lanes(g_ref[rows, lanes], h)
                    scores = dot_nt(key, query) + bias_ref[...]
                    prob = jnp.exp(scores - lse_ref[mine, rows])
                    prob_grad = dot_nt(value, grad)
                    score_grad = (prob * (prob_grad - delta_ref[mine, rows])).astype(BF16)
                    dv = dv + dot(prob.astype(BF16), grad)
                    dk = dk + dot(score_grad, query)
                    dqt_ref[part, rows] += dot(kt_ref[part, keys], score_grad)
                dk_ref[keys, lanes] = dk
                dv_ref[keys, lanes] = dv

        loop(low, high, key_block)

    loop(0, q_ref.shape[0] // BLOCK, query_block)


def normalize(summed):
    center = summed - jnp.mean(summed, axis=-1, keepdims=True)
    spread = jnp.mean(center * center, axis=-1, keepdims=True)
    inverse = lax.rsqrt(spread + EPSILON)
    return center * inverse, inverse


def normalize_back(grad, gain, normal, inverse):
    scaled = grad * gain
    mean = jnp.mean(scaled, axis=-1, keepdims=True)
    along = jnp.mean(scaled * normal, axis=-1, keepdims=True)
    return inverse * (scaled - mean - normal * along)


def column_sum(value):
    return jnp.sum(value, axis=0, keepdims=True)


def gelu_and_slope(hidden):
    size = jnp.abs(hidden) * (0.5 ** 0.5)
    t = 1.0 / (1.0 + 0.3275911 * size)
    bell = jnp.exp(-0.5 * hidden * hidden)
    poly = 1.061405429
    for c in (-1.453152027, 1.421413741, -0.284496736, 0.254829592):
        poly = poly * t + c
    tail = (0.5 * t) * poly * bell
    phi = jnp.where(hidden < 0.0, tail, 1.0 - tail)
    return hidden * phi, phi + hidden * (bell * 0.3989422804014327)


def row_delta(grad, mixed):
    head = lax.broadcasted_iota(jnp.int32, (16, 512), 0)
    lane = lax.broadcasted_iota(jnp.int32, (16, 512), 1)
    pick = jnp.where(lane // 64 == head, 1.0, 0.0).astype(BF16)
    product = grad.astype(F32) * mixed.astype(F32)
    high = product.astype(BF16)
    low = (product - high.astype(F32)).astype(BF16)
    return (dot_nt(pick, high) + dot_nt(pick, low))[:HEADS, :]


N_MIDDLE_IN = 29


def middle_kernel(*refs):
    (seg, pad, mseg, mpad, seg_s, mseg_s, vec, in_b, x_ref, q, k, vt) = refs[:12]
    late_in = refs[12:23]
    layer_out, first_low_out, grads_out, vec_grad, in_b_grad = refs[23:28]
    late_out = refs[28:36]
    scratch = refs[36:]
    late = scratch[:11]
    (kt, v, ck, ckt, cv, cvt, w_s, w_c, w_i, w_o, out_grad) = late
    (column, mcolumn, bias, acc, top, total, mixed, cmixed, lse, clse, delta, first_sum, first_norm,
     first_low, cq, second_low, d_second, d_low, active, slope, dqt, dv, low_a, grads,
     late_sem, out_sem) = scratch[11:]
    dk, low_b, low_c = first_norm, out_grad, d_low
    pieces = [buffer.at[:, 512 * i : 512 * i + 512] for buffer in (active, slope) for i in range(4)]
    dcq_o, dck_o, dcv_o, memory_grad, dq_o, dk_o, dv_o, tokens_grad = pieces
    copies = [pltpu.make_async_copy(late_in[i], late[i], late_sem.at[i]) for i in range(11)]
    for i in (6, 2, 5, 7, 8, 9, 10, 3, 4, 0, 1):
        copies[i].start()
    rows_total = x_ref.shape[0]
    blocks = rows_total // BLOCK

    def vector(index):
        return vec[index : index + 1, :]

    def add_vec(index, value):
        vec_grad[index : index + 1, :] += value

    vec_grad[...] = jnp.zeros_like(vec_grad)
    in_b_grad[...] = jnp.zeros_like(in_b_grad)
    key_columns(seg, pad, column)
    key_columns(mseg, mpad, mcolumn)

    attend(q, k, vt, seg, column, seg_s, seg_s, True, mixed, lse, bias, acc, top, total)
    copies[6].wait()
    copies[7].wait()

    def first(i):
        rows = rows_at(i, BLOCK)
        summed = x_ref[rows, :].astype(F32) + dot(mixed[rows, :], w_s[:, 1536:2048]) + vector(SELF_O_B)
        first_sum[rows, :] = summed
        normal, _ = normalize(summed)
        norm = normal * vector(NORM1_G) + vector(NORM1_B)
        first_norm[rows, :] = norm
        low = norm.astype(BF16)
        first_low[rows, :] = low
        query = (dot(low, w_c[:, 0:512]) + vector(CROSS_Q_B)).astype(BF16)
        cq[rows, :] = query * 0.125

    loop(0, blocks, first)
    first_low_copy = pltpu.make_async_copy(first_low, first_low_out, out_sem.at[0])
    first_low_copy.start()
    copies[2].wait()
    copies[5].wait()
    attend(cq, ck, cvt, seg, mcolumn, seg_s, mseg_s, False, cmixed, clse, bias, acc, top, total)
    copies[8].wait()
    copies[9].wait()
    copies[10].wait()

    def ffn(i):
        rows = rows_at(i, BLOCK)
        summed = first_norm[rows, :] + dot(cmixed[rows, :], w_c[:, 1536:2048]) + vector(CROSS_O_B)
        normal2, inverse2 = normalize(summed)
        second = normal2 * vector(NORM2_G) + vector(NORM2_B)
        low = second.astype(BF16)
        second_low[rows, :] = low
        third = second + vector(FFN_OUT_B)
        for c in range(4):
            cols = slice(512 * c, 512 * c + 512)
            hidden = dot(low, w_i[:, cols]) + in_b[:, cols]
            act, slant = gelu_and_slope(hidden)
            act = act.astype(BF16)
            active[rows, cols] = act
            slope[rows, cols] = slant.astype(BF16)
            third = third + dot(act, w_o[cols, :])
        normal3, inverse3 = normalize(third)
        layer_out[rows, :] = (normal3 * vector(NORM3_G) + vector(NORM3_B)).astype(BF16)
        grad = out_grad[rows, :].astype(F32)
        add_vec(NORM3_G, column_sum(grad * normal3))
        add_vec(NORM3_B, column_sum(grad))
        d_third = normalize_back(grad, vector(NORM3_G), normal3, inverse3)
        add_vec(FFN_OUT_B, column_sum(d_third))
        third_low = d_third.astype(BF16)
        d_low[rows, :] = third_low
        back = d_third
        for c in range(4):
            cols = slice(512 * c, 512 * c + 512)
            d_hidden = (dot_nt(third_low, w_o[cols, :]) * slope[rows, cols].astype(F32)).astype(BF16)
            slope[rows, cols] = d_hidden
            in_b_grad[:, cols] += column_sum(d_hidden.astype(F32))
            back = back + dot_nt(d_hidden, w_i[:, cols])
        add_vec(NORM2_G, column_sum(back * normal2))
        add_vec(NORM2_B, column_sum(back))
        d_sum = normalize_back(back, vector(NORM2_G), normal2, inverse2)
        add_vec(CROSS_O_B, column_sum(d_sum))
        d_second[rows, :] = d_sum
        sum_low = d_sum.astype(BF16)
        low_a[rows, :] = sum_low
        mix_grad = dot_nt(sum_low, w_c[:, 1536:2048]).astype(BF16)
        low_b[rows, :] = mix_grad
        delta[:, rows] = row_delta(mix_grad, cmixed[rows, :])

    loop(0, blocks, ffn)

    for c in range(4):
        cols = slice(512 * c, 512 * c + 512)
        grads[c] = dot_tn(second_low[...], slope[:, cols]).astype(BF16).reshape(32, 16, 512)
        value = dot_tn(active[:, cols], d_low[...]).astype(BF16).reshape(8, 4, 16, 512)
        for u in range(4):
            grads[4 + u, 8 * c : 8 * c + 8] = value[:, u]
    grads[8] = dot_tn(cmixed[...], low_a[...]).astype(BF16).reshape(32, 16, 512)
    grads_copy = pltpu.make_async_copy(grads.at[0:9], grads_out.at[0:9], out_sem.at[1])
    grads_copy.start()

    copies[3].wait()
    copies[4].wait()
    attend_back(cq, ck, ckt, cv, low_b, clse, delta, seg, mcolumn, seg_s, mseg_s, False, bias, dqt, dk, dv)

    def first_back(i):
        rows = rows_at(i, BLOCK)
        dq_low = (dqt[:, rows] * 0.125).astype(BF16).T
        dk_low = dk[rows, :].astype(BF16)
        dv_low = dv[rows, :].astype(BF16)
        dcq_o[rows, :] = dq_low
        dck_o[rows, :] = dk_low
        dcv_o[rows, :] = dv_low
        add_vec(CROSS_Q_B, column_sum(dq_low.astype(F32)))
        add_vec(CROSS_V_B, column_sum(dv_low.astype(F32)))
        memory_grad[rows, :] = (
            dot_nt(dk_low, w_c[:, 512:1024]) + dot_nt(dv_low, w_c[:, 1024:1536])
        ).astype(BF16)
        normal, inverse = normalize(first_sum[rows, :])
        back = d_second[rows, :] + dot_nt(dq_low, w_c[:, 0:512])
        add_vec(NORM1_G, column_sum(back * normal))
        add_vec(NORM1_B, column_sum(back))
        d_sum = normalize_back(back, vector(NORM1_G), normal, inverse)
        add_vec(SELF_O_B, column_sum(d_sum))
        d_second[rows, :] = d_sum
        sum_low = d_sum.astype(BF16)
        low_a[rows, :] = sum_low
        mix_grad = dot_nt(sum_low, w_s[:, 1536:2048]).astype(BF16)
        low_c[rows, :] = mix_grad
        delta[:, rows] = row_delta(mix_grad, mixed[rows, :])

    loop(0, blocks, first_back)
    results = [pltpu.make_async_copy(pieces[i], late_out[i], out_sem.at[3 + i]) for i in range(8)]
    for i in range(4):
        results[i].start()
    grads[9] = dot_tn(mixed[...], low_a[...]).astype(BF16).reshape(32, 16, 512)
    last_copy = pltpu.make_async_copy(grads.at[9:10], grads_out.at[9:10], out_sem.at[2])
    last_copy.start()

    copies[0].wait()
    copies[1].wait()
    attend_back(q, k, kt, v, low_c, lse, delta, seg, column, seg_s, seg_s, True, bias, dqt, dk, dv)

    def finish(i):
        rows = rows_at(i, BLOCK)
        dq_low = (dqt[:, rows] * 0.125).astype(BF16).T
        dk_low = dk[rows, :].astype(BF16)
        dv_low = dv[rows, :].astype(BF16)
        dq_o[rows, :] = dq_low
        dk_o[rows, :] = dk_low
        dv_o[rows, :] = dv_low
        add_vec(SELF_Q_B, column_sum(dq_low.astype(F32)))
        add_vec(SELF_V_B, column_sum(dv_low.astype(F32)))
        tokens_grad[rows, :] = (
            d_second[rows, :]
            + dot_nt(dq_low, w_s[:, 0:512])
            + dot_nt(dk_low, w_s[:, 512:1024])
            + dot_nt(dv_low, w_s[:, 1024:1536])
        ).astype(BF16)

    loop(0, blocks, finish)
    for i in range(4, 8):
        results[i].start()
    for i in range(8):
        results[i].wait()
    first_low_copy.wait()
    grads_copy.wait()
    last_copy.wait()


def middle(seg, pad, mseg, mpad, vec, in_b, tokens, projected, weights, out_grad):
    rows, width = tokens.shape
    q, k, kt, v, vt, ck, ckt, cv, cvt = projected
    wide, turned = (rows, width), (width, rows)
    smem = pl.BlockSpec(memory_space=pltpu.SMEM)
    late = [kt, v, ck, ckt, cv, cvt, *weights, out_grad]
    outs = [
        jax.ShapeDtypeStruct(wide, BF16),
        jax.ShapeDtypeStruct(wide, BF16),
        jax.ShapeDtypeStruct((10, 32, 16, 512), BF16),
        jax.ShapeDtypeStruct((16, 512), F32),
        jax.ShapeDtypeStruct((1, 2048), F32),
    ]
    outs += [jax.ShapeDtypeStruct(wide, BF16)] * 8
    big = lambda shape, kind: pltpu.VMEM(shape, kind)
    scratch = [big(a.shape, a.dtype) for a in late]
    scratch += [
        big((rows, 128), F32),
        big((rows, 128), F32),
        big((BLOCK, BLOCK), F32),
        big((width, BLOCK), F32),
        big((HEADS, BLOCK), F32),
        big((HEADS, BLOCK), F32),
        big(wide, BF16),
        big(wide, BF16),
        big((HEADS, rows), F32),
        big((HEADS, rows), F32),
        big((HEADS, rows), F32),
        big(wide, F32),
        big(wide, F32),
        big(wide, BF16),
        big(wide, BF16),
        big(wide, BF16),
        big(wide, F32),
        big(wide, BF16),
        big((rows, 2048), BF16),
        big((rows, 2048), BF16),
        big(turned, F32),
        big(wide, F32),
        big(wide, BF16),
        big((10, 32, 16, 512), BF16),
        pltpu.SemaphoreType.DMA((11,)),
        pltpu.SemaphoreType.DMA((11,)),
    ]
    return pl.pallas_call(
        middle_kernel,
        out_shape=outs,
        in_specs=[whole(None)] * 4 + [smem] * 2 + [whole(None)] * 6 + [any_space()] * 11,
        out_specs=[whole(None)] + [any_space()] * 2 + [whole(None)] * 2 + [any_space()] * 8,
        scratch_shapes=scratch,
        compiler_params=pltpu.CompilerParams(vmem_limit_bytes=VMEM_LIMIT),
        name="layer",
    )(seg, pad, mseg, mpad, seg, mseg, vec, in_b, tokens, q, k, vt, *late)


def pack_vectors(vec_grad, in_b_grad):
    row = lax.broadcasted_iota(jnp.int32, (32, 16, 512), 0)
    col = lax.broadcasted_iota(jnp.int32, (32, 16, 512), 2)
    own = jnp.where(row == col // 16, jnp.broadcast_to(vec_grad[None], (32, 16, 512)), 0.0)
    column = lax.broadcasted_iota(jnp.int32, (512, 128), 0)
    lane = lax.broadcasted_iota(jnp.int32, (512, 128), 1)
    pick = jnp.where((lane == column % 16) & (lane < 16), 1.0, 0.0).astype(BF16)
    packed = dot(own.reshape(512, 512).astype(BF16), pick)
    row = lax.broadcasted_iota(jnp.int32, (32, 2048), 0)
    col = lax.broadcasted_iota(jnp.int32, (32, 2048), 1)
    own = jnp.where(row == col // 64, jnp.broadcast_to(in_b_grad, (32, 2048)), 0.0).astype(BF16)
    column = lax.broadcasted_iota(jnp.int32, (2048, 128), 0)
    lane = lax.broadcasted_iota(jnp.int32, (2048, 128), 1)
    pick = jnp.where((lane == column % 64) & (lane < 64), 1.0, 0.0).astype(BF16)
    wide = dot(own, pick).astype(BF16)
    target = lax.broadcasted_iota(jnp.int32, (512, 32), 0)
    device = lax.broadcasted_iota(jnp.int32, (512, 32), 1)
    choose = jnp.where(target == device * 16 + FFN_IN_B, 1.0, 0.0).astype(BF16)
    return packed + dot(choose, wide)


def scatter_kernel(*refs):
    (x_ref, m_ref, f_ref, dcq, dck, dcv, dq, dk, dv, vec_grad, in_b_grad, ready) = refs[:12]
    sums, vec_sums = refs[12:14]
    (made, held, in0, in1, in2, in3, in4, g_v, v0, v1, v2, v3, v4, send, recv, keep) = refs[14:]
    d, f, me = place()
    greet(d, f)
    inbox = (in0, in1, in2, in3, in4)
    vec_inbox = (v0, v1, v2, v3, v4)
    n_ready = 10

    def order(u):
        return tuple(reversed(ORDERS["A" if u == UNITS else UNIT_ORDERS[u]]))

    def copy(u, s):
        bits = order(u)
        gone = bits[:s]
        if u == UNITS:
            index = tuple(me[b] if b in gone else 1 - me[b] if b == bits[s] else slice(None) for b in BITS)
            source, target = g_v.at[index], vec_inbox[s]
        elif s == 0:
            index = (slice(None),) * 4 + (1 - me["c"],)
            source = ready.at[(u,) + index] if u < n_ready else made.at[(u - n_ready,) + index]
            target = in0.at[u]
        else:
            index = tuple(me[b] if b in gone else 1 - me[b] if b == bits[s] else slice(None) for b in BITS[:4])
            source, target = held.at[(u,) + index], inbox[s].at[u]
        return pltpu.make_async_remote_copy(
            src_ref=source,
            dst_ref=target,
            send_sem=send.at[u, s],
            recv_sem=recv.at[u, s],
            device_id=partner(bits[s], d, f),
            device_id_type=MESH,
        )

    def own_half(u):
        index = (u,) + (slice(None),) * 4 + (me["c"],)
        return pltpu.make_async_copy(ready.at[index], held.at[u], keep.at[u])

    def add(u, s):
        bits = order(u)
        gone = bits[: s + 1]
        if u == UNITS:
            index = tuple(me[b] if b in gone else slice(None) for b in BITS)
            g_v[index] = g_v[index] + vec_inbox[s][...]
        elif s == 0:
            if u < n_ready:
                own_half(u).wait()
                mine = held[u]
            else:
                mine = made[(u - n_ready,) + (slice(None),) * 4 + (me["c"],)]
            held[u] = mine + in0[u]
        else:
            index = (u,) + tuple(me[b] if b in gone else slice(None) for b in BITS[:4])
            if s == 4:
                sums[u] = held[index].astype(F32) + in4[u].astype(F32)
            else:
                held[index] = held[index] + inbox[s][u]

    bits = (2,) * 5
    g_v[...] = pack_vectors(vec_grad[...], in_b_grad[...]).reshape(bits + (16, 128))

    def prepare(u):
        if u < n_ready:
            own_half(u).start()
        elif u < UNITS:
            left = (f_ref, m_ref, m_ref, x_ref, x_ref, x_ref)[u - n_ready]
            right = (dcq, dck, dcv, dq, dk, dv)[u - n_ready]
            made[u - n_ready] = dot_tn(left[...], right[...]).astype(BF16).reshape(bits + (16, 512))

    steps = [(u + LAG * s, -s, u, s) for u in range(UNITS + 1) for s in range(6)]
    for _, _, u, s in sorted(steps):
        if s == 0:
            prepare(u)
        if s > 0:
            copy(u, s - 1).wait_recv()
            add(u, s - 1)
        if s < 5:
            copy(u, s).start()
    for u in range(UNITS + 1):
        for s in range(5):
            copy(u, s).wait_send()
    vec_sums[...] = g_v[tuple(me[b] for b in BITS)]


def scatter(tokens, memory, first_low, back, vec_grad, in_b_grad, ready):
    bits = (2,) * 5
    unit = (16, 512)
    vec_unit = (16, 128)
    boxes = [(UNITS,) + (2,) * (4 - s) + unit for s in range(5)]
    return pl.pallas_call(
        scatter_kernel,
        out_shape=[
            jax.ShapeDtypeStruct((UNITS,) + unit, F32),
            jax.ShapeDtypeStruct(vec_unit, F32),
        ],
        in_specs=[whole(None)] * 11 + [any_space()],
        out_specs=[whole(None)] * 2,
        scratch_shapes=[pltpu.VMEM((6,) + bits + unit, BF16), pltpu.VMEM((UNITS,) + (2,) * 4 + unit, BF16)]
        + [pltpu.VMEM(b, BF16) for b in boxes]
        + [pltpu.VMEM(bits + vec_unit, F32)]
        + [pltpu.VMEM((2,) * (4 - s) + vec_unit, F32) for s in range(5)]
        + [
            pltpu.SemaphoreType.DMA((UNITS + 1, 5)),
            pltpu.SemaphoreType.DMA((UNITS + 1, 5)),
            pltpu.SemaphoreType.DMA((10,)),
        ],
        compiler_params=pltpu.CompilerParams(
            collective_id=2, has_side_effects=True, vmem_limit_bytes=VMEM_LIMIT
        ),
        name="grads_scatter",
    )(tokens, memory, first_low, *back, vec_grad, in_b_grad, ready.reshape((10,) + bits + unit))


def unpack_kernel(sums, vec_sums, *outs):
    matrices, vectors = outs[:10], outs[10:]
    for i, u in enumerate((13, 14, 15, 9, 10, 11, 12, 8)):
        matrices[i][...] = sums[u]
    for u in range(4):
        matrices[8][:, 512 * u : 512 * u + 512] = sums[u]
        matrices[9][16 * u : 16 * u + 16, :] = sums[4 + u]
    for i in range(13):
        vectors[i][...] = vec_sums[i : i + 1, 0:16]
    vectors[13][...] = vec_sums[FFN_IN_B : FFN_IN_B + 1, 0:64]


def unpack(sums, vec_sums):
    shapes = [(16, 512)] * 8 + [(16, 2048), (64, 512)] + [(1, 16)] * 13 + [(1, 64)]
    return pl.pallas_call(
        unpack_kernel,
        out_shape=[jax.ShapeDtypeStruct(s, F32) for s in shapes],
        in_specs=[whole(None)] * 2,
        out_specs=[whole(None)] * len(shapes),
        name="unpack",
    )(sums, vec_sums)


def weight_kernel(x_ref, m_ref, f_ref, dcq, dck, dcv, dq, dk, dv, out_ref):
    pairs = ((f_ref, dcq), (m_ref, dck), (m_ref, dcv), (x_ref, dq), (x_ref, dk), (x_ref, dv))
    for i, (left, right) in enumerate(pairs):
        out_ref[i] = dot_tn(left[...], right[...])


def local(
    tokens, memory, token_seg, token_pad, memory_seg, memory_pad, out_grad,
    self_q_w, self_q_b, self_k_w, self_v_w, self_v_b, self_o_w, self_o_b, norm1_gain, norm1_bias,
    cross_q_w, cross_q_b, cross_k_w, cross_v_w, cross_v_b, cross_o_w, cross_o_b, norm2_gain, norm2_bias,
    ffn_in_w, ffn_in_b, ffn_out_w, ffn_out_b, norm3_gain, norm3_bias, *, ring,
):
    vectors = (self_q_b, self_v_b, self_o_b, norm1_gain, norm1_bias, cross_q_b, cross_v_b, cross_o_b,
               norm2_gain, norm2_bias, ffn_out_b, norm3_gain, norm3_bias)
    shards = (self_q_w, self_k_w, self_v_w, self_o_w, cross_q_w, cross_k_w, cross_v_w, cross_o_w,
              ffn_in_w, ffn_out_w)
    if ring:
        packed = jnp.concatenate(
            [
                jnp.pad(jnp.stack(vectors), ((0, 2), (0, 112))),
                jnp.pad(ffn_in_b.reshape(1, 64), ((0, 0), (0, 64))),
            ]
        )
        w_s, w_c, w_i, w_o, vec, in_b, projected = gather(tokens, memory, packed, shards)
    else:
        get = partial(lax.all_gather, axis_name=AXES, axis=0, tiled=True)
        full = [get(w) for w in shards]
        w_s, w_c = jnp.concatenate(full[:4], 1), jnp.concatenate(full[4:8], 1)
        w_i, w_o = full[8:]
        vec = jnp.pad(jnp.stack([get(b) for b in vectors]).astype(F32), ((0, 3), (0, 0)))
        in_b = get(ffn_in_b).astype(F32).reshape(1, -1)
        projected = project_only(tokens, memory, vec, w_s, w_c)
    (layer_out, first_low, ready, vec_grad, in_b_grad, dcq, dck, dcv, memory_grad, dq, dk, dv,
     tokens_grad) = middle(
        token_seg, token_pad, memory_seg, memory_pad, vec, in_b, tokens, projected, (w_s, w_c, w_i, w_o), out_grad
    )
    back = (dcq, dck, dcv, dq, dk, dv)
    if ring:
        sums, vec_sums = scatter(tokens, memory, first_low, back, vec_grad, in_b_grad, ready)
        shards = unpack(sums, vec_sums)
        mats, vecs = shards[:10], [s.reshape(-1) for s in shards[10:]]
    else:
        give = partial(lax.psum_scatter, axis_name=AXES, scatter_dimension=0, tiled=True)
        made = pl.pallas_call(
            weight_kernel,
            out_shape=jax.ShapeDtypeStruct((6, 512, 512), F32),
            in_specs=[whole(None)] * 9,
            out_specs=whole(None),
            compiler_params=pltpu.CompilerParams(vmem_limit_bytes=VMEM_LIMIT),
            name="weight_grads",
        )(tokens, memory, first_low, *back)
        done = ready.astype(F32).reshape(10, 512, 512)
        in_w = done[:4].transpose(1, 0, 2).reshape(512, 2048)
        out_w = done[4:8].reshape(4, 32, 16, 512).transpose(1, 0, 2, 3).reshape(2048, 512)
        full = [made[3], made[4], made[5], done[9], made[0], made[1], made[2], done[8], in_w, out_w]
        mats = [give(g) for g in full]
        vecs = [give(vec_grad[i]) for i in range(13)] + [give(in_b_grad[0])]
    (g_sqw, g_skw, g_svw, g_sow, g_cqw, g_ckw, g_cvw, g_cow, g_iw, g_ow) = mats
    (g_sqb, g_svb, g_sob, g_n1g, g_n1b, g_cqb, g_cvb, g_cob, g_n2g, g_n2b, g_ob, g_n3g, g_n3b, g_ib) = vecs
    return (
        layer_out, tokens_grad, memory_grad,
        g_sqw, g_sqb, g_skw, g_svw, g_svb, g_sow, g_sob, g_n1g, g_n1b,
        g_cqw, g_cqb, g_ckw, g_cvw, g_cvb, g_cow, g_cob, g_n2g, g_n2b,
        g_iw, g_ib, g_ow, g_ob, g_n3g, g_n3b,
    )


def solution(mesh):
    ring = mesh.shape["dp"] == 8 and mesh.shape["fsdp"] == 4
    matrix, vector = P(AXES, None), P(AXES)
    return jax.shard_map(
        partial(local, ring=ring),
        mesh=mesh,
        in_specs=(
            (matrix,) * 7
            + (matrix, vector, matrix, matrix, vector, matrix, vector, vector, vector) * 2
            + (matrix, vector, matrix, vector, vector, vector)
        ),
        out_specs=(
            (matrix,) * 3
            + (matrix, vector, matrix, matrix, vector, matrix, vector, vector, vector) * 2
            + (matrix, vector, matrix, vector, vector, vector)
        ),
        check_vma=False,
    )
```

```python
from functools import partial

import jax
import jax.numpy as jnp
from jax import lax
from jax.experimental import pallas as pl
from jax.experimental.pallas import tpu as pltpu
from jax.sharding import PartitionSpec as P

HEADS = 8
EPSILON = 1e-05
MASKED = -1e30
AXES = ("dp", "fsdp")
MESH = pl.DeviceIdType.MESH
BF16 = jnp.bfloat16
F32 = jnp.float32
BLOCK = 256
VMEM_LIMIT = 58 << 20

(SELF_Q_B, SELF_V_B, SELF_O_B, NORM1_G, NORM1_B, CROSS_Q_B, CROSS_V_B, CROSS_O_B,
 NORM2_G, NORM2_B, FFN_OUT_B, NORM3_G, NORM3_B) = range(13)
FFN_IN_B = 15

BITS = ("zh", "zl", "y", "x", "c")
ORDERS = {
    "A": ("zh", "zl", "x", "y", "c"),
    "B": ("zh", "zl", "y", "x", "c"),
    "C": ("x", "zh", "zl", "y", "c"),
    "D": ("y", "zh", "zl", "x", "c"),
}
UNIT_ORDERS = "CDACDBCDACDBCDAB"
UNITS = 16


def dot(left, right):
    return jnp.dot(left, right, preferred_element_type=F32)


def dot_nt(left, right):
    return lax.dot_general(left, right, (((1,), (1,)), ((), ())), preferred_element_type=F32)


def dot_tn(left, right):
    return lax.dot_general(left, right, (((0,), (0,)), ((), ())), preferred_element_type=F32)


def rows_at(index, size):
    return pl.ds(pl.multiple_of(index * size, size), size)


def loop(low, high, body):
    def step(index, carry):
        body(index)
        return carry

    lax.fori_loop(low, high, step, 0)


def whole(shape):
    return pl.BlockSpec(memory_space=pltpu.VMEM)


def any_space():
    return pl.BlockSpec(memory_space=pl.ANY)


def place():
    d = lax.axis_index("dp")
    f = lax.axis_index("fsdp")
    return d, f, {"zh": d // 4, "zl": (d // 2) % 2, "y": d % 2, "x": f // 2, "c": f % 2}


def flip(value, mask):
    return value + mask - 2 * mask * ((value // mask) % 2)


def partner(bit, d, f):
    return {
        "zh": (flip(d, 4), f),
        "zl": (flip(d, 2), f),
        "y": (flip(d, 1), f),
        "x": (d, flip(f, 2)),
        "c": (d, flip(f, 1)),
    }[bit]


def greet(d, f):
    barrier = pltpu.get_barrier_semaphore()
    for bit in BITS:
        pl.semaphore_signal(barrier, inc=1, device_id=partner(bit, d, f), device_id_type=MESH)
    pl.semaphore_wait(barrier, len(BITS))


def spread_vectors(packed, vec_ref, in_b_ref):
    flat = packed.reshape(512, 128)
    lane = lax.broadcasted_iota(jnp.int32, (128, 512), 0)
    column = lax.broadcasted_iota(jnp.int32, (128, 512), 1)
    pick = jnp.where((lane == column % 16) & (lane < 16), 1.0, 0.0).astype(BF16)
    spread = dot(flat, pick)
    row = lax.broadcasted_iota(jnp.int32, (512, 512), 0)
    col = lax.broadcasted_iota(jnp.int32, (512, 512), 1)
    kept = jnp.where(row // 16 == col // 16, spread, 0.0)
    vec_ref[...] = jnp.sum(kept.reshape(32, 16, 512), axis=0)
    device = lax.broadcasted_iota(jnp.int32, (32, 512), 0)
    source = lax.broadcasted_iota(jnp.int32, (32, 512), 1)
    choose = jnp.where(source == device * 16 + FFN_IN_B, 1.0, 0.0).astype(BF16)
    own = dot(choose, flat).astype(BF16)
    lane = lax.broadcasted_iota(jnp.int32, (128, 2048), 0)
    column = lax.broadcasted_iota(jnp.int32, (128, 2048), 1)
    pick = jnp.where((lane == column % 64) & (lane < 64), 1.0, 0.0).astype(BF16)
    spread = dot(own, pick)
    row = lax.broadcasted_iota(jnp.int32, (32, 2048), 0)
    col = lax.broadcasted_iota(jnp.int32, (32, 2048), 1)
    in_b_ref[...] = jnp.sum(jnp.where(row == col // 64, spread, 0.0), axis=0, keepdims=True)


def merge(events, compute):
    events = sorted(events, key=lambda e: e[:2])
    now, waiting = 0.0, None
    while events or compute is not None:
        if waiting is not None and waiting():
            waiting = None
        blocked = waiting is not None or compute is None
        if events and (blocked or events[0][0] <= now):
            time, _, step = events.pop(0)
            if waiting is not None:
                now = max(now, time)
            step()
            continue
        try:
            kind, value = next(compute)
        except StopIteration:
            compute = None
            continue
        if kind == "cost":
            now += value
        elif kind == "need":
            waiting = value
        else:
            events += [(now + time, number, step) for time, number, step in value]
            events.sort(key=lambda e: e[:2])


def interleave(makers, skew):
    running = [maker() for maker in makers]
    done = [False] * len(running)
    time = 0
    while not all(done):
        for i, piece in enumerate(running):
            if not done[i] and time >= i * skew:
                done[i] = next(piece, True) is True
        time += 1


def run_all(compute):
    for _ in compute:
        pass


def span(index, count):
    if isinstance(index, int):
        return slice(index * BLOCK, (index + count) * BLOCK)
    return pl.ds(pl.multiple_of(index * BLOCK, BLOCK), count * BLOCK)


def key_columns(seg_ref, pad_ref, column_ref):
    open_seg = jnp.where(pad_ref[...] == 0, seg_ref[...], -1).astype(F32)
    for i in range(seg_ref.shape[1] // 128):
        piece = jnp.broadcast_to(open_seg[:, 128 * i : 128 * i + 128], (128, 128)).T
        column_ref[128 * i : 128 * i + 128, :] = piece


def mask_rows(bias_ref, column_ref, seg_ref, qb, kb, count, causal):
    query = seg_ref[:, span(qb, 1)].astype(F32)
    column = column_ref[span(kb, count), :]
    allowed = jnp.concatenate([column] * (BLOCK // 128), axis=1) == query
    if causal:
        shape = (count * BLOCK, BLOCK)
        key_pos = kb * BLOCK + lax.broadcasted_iota(jnp.int32, shape, 0)
        query_pos = qb * BLOCK + lax.broadcasted_iota(jnp.int32, shape, 1)
        allowed = (allowed & (key_pos < query_pos)) | (key_pos == query_pos)
    bias_ref[0 : count * BLOCK, :] = jnp.where(allowed, 0.0, MASKED)


def own_lanes(value, head):
    lane = lax.broadcasted_iota(jnp.int32, value.shape, 1)
    return jnp.where(lane // 64 == head, value, jnp.zeros_like(value))


def attend_rows(count, kb, qb, qt_ref, k_ref, vt_ref, bias_ref, turned_ref, lse_ref, prob_ref, out_ref):
    rows, keys, size = span(qb, 1), span(kb, count), count * BLOCK

    def scores(h):
        part = slice(64 * h, 64 * h + 64)
        return dot(k_ref[keys, part], qt_ref[part, rows])

    def spot(h):
        return (slice(0, size), slice(BLOCK * h, BLOCK * h + BLOCK))

    def product(h, total):
        part = slice(64 * h, 64 * h + 64)
        turned_ref[part, :] = dot(vt_ref[part, keys], prob_ref[spot(h)]) * (1.0 / total)

    held = {h: scores(h) for h in range(2)}
    pending, tops, totals = [], [], []
    for h in range(HEADS):
        if h + 2 < HEADS:
            held[h + 2] = scores(h + 2)
        if len(pending) >= 5:
            product(*pending.pop(0))
        score = held.pop(h) + bias_ref[0:size, :]
        top = jnp.max(score, axis=0, keepdims=True)
        prob = jnp.exp(score - top)
        total = jnp.sum(prob, axis=0, keepdims=True)
        prob_ref[spot(h)] = prob.astype(BF16)
        tops.append(top)
        totals.append(total)
        pending.append((h, total))
        yield ("cost", 0.1 * count)
    for item in pending:
        product(*item)
    lse_ref[:, rows] = jnp.concatenate(tops, 0) + jnp.log(jnp.concatenate(totals, 0))
    out_ref[rows, :] = turned_ref[...].astype(BF16).T
    yield ("cost", 0.3)


def attend_rows_back(count, kb, qb, q_ref, qt_ref, k_ref, kt_ref, v_ref, g_ref, gt_ref, lse_ref, delta_ref, bias_ref,
                     dqt_ref, dk_ref, dv_ref, grad_ref, query_ref, prob_ref, slant_ref):
    rows, keys, size = span(qb, 1), span(kb, count), count * BLOCK

    def scores(h):
        part = slice(64 * h, 64 * h + 64)
        return (dot(k_ref[keys, part], qt_ref[part, rows]), dot(v_ref[keys, part], gt_ref[part, rows]))

    for slab in range(2):
        lanes = slice(256 * slab, 256 * slab + 256)
        for j in range(4):
            here = slice(BLOCK * j, BLOCK * j + BLOCK)
            grad_ref[slab, here, :] = own_lanes(g_ref[rows, lanes], j)
            query_ref[slab, here, :] = own_lanes(q_ref[rows, lanes], j)

    def tail(slab):
        lanes = slice(256 * slab, 256 * slab + 256)
        four = slice(4 * BLOCK * slab, 4 * BLOCK * slab + 4 * BLOCK)
        dv_ref[keys, lanes] += dot(prob_ref[0:size, four], grad_ref[slab])
        dk_ref[keys, lanes] += dot(slant_ref[0:size, four], query_ref[slab])
        for h in range(4 * slab, 4 * slab + 4):
            part = slice(64 * h, 64 * h + 64)
            dqt_ref[part, rows] = dot(kt_ref[part, keys], slant_ref[0:size, BLOCK * h : BLOCK * h + BLOCK])

    held = {h: scores(h) for h in range(2)}
    for h in range(HEADS):
        if h + 2 < HEADS:
            held[h + 2] = scores(h + 2)
        if h == 6:
            tail(0)
        score, grad = held.pop(h)
        mine, here = slice(h, h + 1), slice(BLOCK * h, BLOCK * h + BLOCK)
        prob = jnp.exp(score + bias_ref[0:size, :] - lse_ref[mine, rows])
        prob_ref[0:size, here] = prob.astype(BF16)
        slant_ref[0:size, here] = (prob * (grad - delta_ref[mine, rows])).astype(BF16)
        yield ("cost", 0.17 * count)
    tail(1)
    yield ("cost", 0.1)


def document_blocks(qb):
    first = max(0, (qb * BLOCK - 511) // BLOCK)
    return first, qb + 1 - first


FRONT = ("q", "qt", "k", "kt", "v", "mixed", "first_low", "cq", "cqt", "ck", "ckt", "cv", "cvt")
FRONT_SHAPES = {name: "turned" if name in ("qt", "kt", "cqt", "ckt", "cvt") else "straight" for name in FRONT}


def front(x_ref, m_ref, seg, pad, weight, vec_ref, need, a, vt, column, bias, turned, prob, lse, first_sum, put):
    blocks = x_ref.shape[0] // BLOCK

    def vector(index):
        return vec_ref[index : index + 1, :]

    def project(source, index, bias_row, straight, turned_to, scale=None):
        yield ("need", lambda: need(index))
        for i in range(blocks):
            rows = span(i, 1)
            value = dot(source[rows, :], weight(index))
            if bias_row is not None:
                value = value + vector(bias_row)
            value = value.astype(BF16)
            if scale is not None:
                value = value * scale
            straight[rows, :] = value
            if turned_to is not None:
                turned_to[:, rows] = value.T
            yield ("cost", 0.25)

    key_columns(seg, pad, column)
    yield ("need", lambda: need(None))
    yield from project(x_ref, 0, SELF_Q_B, a["q"], a["qt"], 0.125)
    yield from project(x_ref, 1, None, a["k"], a["kt"])
    yield from project(x_ref, 2, SELF_V_B, a["v"], vt)
    put("q", "qt", "k", "kt", "v")
    for qb in range(blocks):
        kb, count = document_blocks(qb)
        mask_rows(bias, column, seg, qb, kb, count, True)
        yield from attend_rows(count, kb, qb, a["qt"], a["k"], vt, bias, turned, lse, prob, a["mixed"])
    put("mixed")
    yield ("need", lambda: need(3))
    for i in range(blocks):
        rows = span(i, 1)
        summed = x_ref[rows, :].astype(F32) + dot(a["mixed"][rows, :], weight(3)) + vector(SELF_O_B)
        first_sum[rows, :] = summed
        normal, _ = normalize(summed)
        a["first_low"][rows, :] = (normal * vector(NORM1_G) + vector(NORM1_B)).astype(BF16)
        yield ("cost", 0.4)
    put("first_low", "first_sum")
    yield from project(m_ref, 5, None, a["ck"], a["ckt"])
    yield from project(m_ref, 6, CROSS_V_B, a["cv"], a["cvt"])
    put("ck", "ckt", "cv", "cvt")
    yield from project(a["first_low"], 4, CROSS_Q_B, a["cq"], a["cqt"], 0.125)
    put("cq", "cqt")


def front_scratch(rows, width):
    shape = {"straight": (rows, width), "turned": (width, rows)}
    return [pltpu.VMEM(shape[FRONT_SHAPES[name]], BF16) for name in FRONT] + [
        pltpu.VMEM((rows, width), F32),
        pltpu.VMEM((width, rows), BF16),
        pltpu.VMEM((rows, 128), F32),
        pltpu.VMEM((3 * BLOCK, BLOCK), F32),
        pltpu.VMEM((width, BLOCK), F32),
        pltpu.VMEM((3 * BLOCK, HEADS * BLOCK), BF16),
        pltpu.SemaphoreType.DMA((len(FRONT) + 1,)),
    ]


def front_outs(rows, width):
    shape = {"straight": (rows, width), "turned": (width, rows)}
    return [jax.ShapeDtypeStruct(shape[FRONT_SHAPES[name]], BF16) for name in FRONT] + [
        jax.ShapeDtypeStruct((rows, width), F32)
    ]


def front_parts(outs, scratch):
    names = FRONT + ("first_sum",)
    count = len(FRONT)
    a = dict(zip(FRONT, scratch[:count], strict=True))
    first_sum, vt, column, bias, turned, prob, sem = scratch[count:]
    held = dict(a, first_sum=first_sum)
    copies = {n: pltpu.make_async_copy(held[n], outs[i], sem.at[i]) for i, n in enumerate(names)}

    def put(*which):
        for name in which:
            copies[name].start()

    def finish():
        for name in names:
            copies[name].wait()

    return a, first_sum, vt, column, bias, turned, prob, put, finish


UNIT_PLACES = (
    [("s", 0), ("s", 1), ("s", 2), ("s", 3), ("c", 1), ("c", 2), ("c", 0), ("c", 3)]
    + [("i", i) for i in range(4)]
    + [("o", i) for i in range(4)]
)
GATHER_START, GATHER_STEP, GATHER_FIRST_STEP = 1.1, 4.4, 2.5


def gather_kernel(*refs):
    x_ref, m_ref, seg, pad, packed = refs[:5]
    shards = refs[5:15]
    o_s, o_c, o_i, o_o, vec_out, in_b_out, lse = refs[15:22]
    front_to = refs[22 : 23 + len(FRONT)]
    rest = refs[23 + len(FRONT) :]
    b_s, b_c, b_i, b_o, b_v = rest[:5]
    send, recv, keep = rest[5:8]
    d, f, me = place()
    own = tuple(me[bit] for bit in BITS)
    for i in range(4):
        b_s[own + (slice(None), slice(512 * i, 512 * i + 512))] = shards[i][...]
        b_c[own + (slice(None), slice(512 * i, 512 * i + 512))] = shards[4 + i][...]
    b_i[own] = shards[8][...]
    b_o[own] = shards[9][...]
    b_v[own] = packed[...]
    greet(d, f)

    buffers = {"s": b_s, "c": b_c, "i": b_i, "o": b_o}
    targets = {"s": o_s, "c": o_c, "i": o_i, "o": o_o}
    finished = set()

    def part(u, index):
        kind, i = UNIT_PLACES[u]
        if kind == "o":
            return index + (slice(16 * i, 16 * i + 16), slice(None))
        return index + (slice(None), slice(512 * i, 512 * i + 512))

    def copy(u, s):
        order = ORDERS["A" if u == UNITS else UNIT_ORDERS[u]]
        have = order[:s]
        index = tuple(slice(None) if bit in have else me[bit] for bit in BITS)
        buffer = b_v
        if u < UNITS:
            index, buffer = part(u, index), buffers[UNIT_PLACES[u][0]]
        return pltpu.make_async_remote_copy(
            src_ref=buffer.at[index],
            dst_ref=buffer.at[index],
            send_sem=send.at[u, s],
            recv_sem=recv.at[u, s],
            device_id=partner(order[s], d, f),
            device_id_type=MESH,
        )

    def store(u):
        kind = UNIT_PLACES[u][0]
        index = part(u, (slice(None),) * 5)
        return pltpu.make_async_copy(buffers[kind].at[index], targets[kind].at[index], keep.at[u])

    def step(u, s):
        if s > 0:
            copy(u, s - 1).wait_recv()
        if s < 5:
            copy(u, s).start()
            return
        if u == UNITS:
            spread_vectors(b_v[...].reshape(32, 16, 128), vec_out, in_b_out)
        else:
            store(u).start()
        finished.add(u)

    events = []
    for u in range(UNITS + 1):
        start = 0.0 if u == UNITS else 0.1 + u * GATHER_START
        each = GATHER_FIRST_STEP if u == UNITS or u < 4 else GATHER_STEP
        events += [(start + each * s, u, partial(step, u, s)) for s in range(6)]

    unit_of = {0: 0, 1: 1, 2: 2, 3: 3, 4: 6, 5: 4, 6: 5, None: UNITS}

    def weight(i):
        buffer, column = (b_s, i) if i < 4 else (b_c, i - 4)
        return buffer[:, :, :, :, :, :, 512 * column : 512 * column + 512].reshape(512, 512)

    a, first_sum, vt, column, bias, turned, prob, put, finish = front_parts(front_to, rest[8:])
    compute = front(x_ref, m_ref, seg, pad, weight, vec_out, lambda i: unit_of[i] in finished, a, vt, column, bias,
                    turned, prob, lse, first_sum, put)
    merge(events, compute)
    for u in range(UNITS + 1):
        for s in range(5):
            copy(u, s).wait_send()
        if u < UNITS:
            store(u).wait()
    finish()


def gather_front(tokens, memory, seg, pad, packed, shards):
    rows, width = tokens.shape
    bits = (2,) * 5
    weights = [bits + (16, 2048)] * 3 + [bits + (64, 512)]
    shapes = [jax.ShapeDtypeStruct(s, BF16) for s in weights]
    shapes += [
        jax.ShapeDtypeStruct((16, 512), F32),
        jax.ShapeDtypeStruct((1, 2048), F32),
        jax.ShapeDtypeStruct((HEADS, rows), F32),
    ]
    shapes += front_outs(rows, width)
    result = pl.pallas_call(
        gather_kernel,
        out_shape=shapes,
        in_specs=[whole(None)] * 15,
        out_specs=[any_space()] * 4 + [whole(None)] * 3 + [any_space()] * (len(FRONT) + 1),
        scratch_shapes=[pltpu.VMEM(s, BF16) for s in weights]
        + [pltpu.VMEM(bits + (16, 128), BF16)]
        + [
            pltpu.SemaphoreType.DMA((UNITS + 1, 5)),
            pltpu.SemaphoreType.DMA((UNITS + 1, 5)),
            pltpu.SemaphoreType.DMA((UNITS,)),
        ]
        + front_scratch(rows, width),
        compiler_params=pltpu.CompilerParams(
            collective_id=1, has_side_effects=True, vmem_limit_bytes=VMEM_LIMIT
        ),
        name="gather_front",
    )(tokens, memory, seg, pad, packed, *shards)
    w_s, w_c, w_i = (w.reshape(512, 2048) for w in result[:3])
    return w_s, w_c, w_i, result[3].reshape(2048, 512), *result[4:7], result[7:]


def front_kernel(*refs):
    x_ref, m_ref, seg, pad, vec_ref, w_s, w_c, lse = refs[:8]
    outs, scratch = refs[8 : 9 + len(FRONT)], refs[9 + len(FRONT) :]

    def weight(i):
        source, column = (w_s, i) if i < 4 else (w_c, i - 4)
        return source[:, 512 * column : 512 * column + 512]

    a, first_sum, vt, column, bias, turned, prob, put, finish = front_parts(outs, scratch)
    run_all(front(x_ref, m_ref, seg, pad, weight, vec_ref, lambda i: True, a, vt, column, bias, turned, prob, lse,
                  first_sum, put))
    finish()


def front_only(tokens, memory, seg, pad, vec, w_s, w_c):
    rows, width = tokens.shape
    result = pl.pallas_call(
        front_kernel,
        out_shape=[jax.ShapeDtypeStruct((HEADS, rows), F32)] + front_outs(rows, width),
        in_specs=[whole(None)] * 7,
        out_specs=[whole(None)] + [any_space()] * (len(FRONT) + 1),
        scratch_shapes=front_scratch(rows, width),
        compiler_params=pltpu.CompilerParams(vmem_limit_bytes=VMEM_LIMIT),
        name="front",
    )(tokens, memory, seg, pad, vec, w_s, w_c)
    return result[0], result[1:]


def lower_bound(seg_ref, value):
    last = seg_ref.shape[1] - 1

    def step(_, carry):
        low, high = carry
        middle = jnp.minimum((low + high) // 2, last)
        below = seg_ref[0, middle] < value
        return (jnp.where(below, middle + 1, low), jnp.where(below, high, middle))

    steps = (last + 1).bit_length()
    return lax.fori_loop(0, steps, step, (jnp.int32(0), jnp.int32(last + 1)))[0]


def normalize(summed):
    center = summed - jnp.mean(summed, axis=-1, keepdims=True)
    spread = jnp.mean(center * center, axis=-1, keepdims=True)
    inverse = lax.rsqrt(spread + EPSILON)
    return center * inverse, inverse


def normalize_back(grad, gain, normal, inverse):
    scaled = grad * gain
    mean = jnp.mean(scaled, axis=-1, keepdims=True)
    along = jnp.mean(scaled * normal, axis=-1, keepdims=True)
    return inverse * (scaled - mean - normal * along)


def column_sum(value):
    return jnp.sum(value, axis=0, keepdims=True)


def gelu_and_slope(hidden):
    size = jnp.abs(hidden) * (0.5 ** 0.5)
    t = 1.0 / (1.0 + 0.3275911 * size)
    bell = jnp.exp(-0.5 * hidden * hidden)
    poly = 1.061405429
    for c in (-1.453152027, 1.421413741, -0.284496736, 0.254829592):
        poly = poly * t + c
    tail = (0.5 * t) * poly * bell
    phi = jnp.where(hidden < 0.0, tail, 1.0 - tail)
    return hidden * phi, phi + hidden * (bell * 0.3989422804014327)


def row_delta(grad, mixed):
    head = lax.broadcasted_iota(jnp.int32, (16, 512), 0)
    lane = lax.broadcasted_iota(jnp.int32, (16, 512), 1)
    pick = jnp.where(lane // 64 == head, 1.0, 0.0).astype(BF16)
    product = grad.astype(F32) * mixed.astype(F32)
    high = product.astype(BF16)
    low = (product - high.astype(F32)).astype(BF16)
    return (dot_nt(pick, high) + dot_nt(pick, low))[:HEADS, :]


def for_count(query_seg, key_seg, qb, blocks, body):
    low = lower_bound(key_seg, query_seg[0, qb * BLOCK]) // BLOCK
    last = query_seg[0, qb * BLOCK + BLOCK - 1]
    high = (lower_bound(key_seg, last + 1) + BLOCK - 1) // BLOCK
    for count in range(1, blocks + 1):
        pl.when(high - low == count)(partial(body, count, low))


def middle_kernel(*refs):
    (seg, mseg, mpad, seg_s, mseg_s, vec, in_b, cqt, ck, cvt) = refs[:10]
    late_in = refs[10:18]
    (layer_out, grads_out, vec_grad, in_b_grad) = refs[18:22]
    late_out = refs[22:27]
    scratch = refs[27:]
    (cq, ckt, cv, first_sum, w_c, w_i, w_o, out_grad) = scratch[:8]
    (column, bias, turned, cmixed, clse, delta, second_low, d_second, d_low, active, slope, dqt, dk, dv, low_a, low_b,
     low_bt, grad4, query4, grads, late_sem, out_sem) = scratch[8:]
    pieces = [active.at[:, 512 * i : 512 * i + 512] for i in range(4)] + [d_second]
    dcq_o, dck_o, dcv_o, memory_grad = pieces[:4]
    copies = [pltpu.make_async_copy(late_in[i], scratch[i], late_sem.at[i]) for i in range(8)]
    for i in (3, 4, 5, 6, 7, 0, 1, 2):
        copies[i].start()
    rows_total = cqt.shape[1]
    blocks = rows_total // BLOCK

    def vector(index):
        return vec[index : index + 1, :]

    def add_vec(index, value):
        vec_grad[index : index + 1, :] += value

    vec_grad[...] = jnp.zeros_like(vec_grad)
    in_b_grad[...] = jnp.zeros_like(in_b_grad)
    key_columns(mseg, mpad, column)

    def query_block(qb):
        def rows_of(count, kb):
            mask_rows(bias, column, seg, qb, kb, count, False)
            run_all(attend_rows(count, kb, qb, cqt, ck, cvt, bias, turned, clse, active, cmixed))

        for_count(seg_s, mseg_s, qb, blocks, rows_of)

    loop(0, blocks, query_block)
    for i in (3, 4, 5, 6, 7):
        copies[i].wait()

    def ffn(i):
        rows = span(i, 1)
        normal1, _ = normalize(first_sum[rows, :])
        first_norm = normal1 * vector(NORM1_G) + vector(NORM1_B)
        summed = first_norm + dot(cmixed[rows, :], w_c[:, 1536:2048]) + vector(CROSS_O_B)
        yield
        normal2, inverse2 = normalize(summed)
        second = normal2 * vector(NORM2_G) + vector(NORM2_B)
        low = second.astype(BF16)
        second_low[rows, :] = low
        third = second + vector(FFN_OUT_B)
        cols = [slice(512 * c, 512 * c + 512) for c in range(4)]

        def hidden(c):
            return dot(low, w_i[:, cols[c]]) + in_b[:, cols[c]]

        def bend(c, value):
            act, slant = gelu_and_slope(value)
            active[rows, cols[c]] = act.astype(BF16)
            slope[rows, cols[c]] = slant.astype(BF16)

        held = [hidden(0), hidden(1)]
        yield
        bend(0, held[0])
        held.append(hidden(2))
        yield
        bend(1, held[1])
        held.append(hidden(3))
        yield
        third = third + dot(active[rows, 0:512], w_o[0:512, :])
        bend(2, held[2])
        yield
        third = third + dot(active[rows, 512:1024], w_o[512:1024, :])
        bend(3, held[3])
        yield
        third = third + dot(active[rows, 1024:2048], w_o[1024:2048, :])
        yield
        normal3, inverse3 = normalize(third)
        layer_out[rows, :] = (normal3 * vector(NORM3_G) + vector(NORM3_B)).astype(BF16)
        grad = out_grad[rows, :].astype(F32)
        add_vec(NORM3_G, column_sum(grad * normal3))
        add_vec(NORM3_B, column_sum(grad))
        d_third = normalize_back(grad, vector(NORM3_G), normal3, inverse3)
        add_vec(FFN_OUT_B, column_sum(d_third))
        third_low = d_third.astype(BF16)
        d_low[rows, :] = third_low
        yield

        def pull(c):
            return dot_nt(third_low, w_o[cols[c], :])

        def straighten(c, value):
            d_hidden = (value * slope[rows, cols[c]].astype(F32)).astype(BF16)
            slope[rows, cols[c]] = d_hidden
            in_b_grad[:, cols[c]] += column_sum(d_hidden.astype(F32))

        held = [pull(0), pull(1)]
        yield
        straighten(0, held[0])
        held.append(pull(2))
        yield
        straighten(1, held[1])
        held.append(pull(3))
        yield
        back = d_third + dot_nt(slope[rows, 0:1024], w_i[:, 0:1024])
        straighten(2, held[2])
        straighten(3, held[3])
        yield
        back = back + dot_nt(slope[rows, 1024:2048], w_i[:, 1024:2048])
        yield
        add_vec(NORM2_G, column_sum(back * normal2))
        add_vec(NORM2_B, column_sum(back))
        d_sum = normalize_back(back, vector(NORM2_G), normal2, inverse2)
        add_vec(CROSS_O_B, column_sum(d_sum))
        d_second[rows, :] = d_sum
        sum_low = d_sum.astype(BF16)
        low_a[rows, :] = sum_low
        yield
        mix_grad = dot_nt(sum_low, w_c[:, 1536:2048]).astype(BF16)
        low_b[rows, :] = mix_grad
        low_bt[:, rows] = mix_grad.T
        delta[:, rows] = row_delta(mix_grad, cmixed[rows, :])
        yield

    interleave([partial(ffn, i) for i in range(blocks)], FFN_SKEW)

    for c in range(4):
        cols = slice(512 * c, 512 * c + 512)
        grads[c] = dot_tn(second_low[...], slope[:, cols]).astype(BF16).reshape(32, 16, 512)
        value = dot_tn(active[:, cols], d_low[...]).astype(BF16).reshape(8, 4, 16, 512)
        for u in range(4):
            grads[4 + u, 8 * c : 8 * c + 8] = value[:, u]
    grads[8] = dot_tn(cmixed[...], low_a[...]).astype(BF16).reshape(32, 16, 512)
    grads_copy = pltpu.make_async_copy(grads, grads_out, out_sem.at[5])
    grads_copy.start()

    for i in range(3):
        copies[i].wait()
    dk[...] = jnp.zeros_like(dk)
    dv[...] = jnp.zeros_like(dv)

    def query_block_back(qb):
        def rows_of(count, kb):
            mask_rows(bias, column, seg, qb, kb, count, False)
            run_all(attend_rows_back(count, kb, qb, cq, cqt, ck, ckt, cv, low_b, low_bt, clse, delta, bias, dqt, dk,
                                     dv, grad4, query4, active, slope))

        for_count(seg_s, mseg_s, qb, blocks, rows_of)

    loop(0, blocks, query_block_back)

    def first_back(i):
        rows = span(i, 1)
        dq_low = (dqt[:, rows] * 0.125).astype(BF16).T
        dk_low = dk[rows, :].astype(BF16)
        dv_low = dv[rows, :].astype(BF16)
        dcq_o[rows, :] = dq_low
        dck_o[rows, :] = dk_low
        dcv_o[rows, :] = dv_low
        yield
        back = d_second[rows, :] + dot_nt(dq_low, w_c[:, 0:512])
        add_vec(CROSS_Q_B, column_sum(dq_low.astype(F32)))
        add_vec(CROSS_V_B, column_sum(dv_low.astype(F32)))
        yield
        memory_grad[rows, :] = (
            dot_nt(dk_low, w_c[:, 512:1024]) + dot_nt(dv_low, w_c[:, 1024:1536])
        ).astype(BF16)
        normal, inverse = normalize(first_sum[rows, :])
        add_vec(NORM1_G, column_sum(back * normal))
        add_vec(NORM1_B, column_sum(back))
        d_sum = normalize_back(back, vector(NORM1_G), normal, inverse)
        add_vec(SELF_O_B, column_sum(d_sum))
        d_second[rows, :] = d_sum
        yield

    interleave([partial(first_back, i) for i in range(blocks)], 1)
    results = [pltpu.make_async_copy(pieces[i], late_out[i], out_sem.at[i]) for i in range(5)]
    for result in results:
        result.start()
    for result in results:
        result.wait()
    grads_copy.wait()


FFN_SKEW = 3


def middle(seg, mseg, mpad, vec, in_b, a, first_sum, w_c, w_i, w_o, out_grad):
    rows, width = out_grad.shape
    wide, turned = (rows, width), (width, rows)
    smem = pl.BlockSpec(memory_space=pltpu.SMEM)
    late = [a["cq"], a["ckt"], a["cv"], first_sum, w_c, w_i, w_o, out_grad]
    outs = [
        jax.ShapeDtypeStruct(wide, BF16),
        jax.ShapeDtypeStruct((9, 32, 16, 512), BF16),
        jax.ShapeDtypeStruct((16, 512), F32),
        jax.ShapeDtypeStruct((1, 2048), F32),
    ]
    outs += [jax.ShapeDtypeStruct(wide, BF16)] * 4 + [jax.ShapeDtypeStruct(wide, F32)]
    scratch = [pltpu.VMEM(b.shape, b.dtype) for b in late]
    scratch += [
        pltpu.VMEM((rows, 128), F32),
        pltpu.VMEM((rows, BLOCK), F32),
        pltpu.VMEM((width, BLOCK), F32),
        pltpu.VMEM(wide, BF16),
        pltpu.VMEM((HEADS, rows), F32),
        pltpu.VMEM((HEADS, rows), F32),
        pltpu.VMEM(wide, BF16),
        pltpu.VMEM(wide, F32),
        pltpu.VMEM(wide, BF16),
        pltpu.VMEM((rows, 2048), BF16),
        pltpu.VMEM((rows, 2048), BF16),
        pltpu.VMEM(turned, F32),
        pltpu.VMEM(wide, F32),
        pltpu.VMEM(wide, F32),
        pltpu.VMEM(wide, BF16),
        pltpu.VMEM(wide, BF16),
        pltpu.VMEM(turned, BF16),
        pltpu.VMEM((2, 4 * BLOCK, 256), BF16),
        pltpu.VMEM((2, 4 * BLOCK, 256), BF16),
        pltpu.VMEM((9, 32, 16, 512), BF16),
        pltpu.SemaphoreType.DMA((8,)),
        pltpu.SemaphoreType.DMA((6,)),
    ]
    return pl.pallas_call(
        middle_kernel,
        out_shape=outs,
        in_specs=[whole(None)] * 3 + [smem] * 2 + [whole(None)] * 5 + [any_space()] * 8,
        out_specs=[whole(None), any_space()] + [whole(None)] * 2 + [any_space()] * 5,
        scratch_shapes=scratch,
        compiler_params=pltpu.CompilerParams(vmem_limit_bytes=VMEM_LIMIT),
        name="layer",
    )(seg, mseg, mpad, seg, mseg, vec, in_b, a["cqt"], a["ck"], a["cvt"], *late)


MADE = 7
READY = UNITS - MADE


def rear(x_ref, m_ref, seg, pad, r, w_s, vec_grad, tokens_grad, made, scratch, arrived, put):
    (column, bias, delta, low, grad, gradt, dv_low, dqt, dk, dv, grad4, query4, prob, slant) = scratch
    blocks = x_ref.shape[0] // BLOCK

    def add_vec(index, value):
        vec_grad[index : index + 1, :] += value

    def unit(index, left, right):
        made[index] = dot_tn(left[...], right[...]).astype(BF16).reshape(made.shape[1:])

    key_columns(seg, pad, column)
    for index, (left, right) in enumerate(((m_ref, r["dck"]), (m_ref, r["dcv"]), (r["first_low"], r["dcq"]))):
        yield ("need", arrived(index))
        unit(index, left, right)
        yield ("cost", 0.7)
        yield ("add", put(index))
    for i in range(blocks):
        rows = span(i, 1)
        sum_low = r["d_first"][rows, :].astype(BF16)
        low[rows, :] = sum_low
        mix_grad = dot_nt(sum_low, w_s[:, 1536:2048]).astype(BF16)
        grad[rows, :] = mix_grad
        gradt[:, rows] = mix_grad.T
        delta[:, rows] = row_delta(mix_grad, r["mixed"][rows, :])
        yield ("cost", 0.5)
    unit(3, r["mixed"], low)
    yield ("cost", 0.7)
    yield ("add", put(3))
    dk[...] = jnp.zeros_like(dk)
    dv[...] = jnp.zeros_like(dv)
    for qb in range(blocks):
        kb, count = document_blocks(qb)
        mask_rows(bias, column, seg, qb, kb, count, True)
        yield from attend_rows_back(count, kb, qb, r["q"], r["qt"], r["k"], r["kt"], r["v"], grad, gradt, r["lse"],
                                    delta, bias, dqt, dk, dv, grad4, query4, prob, slant)
    dq_low, dk_low = grad, low
    for i in range(blocks):
        rows = span(i, 1)
        query = (dqt[:, rows] * 0.125).astype(BF16).T
        value = dv[rows, :].astype(BF16)
        dq_low[rows, :] = query
        dk_low[rows, :] = dk[rows, :].astype(BF16)
        dv_low[rows, :] = value
        add_vec(SELF_Q_B, column_sum(query.astype(F32)))
        add_vec(SELF_V_B, column_sum(value.astype(F32)))
        yield ("cost", 0.3)
    for index, right in ((4, dq_low), (5, dk_low), (6, dv_low)):
        unit(index, x_ref, right)
        yield ("cost", 0.7)
        yield ("add", put(index))
    yield ("add", put(MADE))
    for i in range(blocks):
        rows = span(i, 1)
        tokens_grad[rows, :] = (
            r["d_first"][rows, :]
            + dot_nt(dq_low[rows, :], w_s[:, 0:512])
            + dot_nt(dk_low[rows, :], w_s[:, 512:1024])
            + dot_nt(dv_low[rows, :], w_s[:, 1024:1536])
        ).astype(BF16)
        yield ("cost", 0.6)


def rear_scratch(rows, width):
    wide, turned = (rows, width), (width, rows)
    return [
        pltpu.VMEM((rows, 128), F32),
        pltpu.VMEM((3 * BLOCK, BLOCK), F32),
        pltpu.VMEM((HEADS, rows), F32),
        pltpu.VMEM(wide, BF16),
        pltpu.VMEM(wide, BF16),
        pltpu.VMEM(turned, BF16),
        pltpu.VMEM(wide, BF16),
        pltpu.VMEM(turned, F32),
        pltpu.VMEM(wide, F32),
        pltpu.VMEM(wide, F32),
        pltpu.VMEM((2, 4 * BLOCK, 256), BF16),
        pltpu.VMEM((2, 4 * BLOCK, 256), BF16),
        pltpu.VMEM((3 * BLOCK, HEADS * BLOCK), BF16),
        pltpu.VMEM((3 * BLOCK, HEADS * BLOCK), BF16),
    ]


REAR_IN = ("dck", "dcv", "dcq", "first_low", "d_first", "mixed", "q", "qt", "k", "kt", "v")
SCATTER_START, SCATTER_STEP = 1.1, 4.4


def scatter_kernel(*refs):
    x_ref, m_ref, seg, pad, lse, vec_in, in_b_grad, ready = refs[:8]
    count = len(REAR_IN)
    late_in = refs[8 : 9 + count]
    tokens_grad, sums, vec_sums = refs[9 + count : 12 + count]
    rest = refs[12 + count :]
    late = rest[: count + 1]
    (vec_grad, made, held, in0, in1, in2, in3, in4, g_v, v0, v1, v2, v3, v4, send, recv, keep, late_sem) = rest[
        count + 1 : count + 19
    ]
    scratch = rest[count + 19 :]
    copies = [pltpu.make_async_copy(late_in[i], late[i], late_sem.at[i]) for i in range(count + 1)]
    for item in copies:
        item.start()
    r = dict(zip(REAR_IN, late[:count], strict=True), lse=lse)
    w_s = late[count]
    vec_grad[...] = vec_in[...]
    d, f, me = place()
    greet(d, f)
    inbox = (in0, in1, in2, in3, in4)
    vec_inbox = (v0, v1, v2, v3, v4)
    bits5 = (2,) * 5

    def order(u):
        return tuple(reversed(ORDERS["A" if u == UNITS else UNIT_ORDERS[u]]))

    def copy(u, s):
        bits = order(u)
        gone = bits[:s]
        if u == UNITS:
            index = tuple(me[b] if b in gone else 1 - me[b] if b == bits[s] else slice(None) for b in BITS)
            source, target = g_v.at[index], vec_inbox[s]
        elif s == 0:
            index = (slice(None),) * 4 + (1 - me["c"],)
            source = ready.at[(u,) + index] if u < READY else made.at[(u - READY,) + index]
            target = in0.at[u]
        else:
            index = tuple(me[b] if b in gone else 1 - me[b] if b == bits[s] else slice(None) for b in BITS[:4])
            source, target = held.at[(u,) + index], inbox[s].at[u]
        return pltpu.make_async_remote_copy(
            src_ref=source,
            dst_ref=target,
            send_sem=send.at[u, s],
            recv_sem=recv.at[u, s],
            device_id=partner(bits[s], d, f),
            device_id_type=MESH,
        )

    def own_half(u):
        index = (u,) + (slice(None),) * 4 + (me["c"],)
        return pltpu.make_async_copy(ready.at[index], held.at[u], keep.at[u])

    def add(u, s):
        gone = order(u)[: s + 1]
        if u == UNITS:
            index = tuple(me[b] if b in gone else slice(None) for b in BITS)
            g_v[index] = g_v[index] + vec_inbox[s][...]
        elif s == 0:
            if u < READY:
                own_half(u).wait()
                mine = held[u]
            else:
                mine = made[(u - READY,) + (slice(None),) * 4 + (me["c"],)]
            held[u] = mine + in0[u]
        else:
            index = (u,) + tuple(me[b] if b in gone else slice(None) for b in BITS[:4])
            if s == 4:
                sums[u] = held[index].astype(F32) + in4[u].astype(F32)
            else:
                held[index] = held[index] + inbox[s][u]

    def step(u, s):
        if s == 0 and u < READY:
            own_half(u).start()
        if s == 0 and u == UNITS:
            g_v[...] = pack_vectors(vec_grad[...], in_b_grad[...]).reshape(bits5 + (16, 128))
        if s > 0:
            copy(u, s - 1).wait_recv()
            add(u, s - 1)
        if s < 5:
            copy(u, s).start()

    def steps(u, start, each):
        return [(start + each * s, u, partial(step, u, s)) for s in range(6)]

    events = []
    for u in range(READY):
        events += steps(u, SCATTER_START * u, SCATTER_STEP)

    def put(index):
        return steps(UNITS if index == MADE else READY + index, 0.0, 2.5 if index > 3 else SCATTER_STEP)

    arrivals = {0: (0,), 1: (1,), 2: tuple(range(2, count + 1))}

    def arrived(index):
        def check():
            for i in arrivals[index]:
                copies[i].wait()
            return True

        return check

    merge(events, rear(x_ref, m_ref, seg, pad, r, w_s, vec_grad, tokens_grad, made, scratch, arrived, put))
    for u in range(UNITS + 1):
        for s in range(5):
            copy(u, s).wait_send()
    vec_sums[...] = g_v[tuple(me[b] for b in BITS)]


def scatter_rear(tokens, memory, seg, pad, lse, vec_grad, in_b_grad, ready, late, w_s):
    rows, width = tokens.shape
    bits = (2,) * 5
    unit = (16, 512)
    vec_unit = (16, 128)
    boxes = [(UNITS,) + (2,) * (4 - s) + unit for s in range(5)]
    return pl.pallas_call(
        scatter_kernel,
        out_shape=[
            jax.ShapeDtypeStruct((rows, width), BF16),
            jax.ShapeDtypeStruct((UNITS,) + unit, F32),
            jax.ShapeDtypeStruct(vec_unit, F32),
        ],
        in_specs=[whole(None)] * 7 + [any_space()] * (2 + len(late)),
        out_specs=[whole(None)] * 3,
        scratch_shapes=[pltpu.VMEM(b.shape, b.dtype) for b in late]
        + [pltpu.VMEM(w_s.shape, BF16), pltpu.VMEM((16, 512), F32)]
        + [pltpu.VMEM((MADE,) + bits + unit, BF16), pltpu.VMEM((UNITS,) + (2,) * 4 + unit, BF16)]
        + [pltpu.VMEM(b, BF16) for b in boxes]
        + [pltpu.VMEM(bits + vec_unit, F32)]
        + [pltpu.VMEM((2,) * (4 - s) + vec_unit, F32) for s in range(5)]
        + [
            pltpu.SemaphoreType.DMA((UNITS + 1, 5)),
            pltpu.SemaphoreType.DMA((UNITS + 1, 5)),
            pltpu.SemaphoreType.DMA((READY,)),
            pltpu.SemaphoreType.DMA((len(late) + 1,)),
        ]
        + rear_scratch(rows, width),
        compiler_params=pltpu.CompilerParams(
            collective_id=2, has_side_effects=True, vmem_limit_bytes=VMEM_LIMIT
        ),
        name="scatter_rear",
    )(tokens, memory, seg, pad, lse, vec_grad, in_b_grad, ready.reshape((READY,) + bits + unit), *late, w_s)


def rear_kernel(*refs):
    x_ref, m_ref, seg, pad, lse, vec_in = refs[:6]
    count = len(REAR_IN)
    r = dict(zip(REAR_IN, refs[6 : 6 + count], strict=True), lse=lse)
    w_s, tokens_grad, vec_grad, made = refs[6 + count : 10 + count]
    vec_grad[...] = vec_in[...]
    run_all(rear(x_ref, m_ref, seg, pad, r, w_s, vec_grad, tokens_grad, made, refs[10 + count :], lambda i: None,
                 lambda i: None))


def rear_only(tokens, memory, seg, pad, lse, vec_grad, late, w_s):
    rows, width = tokens.shape
    return pl.pallas_call(
        rear_kernel,
        out_shape=[
            jax.ShapeDtypeStruct((rows, width), BF16),
            jax.ShapeDtypeStruct((16, 512), F32),
            jax.ShapeDtypeStruct((MADE, 512, 512), BF16),
        ],
        in_specs=[whole(None)] * (7 + len(late)),
        out_specs=[whole(None)] * 3,
        scratch_shapes=rear_scratch(rows, width),
        compiler_params=pltpu.CompilerParams(vmem_limit_bytes=VMEM_LIMIT),
        name="rear",
    )(tokens, memory, seg, pad, lse, vec_grad, *late, w_s)


def pack_vectors(vec_grad, in_b_grad):
    row = lax.broadcasted_iota(jnp.int32, (32, 16, 512), 0)
    col = lax.broadcasted_iota(jnp.int32, (32, 16, 512), 2)
    own = jnp.where(row == col // 16, jnp.broadcast_to(vec_grad[None], (32, 16, 512)), 0.0)
    column = lax.broadcasted_iota(jnp.int32, (512, 128), 0)
    lane = lax.broadcasted_iota(jnp.int32, (512, 128), 1)
    pick = jnp.where((lane == column % 16) & (lane < 16), 1.0, 0.0).astype(BF16)
    packed = dot(own.reshape(512, 512).astype(BF16), pick)
    row = lax.broadcasted_iota(jnp.int32, (32, 2048), 0)
    col = lax.broadcasted_iota(jnp.int32, (32, 2048), 1)
    own = jnp.where(row == col // 64, jnp.broadcast_to(in_b_grad, (32, 2048)), 0.0).astype(BF16)
    column = lax.broadcasted_iota(jnp.int32, (2048, 128), 0)
    lane = lax.broadcasted_iota(jnp.int32, (2048, 128), 1)
    pick = jnp.where((lane == column % 64) & (lane < 64), 1.0, 0.0).astype(BF16)
    wide = dot(own, pick).astype(BF16)
    target = lax.broadcasted_iota(jnp.int32, (512, 32), 0)
    device = lax.broadcasted_iota(jnp.int32, (512, 32), 1)
    choose = jnp.where(target == device * 16 + FFN_IN_B, 1.0, 0.0).astype(BF16)
    return packed + dot(choose, wide)


def unpack_kernel(sums, vec_sums, *outs):
    matrices, vectors = outs[:10], outs[10:]
    for i, u in enumerate((13, 14, 15, 12, 11, 9, 10, 8)):
        matrices[i][...] = sums[u]
    for u in range(4):
        matrices[8][:, 512 * u : 512 * u + 512] = sums[u]
        matrices[9][16 * u : 16 * u + 16, :] = sums[4 + u]
    for i in range(13):
        vectors[i][...] = vec_sums[i : i + 1, 0:16]
    vectors[13][...] = vec_sums[FFN_IN_B : FFN_IN_B + 1, 0:64]


def unpack(sums, vec_sums):
    shapes = [(16, 512)] * 8 + [(16, 2048), (64, 512)] + [(1, 16)] * 13 + [(1, 64)]
    return pl.pallas_call(
        unpack_kernel,
        out_shape=[jax.ShapeDtypeStruct(s, F32) for s in shapes],
        in_specs=[whole(None)] * 2,
        out_specs=[whole(None)] * len(shapes),
        name="unpack",
    )(sums, vec_sums)


def local(
    tokens, memory, token_seg, token_pad, memory_seg, memory_pad, out_grad,
    self_q_w, self_q_b, self_k_w, self_v_w, self_v_b, self_o_w, self_o_b, norm1_gain, norm1_bias,
    cross_q_w, cross_q_b, cross_k_w, cross_v_w, cross_v_b, cross_o_w, cross_o_b, norm2_gain, norm2_bias,
    ffn_in_w, ffn_in_b, ffn_out_w, ffn_out_b, norm3_gain, norm3_bias, *, ring,
):
    vectors = (self_q_b, self_v_b, self_o_b, norm1_gain, norm1_bias, cross_q_b, cross_v_b, cross_o_b,
               norm2_gain, norm2_bias, ffn_out_b, norm3_gain, norm3_bias)
    shards = (self_q_w, self_k_w, self_v_w, self_o_w, cross_q_w, cross_k_w, cross_v_w, cross_o_w,
              ffn_in_w, ffn_out_w)
    if ring:
        packed = jnp.concatenate(
            [
                jnp.pad(jnp.stack(vectors), ((0, 2), (0, 112))),
                jnp.pad(ffn_in_b.reshape(1, 64), ((0, 0), (0, 64))),
            ]
        )
        w_s, w_c, w_i, w_o, vec, in_b, lse, fronts = gather_front(
            tokens, memory, token_seg, token_pad, packed, shards
        )
    else:
        get = partial(lax.all_gather, axis_name=AXES, axis=0, tiled=True)
        full = [get(w) for w in shards]
        w_s, w_c = jnp.concatenate(full[:4], 1), jnp.concatenate(full[4:8], 1)
        w_i, w_o = full[8:]
        vec = jnp.pad(jnp.stack([get(b) for b in vectors]).astype(F32), ((0, 3), (0, 0)))
        in_b = get(ffn_in_b).astype(F32).reshape(1, -1)
        lse, fronts = front_only(tokens, memory, token_seg, token_pad, vec, w_s, w_c)
    a = dict(zip(FRONT, fronts[:-1], strict=True))
    layer_out, ready, vec_grad, in_b_grad, dcq, dck, dcv, memory_grad, d_first = middle(
        token_seg, memory_seg, memory_pad, vec, in_b, a, fronts[-1], w_c, w_i, w_o, out_grad
    )
    late = [dck, dcv, dcq, a["first_low"], d_first, a["mixed"], a["q"], a["qt"], a["k"], a["kt"], a["v"]]
    if ring:
        tokens_grad, sums, vec_sums = scatter_rear(
            tokens, memory, token_seg, token_pad, lse, vec_grad, in_b_grad, ready, late, w_s
        )
        results = unpack(sums, vec_sums)
        mats, vecs = results[:10], [v.reshape(-1) for v in results[10:]]
    else:
        give = partial(lax.psum_scatter, axis_name=AXES, scatter_dimension=0, tiled=True)
        tokens_grad, vec_grad, made = rear_only(tokens, memory, token_seg, token_pad, lse, vec_grad, late, w_s)
        made = made.astype(F32)
        done = ready.astype(F32).reshape(9, 512, 512)
        in_w = done[:4].transpose(1, 0, 2).reshape(512, 2048)
        out_w = done[4:8].reshape(4, 32, 16, 512).transpose(1, 0, 2, 3).reshape(2048, 512)
        full = [made[4], made[5], made[6], made[3], made[2], made[0], made[1], done[8], in_w, out_w]
        mats = [give(g) for g in full]
        vecs = [give(vec_grad[i]) for i in range(13)] + [give(in_b_grad[0])]
    (g_sqw, g_skw, g_svw, g_sow, g_cqw, g_ckw, g_cvw, g_cow, g_iw, g_ow) = mats
    (g_sqb, g_svb, g_sob, g_n1g, g_n1b, g_cqb, g_cvb, g_cob, g_n2g, g_n2b, g_ob, g_n3g, g_n3b, g_ib) = vecs
    return (
        layer_out, tokens_grad, memory_grad,
        g_sqw, g_sqb, g_skw, g_svw, g_svb, g_sow, g_sob, g_n1g, g_n1b,
        g_cqw, g_cqb, g_ckw, g_cvw, g_cvb, g_cow, g_cob, g_n2g, g_n2b,
        g_iw, g_ib, g_ow, g_ob, g_n3g, g_n3b,
    )


def solution(mesh):
    ring = mesh.shape["dp"] == 8 and mesh.shape["fsdp"] == 4
    matrix, vector = P(AXES, None), P(AXES)
    return jax.shard_map(
        partial(local, ring=ring),
        mesh=mesh,
        in_specs=(
            (matrix,) * 7
            + (matrix, vector, matrix, matrix, vector, matrix, vector, vector, vector) * 2
            + (matrix, vector, matrix, vector, vector, vector)
        ),
        out_specs=(
            (matrix,) * 3
            + (matrix, vector, matrix, matrix, vector, matrix, vector, vector, vector) * 2
            + (matrix, vector, matrix, vector, vector, vector)
        ),
        check_vma=False,
    )
```

```python
from functools import partial

import jax
import jax.numpy as jnp
from jax import lax
from jax.experimental import pallas as pl
from jax.experimental.pallas import tpu as pltpu
from jax.sharding import PartitionSpec as P

HEADS = 8
EPSILON = 1e-05
MASKED = -1e30
AXES = ("dp", "fsdp")
MESH = pl.DeviceIdType.MESH
BF16 = jnp.bfloat16
F32 = jnp.float32
BLOCK = 256
VMEM_LIMIT = 62 << 20

(SELF_Q_B, SELF_V_B, SELF_O_B, NORM1_G, NORM1_B, CROSS_Q_B, CROSS_V_B, CROSS_O_B,
 NORM2_G, NORM2_B, FFN_OUT_B, NORM3_G, NORM3_B) = range(13)
FFN_IN_B = 15

BITS = ("zh", "zl", "y", "x", "c")
ORDERS = {
    "A": ("zh", "zl", "x", "y", "c"),
    "B": ("zh", "zl", "y", "x", "c"),
    "C": ("x", "zh", "zl", "y", "c"),
    "D": ("y", "zh", "zl", "x", "c"),
}
GATHER_ORDERS = "ABABABCDCDCDCDCD"
SCATTER_ORDERS = "ABCDABCDABCDABCD"
UNITS = 16


def dot(left, right):
    return jnp.dot(left, right, preferred_element_type=F32)


def dot_nt(left, right):
    return lax.dot_general(left, right, (((1,), (1,)), ((), ())), preferred_element_type=F32)


def dot_tn(left, right):
    return lax.dot_general(left, right, (((0,), (0,)), ((), ())), preferred_element_type=F32)


def rows_at(index, size):
    return pl.ds(pl.multiple_of(index * size, size), size)


def loop(low, high, body):
    def step(index, carry):
        body(index)
        return carry

    lax.fori_loop(low, high, step, 0)


def whole(shape):
    return pl.BlockSpec(memory_space=pltpu.VMEM)


def any_space():
    return pl.BlockSpec(memory_space=pl.ANY)


def place():
    d = lax.axis_index("dp")
    f = lax.axis_index("fsdp")
    return d, f, {"zh": d // 4, "zl": (d // 2) % 2, "y": d % 2, "x": f // 2, "c": f % 2}


def flip(value, mask):
    return value + mask - 2 * mask * ((value // mask) % 2)


def partner(bit, d, f):
    return {
        "zh": (flip(d, 4), f),
        "zl": (flip(d, 2), f),
        "y": (flip(d, 1), f),
        "x": (d, flip(f, 2)),
        "c": (d, flip(f, 1)),
    }[bit]


def greet(d, f):
    barrier = pltpu.get_barrier_semaphore()
    for bit in BITS:
        pl.semaphore_signal(barrier, inc=1, device_id=partner(bit, d, f), device_id_type=MESH)
    pl.semaphore_wait(barrier, len(BITS))


def spread_vectors(packed, vec_ref, in_b_ref):
    flat = packed.reshape(512, 128)
    lane = lax.broadcasted_iota(jnp.int32, (128, 512), 0)
    column = lax.broadcasted_iota(jnp.int32, (128, 512), 1)
    pick = jnp.where((lane == column % 16) & (lane < 16), 1.0, 0.0).astype(BF16)
    spread = dot(flat, pick)
    row = lax.broadcasted_iota(jnp.int32, (512, 512), 0)
    col = lax.broadcasted_iota(jnp.int32, (512, 512), 1)
    kept = jnp.where(row // 16 == col // 16, spread, 0.0)
    vec_ref[...] = jnp.sum(kept.reshape(32, 16, 512), axis=0)
    device = lax.broadcasted_iota(jnp.int32, (32, 512), 0)
    source = lax.broadcasted_iota(jnp.int32, (32, 512), 1)
    choose = jnp.where(source == device * 16 + FFN_IN_B, 1.0, 0.0).astype(BF16)
    own = dot(choose, flat).astype(BF16)
    lane = lax.broadcasted_iota(jnp.int32, (128, 2048), 0)
    column = lax.broadcasted_iota(jnp.int32, (128, 2048), 1)
    pick = jnp.where((lane == column % 64) & (lane < 64), 1.0, 0.0).astype(BF16)
    spread = dot(own, pick)
    row = lax.broadcasted_iota(jnp.int32, (32, 2048), 0)
    col = lax.broadcasted_iota(jnp.int32, (32, 2048), 1)
    in_b_ref[...] = jnp.sum(jnp.where(row == col // 64, spread, 0.0), axis=0, keepdims=True)


def merge(events, compute):
    events = sorted(events, key=lambda e: e[:2])
    now, waiting = 0.0, None
    while events or compute is not None:
        if waiting is not None and waiting():
            waiting = None
        blocked = waiting is not None or compute is None
        if events and (blocked or events[0][0] <= now):
            time, _, step = events.pop(0)
            if waiting is not None:
                now = max(now, time)
            step()
            continue
        try:
            kind, value = next(compute)
        except StopIteration:
            compute = None
            continue
        if kind == "cost":
            now += value
        elif kind == "need":
            waiting = value
        else:
            events += [(now + time, number, step) for time, number, step in value]
            events.sort(key=lambda e: e[:2])


def interleave(makers, skew):
    running = [maker() for maker in makers]
    done = [False] * len(running)
    time = 0
    while not all(done):
        for i, piece in enumerate(running):
            if not done[i] and time >= i * skew:
                asked = next(piece, True)
                done[i] = asked is True
                yield asked if isinstance(asked, tuple) else ("cost", 0.25)
        time += 1


def run_all(compute):
    for _ in compute:
        pass


def span(index, count):
    if isinstance(index, int):
        return slice(index * BLOCK, (index + count) * BLOCK)
    return pl.ds(pl.multiple_of(index * BLOCK, BLOCK), count * BLOCK)


def key_columns(seg_ref, pad_ref, column_ref):
    open_seg = jnp.where(pad_ref[...] == 0, seg_ref[...], -1).astype(F32)
    for i in range(seg_ref.shape[1] // 128):
        piece = jnp.broadcast_to(open_seg[:, 128 * i : 128 * i + 128], (128, 128)).T
        column_ref[128 * i : 128 * i + 128, :] = piece


def mask_rows(bias_ref, column_ref, seg_ref, qb, kb, count, causal):
    query = seg_ref[:, span(qb, 1)].astype(F32)
    column = column_ref[span(kb, count), :]
    allowed = jnp.concatenate([column] * (BLOCK // 128), axis=1) == query
    if causal:
        shape = (count * BLOCK, BLOCK)
        key_pos = kb * BLOCK + lax.broadcasted_iota(jnp.int32, shape, 0)
        query_pos = qb * BLOCK + lax.broadcasted_iota(jnp.int32, shape, 1)
        allowed = (allowed & (key_pos < query_pos)) | (key_pos == query_pos)
    bias_ref[0 : count * BLOCK, :] = jnp.where(allowed, 0.0, MASKED)


def own_lanes(value, head):
    lane = lax.broadcasted_iota(jnp.int32, value.shape, 1)
    return jnp.where(lane // 64 == head, value, jnp.zeros_like(value))


def attend_rows(count, kb, qb, qt_ref, k_ref, vt_ref, bias_ref, turned_ref, lse_ref, prob_ref, out_ref):
    rows, keys, size = span(qb, 1), span(kb, count), count * BLOCK

    def scores(h):
        part = slice(64 * h, 64 * h + 64)
        return dot(k_ref[keys, part], qt_ref[part, rows])

    def spot(h):
        return (slice(0, size), slice(BLOCK * h, BLOCK * h + BLOCK))

    def product(h, total):
        part = slice(64 * h, 64 * h + 64)
        turned_ref[part, :] = dot(vt_ref[part, keys], prob_ref[spot(h)]) * (1.0 / total)

    held = {h: scores(h) for h in range(2)}
    pending = []
    for h in range(HEADS):
        if h + 2 < HEADS:
            held[h + 2] = scores(h + 2)
        if len(pending) >= 5:
            product(*pending.pop(0))
        score = held.pop(h) + bias_ref[0:size, :]
        top = jnp.max(score, axis=0, keepdims=True)
        prob = jnp.exp(score - top)
        total = jnp.sum(prob, axis=0, keepdims=True)
        prob_ref[spot(h)] = prob.astype(BF16)
        lse_ref[h : h + 1, rows] = top + jnp.log(total)
        pending.append((h, total))
        yield ("cost", 0.1 * count)
    for item in pending:
        product(*item)
    out_ref[rows, :] = turned_ref[...].astype(BF16).T
    yield ("cost", 0.3)


def attend_rows_back(count, kb, qb, q_ref, qt_ref, k_ref, kt_ref, v_ref, g_ref, gt_ref, lse_ref, delta_ref, bias_ref,
                     dqt_ref, dk_ref, dv_ref, grad_ref, query_ref, prob_ref, slant_ref, fresh=True):
    rows, keys, size = span(qb, 1), span(kb, count), count * BLOCK

    def scores(h):
        part = slice(64 * h, 64 * h + 64)
        return (dot(k_ref[keys, part], qt_ref[part, rows]), dot(v_ref[keys, part], gt_ref[part, rows]))

    for slab in range(2):
        lanes = slice(256 * slab, 256 * slab + 256)
        for j in range(4):
            here = slice(BLOCK * j, BLOCK * j + BLOCK)
            grad_ref[slab, here, :] = own_lanes(g_ref[rows, lanes], j)
            query_ref[slab, here, :] = own_lanes(q_ref[rows, lanes], j)

    def tail(slab):
        lanes = slice(256 * slab, 256 * slab + 256)
        four = slice(4 * BLOCK * slab, 4 * BLOCK * slab + 4 * BLOCK)
        dv_ref[keys, lanes] += dot(prob_ref[0:size, four], grad_ref[slab])
        dk_ref[keys, lanes] += dot(slant_ref[0:size, four], query_ref[slab])
        for h in range(4 * slab, 4 * slab + 4):
            part = slice(64 * h, 64 * h + 64)
            product = dot(kt_ref[part, keys], slant_ref[0:size, BLOCK * h : BLOCK * h + BLOCK])
            dqt_ref[part, rows] = product if fresh else dqt_ref[part, rows] + product

    held = {h: scores(h) for h in range(2)}
    for h in range(HEADS):
        if h + 2 < HEADS:
            held[h + 2] = scores(h + 2)
        if h == 6:
            tail(0)
        score, grad = held.pop(h)
        mine, here = slice(h, h + 1), slice(BLOCK * h, BLOCK * h + BLOCK)
        prob = jnp.exp(score + bias_ref[0:size, :] - lse_ref[mine, rows])
        prob_ref[0:size, here] = prob.astype(BF16)
        slant_ref[0:size, here] = (prob * (grad - delta_ref[mine, rows])).astype(BF16)
        yield ("cost", 0.17 * count)
    tail(1)
    yield ("cost", 0.1)


def document_blocks(qb):
    first = max(0, (qb * BLOCK - 511) // BLOCK)
    return first, qb + 1 - first


FRONT = ("q", "qt", "k", "kt", "v", "mixed", "first_low", "cq", "cqt", "ck", "ckt", "cv", "g", "gt")
FRONT_WIDE = ("first_sum", "d_second")
TURNED = ("qt", "kt", "cqt", "ckt", "gt")
FFN_SKEW = 3


def front(inputs, weight, need, vec_ref, in_b, a, t, outs, put):
    x_ref, m_ref, seg, pad, mseg, mpad, out_grad = inputs
    lse, clse, delta, layer_out, vec_grad, in_b_grad, ready = outs
    blocks = x_ref.shape[0] // BLOCK
    vt, column, bias, turned, active = t["vt"], t["column"], t["bias"], t["turned"], t["active"]
    first_sum = a["first_sum"]

    def vector(index):
        return vec_ref[index : index + 1, :]

    def add_vec(index, value):
        vec_grad[index : index + 1, :] += value

    def project(source, kind, index, bias_row, straight, turned_to, scale=None):
        yield ("need", lambda: need(kind, index))
        for i in range(blocks):
            rows = span(i, 1)
            value = dot(source[rows, :], weight(kind, index))
            if bias_row is not None:
                value = value + vector(bias_row)
            value = value.astype(BF16)
            if scale is not None:
                value = value * scale
            if straight is not None:
                straight[rows, :] = value
            if turned_to is not None:
                turned_to[:, rows] = value.T
            yield ("cost", 0.25)

    vec_grad[...] = jnp.zeros_like(vec_grad)
    in_b_grad[...] = jnp.zeros_like(in_b_grad)
    key_columns(seg, pad, column)
    yield ("need", lambda: need("v", 0))
    yield from project(x_ref, "s", 0, SELF_Q_B, a["q"], a["qt"], 0.125)
    yield from project(x_ref, "s", 1, None, a["k"], a["kt"])
    yield from project(x_ref, "s", 2, SELF_V_B, a["v"], vt)
    put("q", "qt", "k", "kt", "v")
    for qb in range(blocks):
        kb, count = document_blocks(qb)
        mask_rows(bias, column, seg, qb, kb, count, True)
        yield from attend_rows(count, kb, qb, a["qt"], a["k"], vt, bias, turned, lse, active, a["mixed"])
    put("mixed")
    yield ("need", lambda: need("s", 3))
    for i in range(blocks):
        rows = span(i, 1)
        summed = x_ref[rows, :].astype(F32) + dot(a["mixed"][rows, :], weight("s", 3)) + vector(SELF_O_B)
        first_sum[rows, :] = summed
        normal, _ = normalize(summed)
        a["first_low"][rows, :] = (normal * vector(NORM1_G) + vector(NORM1_B)).astype(BF16)
        yield ("cost", 0.4)
    put("first_low", "first_sum")
    yield from project(m_ref, "c", 1, None, a["ck"], a["ckt"])
    yield from project(m_ref, "c", 2, CROSS_V_B, a["cv"], vt)
    put("ck", "ckt", "cv")
    yield from project(a["first_low"], "c", 0, CROSS_Q_B, a["cq"], a["cqt"], 0.125)
    put("cq", "cqt")
    key_columns(mseg, mpad, column)
    cmixed, second_low, d_low, slope, low_a = (t[n] for n in ("cmixed", "second_low", "d_low", "slope", "low_a"))
    for qb in range(blocks):
        mask_rows(bias, column, seg, qb, 0, blocks, False)
        yield from attend_rows(blocks, 0, qb, a["cqt"], a["ck"], vt, bias, turned, clse, active, cmixed)
    yield ("need", lambda: need("c", 3) and all(need("i", i) for i in range(4)))

    def ffn(i):
        rows = span(i, 1)
        normal1, _ = normalize(first_sum[rows, :])
        first_norm = normal1 * vector(NORM1_G) + vector(NORM1_B)
        summed = first_norm + dot(cmixed[rows, :], weight("c", 3)) + vector(CROSS_O_B)
        yield
        normal2, inverse2 = normalize(summed)
        second = normal2 * vector(NORM2_G) + vector(NORM2_B)
        low = second.astype(BF16)
        second_low[rows, :] = low
        third = second + vector(FFN_OUT_B)
        cols = [slice(512 * c, 512 * c + 512) for c in range(4)]

        def hidden(c):
            return dot(low, weight("i", c)) + in_b[:, cols[c]]

        def bend(c, value):
            act, slant = gelu_and_slope(value)
            active[rows, cols[c]] = act.astype(BF16)
            slope[rows, cols[c]] = slant.astype(BF16)

        held = [hidden(0), hidden(1)]
        yield
        bend(0, held[0])
        held.append(hidden(2))
        yield
        bend(1, held[1])
        held.append(hidden(3))
        yield
        if i == 0:
            yield ("need", lambda: all(need("o", u) for u in range(4)))
        third = third + dot(active[rows, cols[0]], weight("o", 0))
        bend(2, held[2])
        yield
        third = third + dot(active[rows, cols[1]], weight("o", 1))
        bend(3, held[3])
        yield
        third = third + dot(active[rows, cols[2]], weight("o", 2)) + dot(active[rows, cols[3]], weight("o", 3))
        yield
        normal3, inverse3 = normalize(third)
        layer_out[rows, :] = (normal3 * vector(NORM3_G) + vector(NORM3_B)).astype(BF16)
        grad = out_grad[rows, :].astype(F32)
        add_vec(NORM3_G, column_sum(grad * normal3))
        add_vec(NORM3_B, column_sum(grad))
        d_third = normalize_back(grad, vector(NORM3_G), normal3, inverse3)
        add_vec(FFN_OUT_B, column_sum(d_third))
        third_low = d_third.astype(BF16)
        d_low[rows, :] = third_low
        yield

        def pull(c):
            return dot_nt(third_low, weight("o", c))

        def straighten(c, value):
            d_hidden = (value * slope[rows, cols[c]].astype(F32)).astype(BF16)
            slope[rows, cols[c]] = d_hidden
            in_b_grad[:, cols[c]] += column_sum(d_hidden.astype(F32))

        held = [pull(0), pull(1)]
        yield
        straighten(0, held[0])
        held.append(pull(2))
        yield
        straighten(1, held[1])
        held.append(pull(3))
        yield
        back = d_third + dot_nt(slope[rows, cols[0]], weight("i", 0))
        straighten(2, held[2])
        yield
        back = back + dot_nt(slope[rows, cols[1]], weight("i", 1))
        straighten(3, held[3])
        yield
        back = back + dot_nt(slope[rows, cols[2]], weight("i", 2)) + dot_nt(slope[rows, cols[3]], weight("i", 3))
        yield
        add_vec(NORM2_G, column_sum(back * normal2))
        add_vec(NORM2_B, column_sum(back))
        d_sum = normalize_back(back, vector(NORM2_G), normal2, inverse2)
        add_vec(CROSS_O_B, column_sum(d_sum))
        a["d_second"][rows, :] = d_sum
        sum_low = d_sum.astype(BF16)
        low_a[rows, :] = sum_low
        yield
        mix_grad = dot_nt(sum_low, weight("c", 3)).astype(BF16)
        a["g"][rows, :] = mix_grad
        a["gt"][:, rows] = mix_grad.T
        delta[:, rows] = row_delta(mix_grad, cmixed[rows, :])
        yield

    yield from interleave([partial(ffn, i) for i in range(blocks)], FFN_SKEW)
    put("d_second", "g", "gt")
    for c in range(4):
        cols = slice(512 * c, 512 * c + 512)
        ready[c] = dot_tn(second_low[...], slope[:, cols]).astype(BF16).reshape(32, 16, 512)
        value = dot_tn(active[:, cols], d_low[...]).astype(BF16).reshape(8, 4, 16, 512)
        for u in range(4):
            ready[4 + u, 8 * c : 8 * c + 8] = value[:, u]
    ready[8] = dot_tn(cmixed[...], low_a[...]).astype(BF16).reshape(32, 16, 512)


def front_shape(name, rows, width):
    return (width, rows) if name in TURNED else (rows, width)


FRONT_SCRATCH = ("vt", "column", "bias", "turned", "active", "cmixed", "second_low", "d_low", "slope", "low_a")


def front_scratch(rows, width):
    wide = (rows, width)
    return (
        [pltpu.VMEM(front_shape(name, rows, width), BF16) for name in FRONT]
        + [pltpu.VMEM(wide, F32) for _ in FRONT_WIDE]
        + [
            pltpu.SemaphoreType.DMA((len(FRONT) + len(FRONT_WIDE) + 1,)),
            pltpu.VMEM((9, 32, 16, 512), BF16),
            pltpu.VMEM((width, rows), BF16),
            pltpu.VMEM((rows, 128), F32),
            pltpu.VMEM((rows, BLOCK), F32),
            pltpu.VMEM((width, BLOCK), F32),
            pltpu.VMEM((rows, 2048), BF16),
            pltpu.VMEM(wide, BF16),
            pltpu.VMEM(wide, BF16),
            pltpu.VMEM(wide, BF16),
            pltpu.VMEM((rows, 2048), BF16),
            pltpu.VMEM(wide, BF16),
        ]
    )


def front_outs(rows, width):
    rowwise = jax.ShapeDtypeStruct((HEADS, rows), F32)
    return (
        [rowwise] * 3
        + [
            jax.ShapeDtypeStruct((rows, width), BF16),
            jax.ShapeDtypeStruct((16, 512), F32),
            jax.ShapeDtypeStruct((1, 2048), F32),
            jax.ShapeDtypeStruct((9, 32, 16, 512), BF16),
        ]
        + [jax.ShapeDtypeStruct(front_shape(name, rows, width), BF16) for name in FRONT]
        + [jax.ShapeDtypeStruct((rows, width), F32) for _ in FRONT_WIDE]
    )


N_SMALL = 6
N_FRONT_OUT = N_SMALL + 1 + len(FRONT) + len(FRONT_WIDE)


def run_front(inputs, weight, need, vec_ref, in_b, outs, scratch, events):
    names = FRONT + FRONT_WIDE
    count = len(names)
    a = dict(zip(names, scratch[:count], strict=True))
    sem, ready = scratch[count : count + 2]
    t = dict(zip(FRONT_SCRATCH, scratch[count + 2 :], strict=True))
    copies = {n: pltpu.make_async_copy(a[n], outs[N_SMALL + 1 + i], sem.at[i]) for i, n in enumerate(names)}

    def put(*which):
        for name in which:
            copies[name].start()

    merge(events, front(inputs, weight, need, vec_ref, in_b, a, t, [*outs[:N_SMALL], ready], put))
    last = pltpu.make_async_copy(ready, outs[N_SMALL], sem.at[count])
    last.start()
    for name in names:
        copies[name].wait()
    last.wait()


UNIT_PLACES = (
    [("s", 0), ("s", 1), ("s", 2), ("s", 3), ("c", 1), ("c", 2), ("c", 0), ("c", 3)]
    + [("i", i) for i in range(4)]
    + [("o", i) for i in range(4)]
)
GATHER_START, GATHER_STEP, GATHER_FIRST_STEP, GATHER_PAUSE = 1.1, 4.4, 2.5, 0.0


def gather_kernel(*refs):
    inputs, packed, shards = refs[:7], refs[7], refs[8:18]
    o_s, o_c, vec_out, in_b = refs[18:22]
    outs = refs[22 : 22 + N_FRONT_OUT]
    rest = refs[22 + N_FRONT_OUT :]
    b_s, b_c, b_i, b_o, b_v = rest[:5]
    send, recv, keep = rest[5:8]
    d, f, me = place()
    own = tuple(me[bit] for bit in BITS)
    for i in range(4):
        b_s[own + (slice(None), slice(512 * i, 512 * i + 512))] = shards[i][...]
        b_c[own + (slice(None), slice(512 * i, 512 * i + 512))] = shards[4 + i][...]
    b_i[own] = shards[8][...]
    b_o[own] = shards[9][...]
    b_v[own] = packed[...]
    greet(d, f)

    buffers = {"s": b_s, "c": b_c, "i": b_i, "o": b_o}
    targets = {"s": o_s, "c": o_c}
    finished = set()

    def part(u, index):
        kind, i = UNIT_PLACES[u]
        if kind == "o":
            return index + (slice(16 * i, 16 * i + 16), slice(None))
        return index + (slice(None), slice(512 * i, 512 * i + 512))

    def copy(u, s):
        order = ORDERS["A" if u == UNITS else GATHER_ORDERS[u]]
        have = order[:s]
        index = tuple(slice(None) if bit in have else me[bit] for bit in BITS)
        buffer = b_v
        if u < UNITS:
            index, buffer = part(u, index), buffers[UNIT_PLACES[u][0]]
        return pltpu.make_async_remote_copy(
            src_ref=buffer.at[index],
            dst_ref=buffer.at[index],
            send_sem=send.at[u, s],
            recv_sem=recv.at[u, s],
            device_id=partner(order[s], d, f),
            device_id_type=MESH,
        )

    def store(u):
        kind = UNIT_PLACES[u][0]
        index = part(u, (slice(None),) * 5)
        return pltpu.make_async_copy(buffers[kind].at[index], targets[kind].at[index], keep.at[u])

    def step(u, s):
        if s > 0:
            copy(u, s - 1).wait_recv()
        if s < 5:
            copy(u, s).start()
            return
        if u == UNITS:
            pl.when(d >= 0)(lambda: spread_vectors(b_v[...].reshape(32, 16, 128), vec_out, in_b))
        elif u < 8:
            store(u).start()
        finished.add(u)

    events = []
    for u in range(UNITS + 1):
        start = 0.0 if u == UNITS else 0.1 + u * GATHER_START + (GATHER_PAUSE if u > 3 else 0.0)
        each = GATHER_FIRST_STEP if u == UNITS or u < 4 else GATHER_STEP
        events += [(start + each * s, u, partial(step, u, s)) for s in range(6)]

    unit_of = {place: u for u, place in enumerate(UNIT_PLACES)}
    unit_of["v", 0] = UNITS

    def weight(kind, i):
        if kind == "o":
            return b_o[i // 2, i % 2].reshape(512, 512)
        return buffers[kind][:, :, :, :, :, :, 512 * i : 512 * i + 512].reshape(512, 512)

    run_front(inputs, weight, lambda kind, i: unit_of[kind, i] in finished, vec_out, in_b, outs, rest[8:], events)
    for u in range(UNITS + 1):
        for s in range(5):
            copy(u, s).wait_send()
        if u < 8:
            store(u).wait()


def gather_front(inputs, packed, shards):
    rows, width = inputs[0].shape
    bits = (2,) * 5
    weights = [bits + (16, 2048)] * 3 + [bits + (64, 512)]
    shapes = [jax.ShapeDtypeStruct(s, BF16) for s in weights[:2]]
    shapes += [jax.ShapeDtypeStruct((16, 512), F32), jax.ShapeDtypeStruct((1, 2048), F32)]
    shapes += front_outs(rows, width)
    result = pl.pallas_call(
        gather_kernel,
        out_shape=shapes,
        in_specs=[whole(None)] * 18,
        out_specs=[any_space()] * 2 + [whole(None)] * (2 + N_SMALL) + [any_space()] * (N_FRONT_OUT - N_SMALL),
        scratch_shapes=[pltpu.VMEM(s, BF16) for s in weights]
        + [pltpu.VMEM(bits + (16, 128), BF16)]
        + [
            pltpu.SemaphoreType.DMA((UNITS + 1, 5)),
            pltpu.SemaphoreType.DMA((UNITS + 1, 5)),
            pltpu.SemaphoreType.DMA((8,)),
        ]
        + front_scratch(rows, width),
        compiler_params=pltpu.CompilerParams(
            collective_id=1, has_side_effects=True, vmem_limit_bytes=VMEM_LIMIT
        ),
        name="gather_front",
    )(*inputs, packed, *shards)
    return result[0].reshape(512, 2048), result[1].reshape(512, 2048), result[2], result[4:]


def front_kernel(*refs):
    inputs, vec_ref, in_b = refs[:7], refs[7], refs[8]
    sources = dict(zip("scio", refs[9:13], strict=True))
    outs, scratch = refs[13 : 13 + N_FRONT_OUT], refs[13 + N_FRONT_OUT :]

    def weight(kind, i):
        part = slice(512 * i, 512 * i + 512)
        return sources[kind][part, :] if kind == "o" else sources[kind][:, part]

    run_front(inputs, weight, lambda kind, i: True, vec_ref, in_b, outs, scratch, [])


def front_only(inputs, vec, in_b, weights):
    rows, width = inputs[0].shape
    return pl.pallas_call(
        front_kernel,
        out_shape=front_outs(rows, width),
        in_specs=[whole(None)] * 13,
        out_specs=[whole(None)] * N_SMALL + [any_space()] * (N_FRONT_OUT - N_SMALL),
        scratch_shapes=front_scratch(rows, width),
        compiler_params=pltpu.CompilerParams(vmem_limit_bytes=VMEM_LIMIT),
        name="front",
    )(*inputs, vec, in_b, *weights)


def normalize(summed):
    center = summed - jnp.mean(summed, axis=-1, keepdims=True)
    spread = jnp.mean(center * center, axis=-1, keepdims=True)
    inverse = lax.rsqrt(spread + EPSILON)
    return center * inverse, inverse


def normalize_back(grad, gain, normal, inverse):
    scaled = grad * gain
    mean = jnp.mean(scaled, axis=-1, keepdims=True)
    along = jnp.mean(scaled * normal, axis=-1, keepdims=True)
    return inverse * (scaled - mean - normal * along)


def column_sum(value):
    return jnp.sum(value, axis=0, keepdims=True)


def gelu_and_slope(hidden):
    phi = 0.5 + 0.5 * lax.erf(hidden * (0.5 ** 0.5))
    bell = jnp.exp(-0.5 * hidden * hidden)
    return hidden * phi, phi + hidden * (bell * 0.3989422804014327)


def row_delta(grad, mixed):
    head = lax.broadcasted_iota(jnp.int32, (16, 512), 0)
    lane = lax.broadcasted_iota(jnp.int32, (16, 512), 1)
    pick = jnp.where(lane // 64 == head, 1.0, 0.0).astype(BF16)
    product = grad.astype(F32) * mixed.astype(F32)
    high = product.astype(BF16)
    low = (product - high.astype(F32)).astype(BF16)
    return (dot_nt(pick, high) + dot_nt(pick, low))[:HEADS, :]


MADE = 7
READY = UNITS - MADE


def rear(inputs, r, vec, vec_grad, made, scratch, arrived, put, emit):
    x_ref, m_ref, seg, pad, mseg, mpad = inputs
    (column, bias, delta, dqt, dk, dv, grad4, query4, prob, slant) = scratch
    w_s, w_c, d_sums = r["w_s"], r["w_c"], r["d_second"]
    blocks = x_ref.shape[0] // BLOCK

    def add_vec(index, value):
        vec_grad[index : index + 1, :] += value

    def unit(index, left, right):
        made[index] = dot_tn(left[...], right[...]).astype(BF16).reshape(made.shape[1:])

    def lower(i, dq_low, dk_low, dv_low, q_row, v_row):
        rows = span(i, 1)
        query = (dqt[:, rows] * 0.125).astype(BF16).T
        value = dv[rows, :].astype(BF16)
        dq_low[rows, :] = query
        dk_low[rows, :] = dk[rows, :].astype(BF16)
        dv_low[rows, :] = value
        add_vec(q_row, column_sum(query.astype(F32)))
        add_vec(v_row, column_sum(value.astype(F32)))

    yield ("need", arrived("cq", "cqt", "ck", "ckt", "cv", "g", "gt"))
    key_columns(mseg, mpad, column)
    dk[...] = jnp.zeros_like(dk)
    dv[...] = jnp.zeros_like(dv)
    for qb in range(blocks):
        for kb in range(0, blocks, 2):
            mask_rows(bias, column, seg, qb, kb, 2, False)
            yield from attend_rows_back(2, kb, qb, r["cq"], r["cqt"], r["ck"], r["ckt"], r["cv"], r["g"], r["gt"],
                                        r["clse"], r["cdelta"], bias, dqt, dk, dv, grad4, query4, prob, slant, kb == 0)
    dcq, dck, dcv = r["cq"], r["ck"], r["cv"]
    for i in range(blocks):
        lower(i, dcq, dck, dcv, CROSS_Q_B, CROSS_V_B)
        yield ("cost", 0.3)
    yield ("need", arrived("first_low", "w_c", "d_second", "first_sum", "w_s", "mixed"))
    for index, (left, right) in enumerate(((m_ref, dck), (m_ref, dcv), (r["first_low"], dcq))):
        unit(index, left, right)
        yield ("cost", 0.7)
        yield ("add", put(index))
    low, grad, gradt = r["g"], r["first_low"], r["gt"]
    for i in range(blocks):
        rows = span(i, 1)
        normal, inverse = normalize(r["first_sum"][rows, :])
        back = d_sums[rows, :] + dot_nt(dcq[rows, :], w_c[:, 0:512])
        add_vec(NORM1_G, column_sum(back * normal))
        add_vec(NORM1_B, column_sum(back))
        d_sum = normalize_back(back, vec[NORM1_G : NORM1_G + 1, :], normal, inverse)
        add_vec(SELF_O_B, column_sum(d_sum))
        d_sums[rows, :] = d_sum
        sum_low = d_sum.astype(BF16)
        low[rows, :] = sum_low
        yield ("cost", 0.4)
        dck[rows, :] = (
            dot_nt(dck[rows, :], w_c[:, 512:1024]) + dot_nt(dcv[rows, :], w_c[:, 1024:1536])
        ).astype(BF16)
        mix_grad = dot_nt(sum_low, w_s[:, 1536:2048]).astype(BF16)
        grad[rows, :] = mix_grad
        gradt[:, rows] = mix_grad.T
        delta[:, rows] = row_delta(mix_grad, r["mixed"][rows, :])
        yield ("cost", 0.7)
    emit(1, dck)
    unit(3, r["mixed"], low)
    yield ("cost", 0.7)
    yield ("add", put(3))
    yield ("need", arrived("q", "qt", "k", "kt", "v"))
    key_columns(seg, pad, column)
    dk[...] = jnp.zeros_like(dk)
    dv[...] = jnp.zeros_like(dv)
    for qb in range(blocks):
        kb, count = document_blocks(qb)
        mask_rows(bias, column, seg, qb, kb, count, True)
        yield from attend_rows_back(count, kb, qb, r["q"], r["qt"], r["k"], r["kt"], r["v"], grad, gradt, r["lse"],
                                    delta, bias, dqt, dk, dv, grad4, query4, prob, slant)
    dq_low, dk_low, dv_low = grad, low, dcv
    for i in range(blocks):
        lower(i, dq_low, dk_low, dv_low, SELF_Q_B, SELF_V_B)
        yield ("cost", 0.3)
    for index, right in ((4, dq_low), (5, dk_low), (6, dv_low)):
        unit(index, x_ref, right)
        yield ("cost", 0.7)
        yield ("add", put(index))
    yield ("add", put(MADE))
    for i in range(blocks):
        rows = span(i, 1)
        dq_low[rows, :] = (
            d_sums[rows, :]
            + dot_nt(dq_low[rows, :], w_s[:, 0:512])
            + dot_nt(dk_low[rows, :], w_s[:, 512:1024])
            + dot_nt(dv_low[rows, :], w_s[:, 1024:1536])
        ).astype(BF16)
        yield ("cost", 0.6)
    emit(0, dq_low)


def emitter(outs, sem):
    copies = []

    def emit(index, ref):
        copy = pltpu.make_async_copy(ref, outs[index], sem.at[index])
        copy.start()
        copies.append(copy)

    return emit, copies


def rear_scratch(rows, width):
    wide = (rows, width)
    return [
        pltpu.VMEM((rows, 128), F32),
        pltpu.VMEM((3 * BLOCK, BLOCK), F32),
        pltpu.VMEM((HEADS, rows), F32),
        pltpu.VMEM((width, rows), F32),
        pltpu.VMEM(wide, F32),
        pltpu.VMEM(wide, F32),
        pltpu.VMEM((2, 4 * BLOCK, 256), BF16),
        pltpu.VMEM((2, 4 * BLOCK, 256), BF16),
        pltpu.VMEM((3 * BLOCK, HEADS * BLOCK), BF16),
        pltpu.VMEM((3 * BLOCK, HEADS * BLOCK), BF16),
    ]


REAR_IN = ("cq", "cqt", "ck", "ckt", "cv", "g", "gt", "first_low", "w_c", "d_second", "first_sum", "w_s", "mixed",
           "q", "qt", "k", "kt", "v")
REAR_SMALL = ("lse", "clse", "cdelta")
SCATTER_START, SCATTER_STEP, SCATTER_MADE_STEP, SCATTER_LAST_STEP = 3.0, 6.0, 6.0, 3.0


def rear_inputs(late_in, late, sem):
    copies = {n: pltpu.make_async_copy(late_in[i], late[i], sem.at[i]) for i, n in enumerate(REAR_IN)}
    for copy in copies.values():
        copy.start()

    def arrived(*names):
        def check():
            for name in names:
                copies[name].wait()
            return True

        return check

    return dict(zip(REAR_IN, late, strict=True)), arrived


def scatter_kernel(*refs):
    inputs, small, vec, vec_in, in_b_grad, ready = refs[:6], refs[6:9], refs[9], refs[10], refs[11], refs[12]
    count = len(REAR_IN)
    late_in = refs[13 : 13 + count]
    sums, vec_sums = refs[15 + count : 17 + count]
    rest = refs[17 + count :]
    (vec_grad, made, held, in0, in1, in2, in3, in4, g_v, v0, v1, v2, v3, v4, send, recv, keep, late_sem, out_sem) = rest[
        count : count + 19
    ]
    emit, emitted = emitter(refs[13 + count : 15 + count], out_sem)
    r, arrived = rear_inputs(late_in, rest[:count], late_sem)
    r.update(zip(REAR_SMALL, small, strict=True))
    vec_grad[...] = vec_in[...]
    d, f, me = place()
    greet(d, f)
    inbox = (in0, in1, in2, in3, in4)
    vec_inbox = (v0, v1, v2, v3, v4)
    bits5 = (2,) * 5

    def order(u):
        return tuple(reversed(ORDERS["A" if u == UNITS else SCATTER_ORDERS[u]]))

    def copy(u, s):
        bits = order(u)
        gone = bits[:s]
        if u == UNITS:
            index = tuple(me[b] if b in gone else 1 - me[b] if b == bits[s] else slice(None) for b in BITS)
            source, target = g_v.at[index], vec_inbox[s]
        elif s == 0:
            index = (slice(None),) * 4 + (1 - me["c"],)
            source = ready.at[(u,) + index] if u < READY else made.at[(u - READY,) + index]
            target = in0.at[u]
        else:
            index = tuple(me[b] if b in gone else 1 - me[b] if b == bits[s] else slice(None) for b in BITS[:4])
            source, target = held.at[(u,) + index], inbox[s].at[u]
        return pltpu.make_async_remote_copy(
            src_ref=source,
            dst_ref=target,
            send_sem=send.at[u, s],
            recv_sem=recv.at[u, s],
            device_id=partner(bits[s], d, f),
            device_id_type=MESH,
        )

    def own_half(u):
        index = (u,) + (slice(None),) * 4 + (me["c"],)
        return pltpu.make_async_copy(ready.at[index], held.at[u], keep.at[u])

    def add(u, s):
        gone = order(u)[: s + 1]
        if u == UNITS:
            index = tuple(me[b] if b in gone else slice(None) for b in BITS)
            g_v[index] = g_v[index] + vec_inbox[s][...]
        elif s == 0:
            if u < READY:
                own_half(u).wait()
                mine = held[u]
            else:
                mine = made[(u - READY,) + (slice(None),) * 4 + (me["c"],)]
            held[u] = mine + in0[u]
        else:
            index = (u,) + tuple(me[b] if b in gone else slice(None) for b in BITS[:4])
            if s == 4:
                sums[u] = held[index].astype(F32) + in4[u].astype(F32)
            else:
                held[index] = held[index] + inbox[s][u]

    def step(u, s):
        if s == 0 and u < READY:
            own_half(u).start()
        if s == 0 and u == UNITS:
            g_v[...] = pack_vectors(vec_grad[...], in_b_grad[...]).reshape(bits5 + (16, 128))
        if s > 0:
            copy(u, s - 1).wait_recv()
            add(u, s - 1)
        if s < 5:
            copy(u, s).start()

    def steps(u, start, each):
        return [(start + each * s, u, partial(step, u, s)) for s in range(6)]

    events = []
    for u in range(READY):
        events += steps(u, SCATTER_START * u, SCATTER_STEP)

    def put(index):
        each = SCATTER_LAST_STEP if index > 3 else SCATTER_MADE_STEP
        return steps(UNITS if index == MADE else READY + index, 0.0, each)

    merge(events, rear(inputs, r, vec, vec_grad, made, rest[count + 19 :], arrived, put, emit))
    for u in range(UNITS + 1):
        for s in range(5):
            copy(u, s).wait_send()
    vec_sums[...] = g_v[tuple(me[b] for b in BITS)]
    for item in emitted:
        item.wait()


def scatter_rear(inputs, small, vec, vec_grad, in_b_grad, ready, late):
    rows, width = inputs[0].shape
    bits = (2,) * 5
    unit = (16, 512)
    vec_unit = (16, 128)
    boxes = [(UNITS,) + (2,) * (4 - s) + unit for s in range(5)]
    return pl.pallas_call(
        scatter_kernel,
        out_shape=[jax.ShapeDtypeStruct((rows, width), BF16)] * 2
        + [
            jax.ShapeDtypeStruct((UNITS,) + unit, F32),
            jax.ShapeDtypeStruct(vec_unit, F32),
        ],
        in_specs=[whole(None)] * 12 + [any_space()] * (1 + len(late)),
        out_specs=[any_space()] * 2 + [whole(None)] * 2,
        scratch_shapes=[pltpu.VMEM(b.shape, b.dtype) for b in late]
        + [pltpu.VMEM((16, 512), F32)]
        + [pltpu.VMEM((MADE,) + bits + unit, BF16), pltpu.VMEM((UNITS,) + (2,) * 4 + unit, BF16)]
        + [pltpu.VMEM(b, BF16) for b in boxes]
        + [pltpu.VMEM(bits + vec_unit, F32)]
        + [pltpu.VMEM((2,) * (4 - s) + vec_unit, F32) for s in range(5)]
        + [
            pltpu.SemaphoreType.DMA((UNITS + 1, 5)),
            pltpu.SemaphoreType.DMA((UNITS + 1, 5)),
            pltpu.SemaphoreType.DMA((READY,)),
            pltpu.SemaphoreType.DMA((len(late),)),
            pltpu.SemaphoreType.DMA((2,)),
        ]
        + rear_scratch(rows, width),
        compiler_params=pltpu.CompilerParams(
            collective_id=2, has_side_effects=True, vmem_limit_bytes=VMEM_LIMIT
        ),
        name="scatter_rear",
    )(*inputs, *small, vec, vec_grad, in_b_grad, ready.reshape((READY,) + bits + unit), *late)


def rear_kernel(*refs):
    inputs, small, vec, vec_in = refs[:6], refs[6:9], refs[9], refs[10]
    count = len(REAR_IN)
    vec_grad, made = refs[13 + count : 15 + count]
    rest = refs[15 + count :]
    emit, emitted = emitter(refs[11 + count : 13 + count], rest[count + 1])
    r, arrived = rear_inputs(refs[11 : 11 + count], rest[:count], rest[count])
    r.update(zip(REAR_SMALL, small, strict=True))
    vec_grad[...] = vec_in[...]
    for kind, value in rear(inputs, r, vec, vec_grad, made, rest[count + 2 :], arrived, lambda i: None, emit):
        if kind == "need":
            value()
    for item in emitted:
        item.wait()


def rear_only(inputs, small, vec, vec_grad, late):
    rows, width = inputs[0].shape
    return pl.pallas_call(
        rear_kernel,
        out_shape=[jax.ShapeDtypeStruct((rows, width), BF16)] * 2
        + [
            jax.ShapeDtypeStruct((16, 512), F32),
            jax.ShapeDtypeStruct((MADE, 32, 16, 512), BF16),
        ],
        in_specs=[whole(None)] * 11 + [any_space()] * len(late),
        out_specs=[any_space()] * 2 + [whole(None)] * 2,
        scratch_shapes=[pltpu.VMEM(b.shape, b.dtype) for b in late]
        + [pltpu.SemaphoreType.DMA((len(late),)), pltpu.SemaphoreType.DMA((2,))]
        + rear_scratch(rows, width),
        compiler_params=pltpu.CompilerParams(vmem_limit_bytes=VMEM_LIMIT),
        name="rear",
    )(*inputs, *small, vec, vec_grad, *late)


def pack_vectors(vec_grad, in_b_grad):
    row = lax.broadcasted_iota(jnp.int32, (32, 16, 512), 0)
    col = lax.broadcasted_iota(jnp.int32, (32, 16, 512), 2)
    own = jnp.where(row == col // 16, jnp.broadcast_to(vec_grad[None], (32, 16, 512)), 0.0)
    column = lax.broadcasted_iota(jnp.int32, (512, 128), 0)
    lane = lax.broadcasted_iota(jnp.int32, (512, 128), 1)
    pick = jnp.where((lane == column % 16) & (lane < 16), 1.0, 0.0).astype(BF16)
    packed = dot(own.reshape(512, 512).astype(BF16), pick)
    row = lax.broadcasted_iota(jnp.int32, (32, 2048), 0)
    col = lax.broadcasted_iota(jnp.int32, (32, 2048), 1)
    own = jnp.where(row == col // 64, jnp.broadcast_to(in_b_grad, (32, 2048)), 0.0).astype(BF16)
    column = lax.broadcasted_iota(jnp.int32, (2048, 128), 0)
    lane = lax.broadcasted_iota(jnp.int32, (2048, 128), 1)
    pick = jnp.where((lane == column % 64) & (lane < 64), 1.0, 0.0).astype(BF16)
    wide = dot(own, pick).astype(BF16)
    target = lax.broadcasted_iota(jnp.int32, (512, 32), 0)
    device = lax.broadcasted_iota(jnp.int32, (512, 32), 1)
    choose = jnp.where(target == device * 16 + FFN_IN_B, 1.0, 0.0).astype(BF16)
    return packed + dot(choose, wide)


def unpack_kernel(sums, vec_sums, *refs):
    held, kept, outs = refs[:3], refs[3:6], refs[6:]
    matrices, vectors = outs[:10], outs[10:]
    for source, target in zip(held, kept, strict=True):
        target[...] = source[...]
    for i, u in enumerate((13, 14, 15, 12, 11, 9, 10, 8)):
        matrices[i][...] = sums[u]
    for u in range(4):
        matrices[8][:, 512 * u : 512 * u + 512] = sums[u]
        matrices[9][16 * u : 16 * u + 16, :] = sums[4 + u]
    for i in range(13):
        vectors[i][...] = vec_sums[i : i + 1, 0:16]
    vectors[13][...] = vec_sums[FFN_IN_B : FFN_IN_B + 1, 0:64]


def unpack(sums, vec_sums, held):
    shapes = [(16, 512)] * 8 + [(16, 2048), (64, 512)] + [(1, 16)] * 13 + [(1, 64)]
    return pl.pallas_call(
        unpack_kernel,
        out_shape=[jax.ShapeDtypeStruct(h.shape, h.dtype) for h in held]
        + [jax.ShapeDtypeStruct(s, F32) for s in shapes],
        in_specs=[whole(None)] * 5,
        out_specs=[whole(None)] * (3 + len(shapes)),
        name="unpack",
    )(sums, vec_sums, *held)


def local(
    tokens, memory, token_seg, token_pad, memory_seg, memory_pad, out_grad,
    self_q_w, self_q_b, self_k_w, self_v_w, self_v_b, self_o_w, self_o_b, norm1_gain, norm1_bias,
    cross_q_w, cross_q_b, cross_k_w, cross_v_w, cross_v_b, cross_o_w, cross_o_b, norm2_gain, norm2_bias,
    ffn_in_w, ffn_in_b, ffn_out_w, ffn_out_b, norm3_gain, norm3_bias, *, ring,
):
    vectors = (self_q_b, self_v_b, self_o_b, norm1_gain, norm1_bias, cross_q_b, cross_v_b, cross_o_b,
               norm2_gain, norm2_bias, ffn_out_b, norm3_gain, norm3_bias)
    shards = (self_q_w, self_k_w, self_v_w, self_o_w, cross_q_w, cross_k_w, cross_v_w, cross_o_w,
              ffn_in_w, ffn_out_w)
    inputs = (tokens, memory, token_seg, token_pad, memory_seg, memory_pad, out_grad)
    if ring:
        packed = jnp.concatenate(
            [
                jnp.pad(jnp.stack(vectors), ((0, 2), (0, 112))),
                jnp.pad(ffn_in_b.reshape(1, 64), ((0, 0), (0, 64))),
            ]
        )
        w_s, w_c, vec, fronts = gather_front(inputs, packed, shards)
    else:
        get = partial(lax.all_gather, axis_name=AXES, axis=0, tiled=True)
        full = [get(w) for w in shards]
        w_s, w_c = jnp.concatenate(full[:4], 1), jnp.concatenate(full[4:8], 1)
        vec = jnp.pad(jnp.stack([get(b) for b in vectors]).astype(F32), ((0, 3), (0, 0)))
        in_b = get(ffn_in_b).astype(F32).reshape(1, -1)
        fronts = front_only(inputs, vec, in_b, (w_s, w_c, full[8], full[9]))
    lse, clse, cdelta, layer_out, vec_grad, in_b_grad, ready = fronts[: N_SMALL + 1]
    a = dict(zip(FRONT + FRONT_WIDE, fronts[N_SMALL + 1 :], strict=True), w_s=w_s, w_c=w_c)
    late = [a[name] for name in REAR_IN]
    small = (lse, clse, cdelta)
    if ring:
        tokens_grad, memory_grad, sums, vec_sums = scatter_rear(
            inputs[:6], small, vec, vec_grad, in_b_grad, ready, late
        )
        results = unpack(sums, vec_sums, (layer_out, tokens_grad, memory_grad))
        layer_out, tokens_grad, memory_grad = results[:3]
        mats, vecs = results[3:13], [v.reshape(-1) for v in results[13:]]
    else:
        give = partial(lax.psum_scatter, axis_name=AXES, scatter_dimension=0, tiled=True)
        tokens_grad, memory_grad, vec_grad, made = rear_only(inputs[:6], small, vec, vec_grad, late)
        made = made.astype(F32).reshape(MADE, 512, 512)
        done = ready.astype(F32).reshape(9, 512, 512)
        in_w = done[:4].transpose(1, 0, 2).reshape(512, 2048)
        out_w = done[4:8].reshape(4, 32, 16, 512).transpose(1, 0, 2, 3).reshape(2048, 512)
        full = [made[4], made[5], made[6], made[3], made[2], made[0], made[1], done[8], in_w, out_w]
        mats = [give(g) for g in full]
        vecs = [give(vec_grad[i]) for i in range(13)] + [give(in_b_grad[0])]
    (g_sqw, g_skw, g_svw, g_sow, g_cqw, g_ckw, g_cvw, g_cow, g_iw, g_ow) = mats
    (g_sqb, g_svb, g_sob, g_n1g, g_n1b, g_cqb, g_cvb, g_cob, g_n2g, g_n2b, g_ob, g_n3g, g_n3b, g_ib) = vecs
    return (
        layer_out, tokens_grad, memory_grad,
        g_sqw, g_sqb, g_skw, g_svw, g_svb, g_sow, g_sob, g_n1g, g_n1b,
        g_cqw, g_cqb, g_ckw, g_cvw, g_cvb, g_cow, g_cob, g_n2g, g_n2b,
        g_iw, g_ib, g_ow, g_ob, g_n3g, g_n3b,
    )


def solution(mesh):
    ring = mesh.shape["dp"] == 8 and mesh.shape["fsdp"] == 4
    matrix, vector = P(AXES, None), P(AXES)
    return jax.shard_map(
        partial(local, ring=ring),
        mesh=mesh,
        in_specs=(
            (matrix,) * 7
            + (matrix, vector, matrix, matrix, vector, matrix, vector, vector, vector) * 2
            + (matrix, vector, matrix, vector, vector, vector)
        ),
        out_specs=(
            (matrix,) * 3
            + (matrix, vector, matrix, matrix, vector, matrix, vector, vector, vector) * 2
            + (matrix, vector, matrix, vector, vector, vector)
        ),
        check_vma=False,
    )
```

```python
from functools import partial

import jax
import jax.numpy as jnp
from jax import lax
from jax.experimental import pallas as pl
from jax.experimental.pallas import tpu as pltpu
from jax.sharding import PartitionSpec as P

HEADS = 8
EPSILON = 1e-05
MASKED = -1e30
AXES = ("dp", "fsdp")
MESH = pl.DeviceIdType.MESH
BF16 = jnp.bfloat16
F32 = jnp.float32
BLOCK = 256
VMEM_LIMIT = 62 << 20

(SELF_Q_B, SELF_V_B, SELF_O_B, NORM1_G, NORM1_B, CROSS_Q_B, CROSS_V_B, CROSS_O_B,
 NORM2_G, NORM2_B, FFN_OUT_B, NORM3_G, NORM3_B) = range(13)
FFN_IN_B = 15

BITS = ("zh", "zl", "y", "x", "c")
ORDERS = {
    "A": ("zh", "zl", "x", "y", "c"),
    "B": ("zh", "zl", "y", "x", "c"),
    "C": ("x", "zh", "zl", "y", "c"),
    "D": ("y", "zh", "zl", "x", "c"),
}
GATHER_ORDERS = "ABABABCDCDCDCDCD"
SCATTER_ORDERS = "ABCDABCDABCDABCD"
UNITS = 16


def dot(left, right):
    return jnp.dot(left, right, preferred_element_type=F32)


def dot_nt(left, right):
    return lax.dot_general(left, right, (((1,), (1,)), ((), ())), preferred_element_type=F32)


def dot_tn(left, right):
    return lax.dot_general(left, right, (((0,), (0,)), ((), ())), preferred_element_type=F32)


def rows_at(index, size):
    return pl.ds(pl.multiple_of(index * size, size), size)


def loop(low, high, body):
    def step(index, carry):
        body(index)
        return carry

    lax.fori_loop(low, high, step, 0)


def whole(shape):
    return pl.BlockSpec(memory_space=pltpu.VMEM)


def any_space():
    return pl.BlockSpec(memory_space=pl.ANY)


def place():
    d = lax.axis_index("dp")
    f = lax.axis_index("fsdp")
    return d, f, {"zh": d // 4, "zl": (d // 2) % 2, "y": d % 2, "x": f // 2, "c": f % 2}


def flip(value, mask):
    return value + mask - 2 * mask * ((value // mask) % 2)


def partner(bit, d, f):
    return {
        "zh": (flip(d, 4), f),
        "zl": (flip(d, 2), f),
        "y": (flip(d, 1), f),
        "x": (d, flip(f, 2)),
        "c": (d, flip(f, 1)),
    }[bit]


def greet(d, f):
    barrier = pltpu.get_barrier_semaphore()
    for bit in BITS:
        pl.semaphore_signal(barrier, inc=1, device_id=partner(bit, d, f), device_id_type=MESH)
    pl.semaphore_wait(barrier, len(BITS))


def spread_vectors(packed, vec_ref, in_b_ref):
    flat = packed.reshape(512, 128)
    lane = lax.broadcasted_iota(jnp.int32, (128, 512), 0)
    column = lax.broadcasted_iota(jnp.int32, (128, 512), 1)
    pick = jnp.where((lane == column % 16) & (lane < 16), 1.0, 0.0).astype(BF16)
    spread = dot(flat, pick)
    row = lax.broadcasted_iota(jnp.int32, (512, 512), 0)
    col = lax.broadcasted_iota(jnp.int32, (512, 512), 1)
    kept = jnp.where(row // 16 == col // 16, spread, 0.0)
    vec_ref[...] = jnp.sum(kept.reshape(32, 16, 512), axis=0)
    device = lax.broadcasted_iota(jnp.int32, (32, 512), 0)
    source = lax.broadcasted_iota(jnp.int32, (32, 512), 1)
    choose = jnp.where(source == device * 16 + FFN_IN_B, 1.0, 0.0).astype(BF16)
    own = dot(choose, flat).astype(BF16)
    lane = lax.broadcasted_iota(jnp.int32, (128, 2048), 0)
    column = lax.broadcasted_iota(jnp.int32, (128, 2048), 1)
    pick = jnp.where((lane == column % 64) & (lane < 64), 1.0, 0.0).astype(BF16)
    spread = dot(own, pick)
    row = lax.broadcasted_iota(jnp.int32, (32, 2048), 0)
    col = lax.broadcasted_iota(jnp.int32, (32, 2048), 1)
    in_b_ref[...] = jnp.sum(jnp.where(row == col // 64, spread, 0.0), axis=0, keepdims=True)


def merge(events, compute):
    events = sorted(events, key=lambda e: e[:2])
    now, waiting = 0.0, None
    while events or compute is not None:
        if waiting is not None and waiting():
            waiting = None
        blocked = waiting is not None or compute is None
        if events and (blocked or events[0][0] <= now):
            time, _, step = events.pop(0)
            if waiting is not None:
                now = max(now, time)
            step()
            continue
        try:
            kind, value = next(compute)
        except StopIteration:
            compute = None
            continue
        if kind == "cost":
            now += value
        elif kind == "need":
            waiting = value
        else:
            events += [(now + time, number, step) for time, number, step in value]
            events.sort(key=lambda e: e[:2])


def interleave(makers, skew):
    running = [maker() for maker in makers]
    done = [False] * len(running)
    time = 0
    while not all(done):
        for i, piece in enumerate(running):
            if not done[i] and time >= i * skew:
                asked = next(piece, True)
                done[i] = asked is True
                yield asked if isinstance(asked, tuple) else ("cost", 0.25)
        time += 1


def run_all(compute):
    for _ in compute:
        pass


def span(index, count):
    if isinstance(index, int):
        return slice(index * BLOCK, (index + count) * BLOCK)
    return pl.ds(pl.multiple_of(index * BLOCK, BLOCK), count * BLOCK)


def key_columns(seg_ref, pad_ref, column_ref):
    open_seg = jnp.where(pad_ref[...] == 0, seg_ref[...], -1).astype(F32)
    for i in range(seg_ref.shape[1] // 128):
        piece = jnp.broadcast_to(open_seg[:, 128 * i : 128 * i + 128], (128, 128)).T
        column_ref[128 * i : 128 * i + 128, :] = piece


def mask_rows(bias_ref, column_ref, seg_ref, qb, kb, count, causal):
    query = seg_ref[:, span(qb, 1)].astype(F32)
    column = column_ref[span(kb, count), :]
    allowed = jnp.concatenate([column] * (BLOCK // 128), axis=1) == query
    if causal:
        shape = (count * BLOCK, BLOCK)
        key_pos = kb * BLOCK + lax.broadcasted_iota(jnp.int32, shape, 0)
        query_pos = qb * BLOCK + lax.broadcasted_iota(jnp.int32, shape, 1)
        allowed = (allowed & (key_pos < query_pos)) | (key_pos == query_pos)
    bias_ref[0 : count * BLOCK, :] = jnp.where(allowed, 0.0, MASKED)


def own_lanes(value, head):
    lane = lax.broadcasted_iota(jnp.int32, value.shape, 1)
    return jnp.where(lane // 64 == head, value, jnp.zeros_like(value))


def attend_rows(count, kb, qb, qt_ref, k_ref, vt_ref, bias_ref, turned_ref, lse_ref, prob_ref, out_ref):
    rows, keys, size = span(qb, 1), span(kb, count), count * BLOCK

    def scores(h):
        part = slice(64 * h, 64 * h + 64)
        return dot(k_ref[keys, part], qt_ref[part, rows])

    def spot(h):
        return (slice(0, size), slice(BLOCK * h, BLOCK * h + BLOCK))

    def product(h, total):
        part = slice(64 * h, 64 * h + 64)
        turned_ref[part, :] = dot(vt_ref[part, keys], prob_ref[spot(h)]) * (1.0 / total)

    held = {h: scores(h) for h in range(2)}
    pending = []
    for h in range(HEADS):
        if h + 2 < HEADS:
            held[h + 2] = scores(h + 2)
        if len(pending) >= 5:
            product(*pending.pop(0))
        score = held.pop(h) + bias_ref[0:size, :]
        top = jnp.max(score, axis=0, keepdims=True)
        prob = jnp.exp(score - top)
        total = jnp.sum(prob, axis=0, keepdims=True)
        prob_ref[spot(h)] = prob.astype(BF16)
        lse_ref[h : h + 1, rows] = top + jnp.log(total)
        pending.append((h, total))
        yield ("cost", 0.1 * count)
    for item in pending:
        product(*item)
    out_ref[rows, :] = turned_ref[...].astype(BF16).T
    yield ("cost", 0.3)


def attend_rows_back(count, kb, qb, q_ref, qt_ref, k_ref, kt_ref, v_ref, g_ref, gt_ref, lse_ref, delta_ref, bias_ref,
                     dqt_ref, dk_ref, dv_ref, grad_ref, query_ref, prob_ref, slant_ref, fresh=True):
    rows, keys, size = span(qb, 1), span(kb, count), count * BLOCK

    def scores(h):
        part = slice(64 * h, 64 * h + 64)
        return (dot(k_ref[keys, part], qt_ref[part, rows]), dot(v_ref[keys, part], gt_ref[part, rows]))

    for slab in range(2):
        lanes = slice(256 * slab, 256 * slab + 256)
        for j in range(4):
            here = slice(BLOCK * j, BLOCK * j + BLOCK)
            grad_ref[slab, here, :] = own_lanes(g_ref[rows, lanes], j)
            query_ref[slab, here, :] = own_lanes(q_ref[rows, lanes], j)

    def tail(slab):
        lanes = slice(256 * slab, 256 * slab + 256)
        four = slice(4 * BLOCK * slab, 4 * BLOCK * slab + 4 * BLOCK)
        dv_ref[keys, lanes] += dot(prob_ref[0:size, four], grad_ref[slab])
        dk_ref[keys, lanes] += dot(slant_ref[0:size, four], query_ref[slab])
        for h in range(4 * slab, 4 * slab + 4):
            part = slice(64 * h, 64 * h + 64)
            product = dot(kt_ref[part, keys], slant_ref[0:size, BLOCK * h : BLOCK * h + BLOCK])
            dqt_ref[part, rows] = product if fresh else dqt_ref[part, rows] + product

    held = {h: scores(h) for h in range(2)}
    for h in range(HEADS):
        if h + 2 < HEADS:
            held[h + 2] = scores(h + 2)
        if h == 6:
            tail(0)
        score, grad = held.pop(h)
        mine, here = slice(h, h + 1), slice(BLOCK * h, BLOCK * h + BLOCK)
        prob = jnp.exp(score + bias_ref[0:size, :] - lse_ref[mine, rows])
        prob_ref[0:size, here] = prob.astype(BF16)
        slant_ref[0:size, here] = (prob * (grad - delta_ref[mine, rows])).astype(BF16)
        yield ("cost", 0.17 * count)
    tail(1)
    yield ("cost", 0.1)


def document_blocks(qb):
    first = max(0, (qb * BLOCK - 511) // BLOCK)
    return first, qb + 1 - first


FRONT = ("q", "qt", "k", "kt", "v", "mixed", "first_low", "cq", "cqt", "ck", "ckt", "cv", "g", "gt")
FRONT_WIDE = ("first_sum", "d_second")
TURNED = ("qt", "kt", "cqt", "ckt", "gt")
FFN_SKEW = 3


def front(inputs, weight, need, vec_ref, in_b, a, t, outs, put):
    x_ref, m_ref, seg, pad, mseg, mpad, out_grad = inputs
    lse, clse, delta, layer_out, vec_grad, in_b_grad, ready = outs
    blocks = x_ref.shape[0] // BLOCK
    vt, column, bias, turned, active = t["vt"], t["column"], t["bias"], t["turned"], t["active"]
    first_sum = a["first_sum"]

    def vector(index):
        return vec_ref[index : index + 1, :]

    def add_vec(index, value):
        vec_grad[index : index + 1, :] += value

    def project(source, kind, index, bias_row, straight, turned_to, scale=None):
        yield ("need", lambda: need(kind, index))
        for i in range(blocks):
            rows = span(i, 1)
            value = dot(source[rows, :], weight(kind, index))
            if bias_row is not None:
                value = value + vector(bias_row)
            value = value.astype(BF16)
            if scale is not None:
                value = value * scale
            if straight is not None:
                straight[rows, :] = value
            if turned_to is not None:
                turned_to[:, rows] = value.T
            yield ("cost", 0.25)

    vec_grad[...] = jnp.zeros_like(vec_grad)
    in_b_grad[...] = jnp.zeros_like(in_b_grad)
    key_columns(seg, pad, column)
    yield ("need", lambda: need("v", 0))
    yield from project(x_ref, "s", 0, SELF_Q_B, a["q"], a["qt"], 0.125)
    yield from project(x_ref, "s", 1, None, a["k"], a["kt"])
    yield from project(x_ref, "s", 2, SELF_V_B, a["v"], vt)
    put("q", "qt", "k", "kt", "v")
    for qb in range(blocks):
        kb, count = document_blocks(qb)
        mask_rows(bias, column, seg, qb, kb, count, True)
        yield from attend_rows(count, kb, qb, a["qt"], a["k"], vt, bias, turned, lse, active, a["mixed"])
    put("mixed")
    yield ("need", lambda: need("s", 3))
    for i in range(blocks):
        rows = span(i, 1)
        summed = x_ref[rows, :].astype(F32) + dot(a["mixed"][rows, :], weight("s", 3)) + vector(SELF_O_B)
        first_sum[rows, :] = summed
        normal, _ = normalize(summed)
        a["first_low"][rows, :] = (normal * vector(NORM1_G) + vector(NORM1_B)).astype(BF16)
        yield ("cost", 0.4)
    put("first_low", "first_sum")
    yield from project(m_ref, "c", 1, None, a["ck"], a["ckt"])
    yield from project(m_ref, "c", 2, CROSS_V_B, a["cv"], vt)
    put("ck", "ckt", "cv")
    yield from project(a["first_low"], "c", 0, CROSS_Q_B, a["cq"], a["cqt"], 0.125)
    put("cq", "cqt")
    key_columns(mseg, mpad, column)
    cmixed, second_low, d_low, slope, low_a = (t[n] for n in ("cmixed", "second_low", "d_low", "slope", "low_a"))
    for qb in range(blocks):
        mask_rows(bias, column, seg, qb, 0, blocks, False)
        yield from attend_rows(blocks, 0, qb, a["cqt"], a["ck"], vt, bias, turned, clse, active, cmixed)
    yield ("need", lambda: need("c", 3) and all(need("i", i) for i in range(4)))

    def ffn(i):
        rows = span(i, 1)
        normal1, _ = normalize(first_sum[rows, :])
        first_norm = normal1 * vector(NORM1_G) + vector(NORM1_B)
        summed = first_norm + dot(cmixed[rows, :], weight("c", 3)) + vector(CROSS_O_B)
        yield
        normal2, inverse2 = normalize(summed)
        second = normal2 * vector(NORM2_G) + vector(NORM2_B)
        low = second.astype(BF16)
        second_low[rows, :] = low
        third = second + vector(FFN_OUT_B)
        cols = [slice(512 * c, 512 * c + 512) for c in range(4)]

        def hidden(c):
            return dot(low, weight("i", c)) + in_b[:, cols[c]]

        def bend(c, value):
            act, slant = gelu_and_slope(value)
            active[rows, cols[c]] = act.astype(BF16)
            slope[rows, cols[c]] = slant.astype(BF16)

        held = [hidden(0), hidden(1)]
        yield
        bend(0, held[0])
        held.append(hidden(2))
        yield
        bend(1, held[1])
        held.append(hidden(3))
        yield
        if i == 0:
            yield ("need", lambda: all(need("o", u) for u in range(4)))
        third = third + dot(active[rows, cols[0]], weight("o", 0))
        bend(2, held[2])
        yield
        third = third + dot(active[rows, cols[1]], weight("o", 1))
        bend(3, held[3])
        yield
        third = third + dot(active[rows, cols[2]], weight("o", 2)) + dot(active[rows, cols[3]], weight("o", 3))
        yield
        normal3, inverse3 = normalize(third)
        layer_out[rows, :] = (normal3 * vector(NORM3_G) + vector(NORM3_B)).astype(BF16)
        grad = out_grad[rows, :].astype(F32)
        add_vec(NORM3_G, column_sum(grad * normal3))
        add_vec(NORM3_B, column_sum(grad))
        d_third = normalize_back(grad, vector(NORM3_G), normal3, inverse3)
        add_vec(FFN_OUT_B, column_sum(d_third))
        third_low = d_third.astype(BF16)
        d_low[rows, :] = third_low
        yield

        def pull(c):
            return dot_nt(third_low, weight("o", c))

        def straighten(c, value):
            d_hidden = (value * slope[rows, cols[c]].astype(F32)).astype(BF16)
            slope[rows, cols[c]] = d_hidden
            in_b_grad[:, cols[c]] += column_sum(d_hidden.astype(F32))

        held = [pull(0), pull(1)]
        yield
        straighten(0, held[0])
        held.append(pull(2))
        yield
        straighten(1, held[1])
        held.append(pull(3))
        yield
        back = d_third + dot_nt(slope[rows, cols[0]], weight("i", 0))
        straighten(2, held[2])
        yield
        back = back + dot_nt(slope[rows, cols[1]], weight("i", 1))
        straighten(3, held[3])
        yield
        back = back + dot_nt(slope[rows, cols[2]], weight("i", 2)) + dot_nt(slope[rows, cols[3]], weight("i", 3))
        yield
        add_vec(NORM2_G, column_sum(back * normal2))
        add_vec(NORM2_B, column_sum(back))
        d_sum = normalize_back(back, vector(NORM2_G), normal2, inverse2)
        add_vec(CROSS_O_B, column_sum(d_sum))
        a["d_second"][rows, :] = d_sum
        sum_low = d_sum.astype(BF16)
        low_a[rows, :] = sum_low
        yield
        mix_grad = dot_nt(sum_low, weight("c", 3)).astype(BF16)
        a["g"][rows, :] = mix_grad
        a["gt"][:, rows] = mix_grad.T
        delta[:, rows] = row_delta(mix_grad, cmixed[rows, :])
        yield

    yield from interleave([partial(ffn, i) for i in range(blocks)], FFN_SKEW)
    put("d_second", "g", "gt")
    for c in range(4):
        cols = slice(512 * c, 512 * c + 512)
        ready[c] = dot_tn(second_low[...], slope[:, cols]).astype(BF16).reshape(32, 16, 512)
        value = dot_tn(active[:, cols], d_low[...]).astype(BF16).reshape(8, 4, 16, 512)
        for u in range(4):
            ready[4 + u, 8 * c : 8 * c + 8] = value[:, u]
    ready[8] = dot_tn(cmixed[...], low_a[...]).astype(BF16).reshape(32, 16, 512)


def front_shape(name, rows, width):
    return (width, rows) if name in TURNED else (rows, width)


FRONT_SCRATCH = ("vt", "column", "bias", "turned", "active", "cmixed", "second_low", "d_low", "slope", "low_a")


def front_scratch(rows, width):
    wide = (rows, width)
    return (
        [pltpu.VMEM(front_shape(name, rows, width), BF16) for name in FRONT]
        + [pltpu.VMEM(wide, F32) for _ in FRONT_WIDE]
        + [
            pltpu.SemaphoreType.DMA((len(FRONT) + len(FRONT_WIDE) + 1,)),
            pltpu.VMEM((9, 32, 16, 512), BF16),
            pltpu.VMEM((width, rows), BF16),
            pltpu.VMEM((rows, 128), F32),
            pltpu.VMEM((rows, BLOCK), F32),
            pltpu.VMEM((width, BLOCK), F32),
            pltpu.VMEM((rows, 2048), BF16),
            pltpu.VMEM(wide, BF16),
            pltpu.VMEM(wide, BF16),
            pltpu.VMEM(wide, BF16),
            pltpu.VMEM((rows, 2048), BF16),
            pltpu.VMEM(wide, BF16),
        ]
    )


def front_outs(rows, width):
    rowwise = jax.ShapeDtypeStruct((HEADS, rows), F32)
    return (
        [rowwise] * 3
        + [
            jax.ShapeDtypeStruct((rows, width), BF16),
            jax.ShapeDtypeStruct((16, 512), F32),
            jax.ShapeDtypeStruct((1, 2048), F32),
            jax.ShapeDtypeStruct((9, 32, 16, 512), BF16),
        ]
        + [jax.ShapeDtypeStruct(front_shape(name, rows, width), BF16) for name in FRONT]
        + [jax.ShapeDtypeStruct((rows, width), F32) for _ in FRONT_WIDE]
    )


N_SMALL = 6
N_FRONT_OUT = N_SMALL + 1 + len(FRONT) + len(FRONT_WIDE)


def run_front(inputs, weight, need, vec_ref, in_b, outs, scratch, events):
    names = FRONT + FRONT_WIDE
    count = len(names)
    a = dict(zip(names, scratch[:count], strict=True))
    sem, ready = scratch[count : count + 2]
    t = dict(zip(FRONT_SCRATCH, scratch[count + 2 :], strict=True))
    copies = {n: pltpu.make_async_copy(a[n], outs[N_SMALL + 1 + i], sem.at[i]) for i, n in enumerate(names)}

    def put(*which):
        for name in which:
            copies[name].start()

    merge(events, front(inputs, weight, need, vec_ref, in_b, a, t, [*outs[:N_SMALL], ready], put))
    last = pltpu.make_async_copy(ready, outs[N_SMALL], sem.at[count])
    last.start()
    for name in names:
        copies[name].wait()
    last.wait()


UNIT_PLACES = (
    [("s", 0), ("s", 1), ("s", 2), ("s", 3), ("c", 1), ("c", 2), ("c", 0), ("c", 3)]
    + [("i", i) for i in range(4)]
    + [("o", i) for i in range(4)]
)
GATHER_START, GATHER_STEP, GATHER_FIRST_STEP, GATHER_PAUSE = 1.1, 4.4, 2.5, 0.0


def gather_kernel(*refs):
    inputs, packed, shards, in_b_row = refs[:7], refs[7], refs[8:18], refs[18]
    o_s, o_c, vec_out, in_b = refs[19:23]
    outs = refs[23 : 23 + N_FRONT_OUT]
    rest = refs[23 + N_FRONT_OUT :]
    b_s, b_c, b_i, b_o, b_v = rest[:5]
    send, recv, keep = rest[5:8]
    d, f, me = place()
    own = tuple(me[bit] for bit in BITS)
    for i in range(4):
        b_s[own + (slice(None), slice(512 * i, 512 * i + 512))] = shards[i][...]
        b_c[own + (slice(None), slice(512 * i, 512 * i + 512))] = shards[4 + i][...]
    b_i[own] = shards[8][...]
    b_o[own] = shards[9][...]
    row = lax.broadcasted_iota(jnp.int32, (16, 128), 0)
    last = jnp.concatenate([in_b_row[...].astype(F32), jnp.zeros((1, 64), F32)], axis=1)
    b_v[own] = jnp.where(row == FFN_IN_B, last, packed[...].astype(F32)).astype(BF16)
    greet(d, f)

    buffers = {"s": b_s, "c": b_c, "i": b_i, "o": b_o}
    targets = {"s": o_s, "c": o_c}
    finished = set()

    def part(u, index):
        kind, i = UNIT_PLACES[u]
        if kind == "o":
            return index + (slice(16 * i, 16 * i + 16), slice(None))
        return index + (slice(None), slice(512 * i, 512 * i + 512))

    def copy(u, s):
        order = ORDERS["A" if u == UNITS else GATHER_ORDERS[u]]
        have = order[:s]
        index = tuple(slice(None) if bit in have else me[bit] for bit in BITS)
        buffer = b_v
        if u < UNITS:
            index, buffer = part(u, index), buffers[UNIT_PLACES[u][0]]
        return pltpu.make_async_remote_copy(
            src_ref=buffer.at[index],
            dst_ref=buffer.at[index],
            send_sem=send.at[u, s],
            recv_sem=recv.at[u, s],
            device_id=partner(order[s], d, f),
            device_id_type=MESH,
        )

    def store(u):
        kind = UNIT_PLACES[u][0]
        index = part(u, (slice(None),) * 5)
        return pltpu.make_async_copy(buffers[kind].at[index], targets[kind].at[index], keep.at[u])

    def step(u, s):
        if s > 0:
            copy(u, s - 1).wait_recv()
        if s < 5:
            copy(u, s).start()
            return
        if u == UNITS:
            pl.when(d >= 0)(lambda: spread_vectors(b_v[...].reshape(32, 16, 128), vec_out, in_b))
        elif u < 8:
            store(u).start()
        finished.add(u)

    events = []
    for u in range(UNITS + 1):
        start = 0.0 if u == UNITS else 0.1 + u * GATHER_START + (GATHER_PAUSE if u > 3 else 0.0)
        each = GATHER_FIRST_STEP if u == UNITS or u < 4 else GATHER_STEP
        events += [(start + each * s, u, partial(step, u, s)) for s in range(6)]

    unit_of = {place: u for u, place in enumerate(UNIT_PLACES)}
    unit_of["v", 0] = UNITS

    def weight(kind, i):
        if kind == "o":
            return b_o[i // 2, i % 2].reshape(512, 512)
        return buffers[kind][:, :, :, :, :, :, 512 * i : 512 * i + 512].reshape(512, 512)

    run_front(inputs, weight, lambda kind, i: unit_of[kind, i] in finished, vec_out, in_b, outs, rest[8:], events)
    for u in range(UNITS + 1):
        for s in range(5):
            copy(u, s).wait_send()
        if u < 8:
            store(u).wait()


def gather_front(inputs, packed, shards, in_b_row):
    rows, width = inputs[0].shape
    bits = (2,) * 5
    weights = [bits + (16, 2048)] * 3 + [bits + (64, 512)]
    shapes = [jax.ShapeDtypeStruct(s, BF16) for s in weights[:2]]
    shapes += [jax.ShapeDtypeStruct((16, 512), F32), jax.ShapeDtypeStruct((1, 2048), F32)]
    shapes += front_outs(rows, width)
    result = pl.pallas_call(
        gather_kernel,
        out_shape=shapes,
        in_specs=[whole(None)] * 19,
        out_specs=[any_space()] * 2 + [whole(None)] * (2 + N_SMALL) + [any_space()] * (N_FRONT_OUT - N_SMALL),
        scratch_shapes=[pltpu.VMEM(s, BF16) for s in weights]
        + [pltpu.VMEM(bits + (16, 128), BF16)]
        + [
            pltpu.SemaphoreType.DMA((UNITS + 1, 5)),
            pltpu.SemaphoreType.DMA((UNITS + 1, 5)),
            pltpu.SemaphoreType.DMA((8,)),
        ]
        + front_scratch(rows, width),
        compiler_params=pltpu.CompilerParams(
            collective_id=1, has_side_effects=True, vmem_limit_bytes=VMEM_LIMIT
        ),
        name="gather_front",
    )(*inputs, packed, *shards, in_b_row)
    return result[0].reshape(512, 2048), result[1].reshape(512, 2048), result[2], result[4:]


def front_kernel(*refs):
    inputs, vec_ref, in_b = refs[:7], refs[7], refs[8]
    sources = dict(zip("scio", refs[9:13], strict=True))
    outs, scratch = refs[13 : 13 + N_FRONT_OUT], refs[13 + N_FRONT_OUT :]

    def weight(kind, i):
        part = slice(512 * i, 512 * i + 512)
        return sources[kind][part, :] if kind == "o" else sources[kind][:, part]

    run_front(inputs, weight, lambda kind, i: True, vec_ref, in_b, outs, scratch, [])


def front_only(inputs, vec, in_b, weights):
    rows, width = inputs[0].shape
    return pl.pallas_call(
        front_kernel,
        out_shape=front_outs(rows, width),
        in_specs=[whole(None)] * 13,
        out_specs=[whole(None)] * N_SMALL + [any_space()] * (N_FRONT_OUT - N_SMALL),
        scratch_shapes=front_scratch(rows, width),
        compiler_params=pltpu.CompilerParams(vmem_limit_bytes=VMEM_LIMIT),
        name="front",
    )(*inputs, vec, in_b, *weights)


def normalize(summed):
    center = summed - jnp.mean(summed, axis=-1, keepdims=True)
    spread = jnp.mean(center * center, axis=-1, keepdims=True)
    inverse = lax.rsqrt(spread + EPSILON)
    return center * inverse, inverse


def normalize_back(grad, gain, normal, inverse):
    scaled = grad * gain
    mean = jnp.mean(scaled, axis=-1, keepdims=True)
    along = jnp.mean(scaled * normal, axis=-1, keepdims=True)
    return inverse * (scaled - mean - normal * along)


def column_sum(value):
    return jnp.sum(value, axis=0, keepdims=True)


def gelu_and_slope(hidden):
    phi = 0.5 + 0.5 * lax.erf(hidden * (0.5 ** 0.5))
    bell = jnp.exp(-0.5 * hidden * hidden)
    return hidden * phi, phi + hidden * (bell * 0.3989422804014327)


def row_delta(grad, mixed):
    head = lax.broadcasted_iota(jnp.int32, (16, 512), 0)
    lane = lax.broadcasted_iota(jnp.int32, (16, 512), 1)
    pick = jnp.where(lane // 64 == head, 1.0, 0.0).astype(BF16)
    product = grad.astype(F32) * mixed.astype(F32)
    high = product.astype(BF16)
    low = (product - high.astype(F32)).astype(BF16)
    return (dot_nt(pick, high) + dot_nt(pick, low))[:HEADS, :]


MADE = 7
READY = UNITS - MADE


def rear(inputs, r, vec, vec_grad, made, scratch, arrived, put, emit):
    x_ref, m_ref, seg, pad, mseg, mpad = inputs
    (column, bias, delta, dqt, dk, dv, grad4, query4, prob, slant) = scratch
    w_s, w_c, d_sums = r["w_s"], r["w_c"], r["d_second"]
    blocks = x_ref.shape[0] // BLOCK

    def add_vec(index, value):
        vec_grad[index : index + 1, :] += value

    def unit(index, left, right):
        made[index] = dot_tn(left[...], right[...]).astype(BF16).reshape(made.shape[1:])

    def lower(i, dq_low, dk_low, dv_low, q_row, v_row):
        rows = span(i, 1)
        query = (dqt[:, rows] * 0.125).astype(BF16).T
        value = dv[rows, :].astype(BF16)
        dq_low[rows, :] = query
        dk_low[rows, :] = dk[rows, :].astype(BF16)
        dv_low[rows, :] = value
        add_vec(q_row, column_sum(query.astype(F32)))
        add_vec(v_row, column_sum(value.astype(F32)))

    yield ("need", arrived("cq", "cqt", "ck", "ckt", "cv", "g", "gt"))
    key_columns(mseg, mpad, column)
    dk[...] = jnp.zeros_like(dk)
    dv[...] = jnp.zeros_like(dv)
    for qb in range(blocks):
        for kb in range(0, blocks, 2):
            mask_rows(bias, column, seg, qb, kb, 2, False)
            yield from attend_rows_back(2, kb, qb, r["cq"], r["cqt"], r["ck"], r["ckt"], r["cv"], r["g"], r["gt"],
                                        r["clse"], r["cdelta"], bias, dqt, dk, dv, grad4, query4, prob, slant, kb == 0)
    dcq, dck, dcv = r["cq"], r["ck"], r["cv"]
    for i in range(blocks):
        lower(i, dcq, dck, dcv, CROSS_Q_B, CROSS_V_B)
        yield ("cost", 0.3)
    yield ("need", arrived("first_low", "w_c", "d_second", "first_sum", "w_s", "mixed"))
    for index, (left, right) in enumerate(((m_ref, dck), (m_ref, dcv), (r["first_low"], dcq))):
        unit(index, left, right)
        yield ("cost", 0.7)
        yield ("add", put(index))
    low, grad, gradt = r["g"], r["first_low"], r["gt"]
    for i in range(blocks):
        rows = span(i, 1)
        normal, inverse = normalize(r["first_sum"][rows, :])
        back = d_sums[rows, :] + dot_nt(dcq[rows, :], w_c[:, 0:512])
        add_vec(NORM1_G, column_sum(back * normal))
        add_vec(NORM1_B, column_sum(back))
        d_sum = normalize_back(back, vec[NORM1_G : NORM1_G + 1, :], normal, inverse)
        add_vec(SELF_O_B, column_sum(d_sum))
        d_sums[rows, :] = d_sum
        sum_low = d_sum.astype(BF16)
        low[rows, :] = sum_low
        yield ("cost", 0.4)
        dck[rows, :] = (
            dot_nt(dck[rows, :], w_c[:, 512:1024]) + dot_nt(dcv[rows, :], w_c[:, 1024:1536])
        ).astype(BF16)
        mix_grad = dot_nt(sum_low, w_s[:, 1536:2048]).astype(BF16)
        grad[rows, :] = mix_grad
        gradt[:, rows] = mix_grad.T
        delta[:, rows] = row_delta(mix_grad, r["mixed"][rows, :])
        yield ("cost", 0.7)
    emit(1, dck)
    unit(3, r["mixed"], low)
    yield ("cost", 0.7)
    yield ("add", put(3))
    yield ("need", arrived("q", "qt", "k", "kt", "v"))
    key_columns(seg, pad, column)
    dk[...] = jnp.zeros_like(dk)
    dv[...] = jnp.zeros_like(dv)
    for qb in range(blocks):
        kb, count = document_blocks(qb)
        mask_rows(bias, column, seg, qb, kb, count, True)
        yield from attend_rows_back(count, kb, qb, r["q"], r["qt"], r["k"], r["kt"], r["v"], grad, gradt, r["lse"],
                                    delta, bias, dqt, dk, dv, grad4, query4, prob, slant)
    dq_low, dk_low, dv_low = grad, low, dcv
    for i in range(blocks):
        lower(i, dq_low, dk_low, dv_low, SELF_Q_B, SELF_V_B)
        yield ("cost", 0.3)
    for index, right in ((4, dq_low), (5, dk_low), (6, dv_low)):
        unit(index, x_ref, right)
        yield ("cost", 0.7)
        yield ("add", put(index))
    yield ("add", put(MADE))
    for i in range(blocks):
        rows = span(i, 1)
        dq_low[rows, :] = (
            d_sums[rows, :]
            + dot_nt(dq_low[rows, :], w_s[:, 0:512])
            + dot_nt(dk_low[rows, :], w_s[:, 512:1024])
            + dot_nt(dv_low[rows, :], w_s[:, 1024:1536])
        ).astype(BF16)
        yield ("cost", 0.6)
    emit(0, dq_low)


def emitter(outs, sem):
    copies = []

    def emit(index, ref):
        copy = pltpu.make_async_copy(ref, outs[index], sem.at[index])
        copy.start()
        copies.append(copy)

    return emit, copies


def rear_scratch(rows, width):
    wide = (rows, width)
    return [
        pltpu.VMEM((rows, 128), F32),
        pltpu.VMEM((3 * BLOCK, BLOCK), F32),
        pltpu.VMEM((HEADS, rows), F32),
        pltpu.VMEM((width, rows), F32),
        pltpu.VMEM(wide, F32),
        pltpu.VMEM(wide, F32),
        pltpu.VMEM((2, 4 * BLOCK, 256), BF16),
        pltpu.VMEM((2, 4 * BLOCK, 256), BF16),
        pltpu.VMEM((3 * BLOCK, HEADS * BLOCK), BF16),
        pltpu.VMEM((3 * BLOCK, HEADS * BLOCK), BF16),
    ]


REAR_IN = ("cq", "cqt", "ck", "ckt", "cv", "g", "gt", "first_low", "w_c", "d_second", "first_sum", "w_s", "mixed",
           "q", "qt", "k", "kt", "v")
REAR_SMALL = ("lse", "clse", "cdelta")
SCATTER_START, SCATTER_STEP, SCATTER_MADE_STEP, SCATTER_LAST_STEP = 3.5, 7.0, 7.0, 3.0


def rear_inputs(late_in, late, sem):
    copies = {n: pltpu.make_async_copy(late_in[i], late[i], sem.at[i]) for i, n in enumerate(REAR_IN)}
    for copy in copies.values():
        copy.start()

    def arrived(*names):
        def check():
            for name in names:
                copies[name].wait()
            return True

        return check

    return dict(zip(REAR_IN, late, strict=True)), arrived


def scatter_kernel(*refs):
    inputs, small, vec, vec_in, in_b_grad, ready = refs[:6], refs[6:9], refs[9], refs[10], refs[11], refs[12]
    count = len(REAR_IN)
    late_in = refs[13 : 13 + count]
    sums, vec_sums = refs[15 + count : 17 + count]
    rest = refs[17 + count :]
    (vec_grad, made, held, in0, in1, in2, in3, in4, g_v, v0, v1, v2, v3, v4, send, recv, keep, late_sem, out_sem) = rest[
        count : count + 19
    ]
    emit, emitted = emitter(refs[13 + count : 15 + count], out_sem)
    r, arrived = rear_inputs(late_in, rest[:count], late_sem)
    r.update(zip(REAR_SMALL, small, strict=True))
    vec_grad[...] = vec_in[...]
    d, f, me = place()
    greet(d, f)
    inbox = (in0, in1, in2, in3, in4)
    vec_inbox = (v0, v1, v2, v3, v4)
    bits5 = (2,) * 5

    def order(u):
        return tuple(reversed(ORDERS["A" if u == UNITS else SCATTER_ORDERS[u]]))

    def copy(u, s):
        bits = order(u)
        gone = bits[:s]
        if u == UNITS:
            index = tuple(me[b] if b in gone else 1 - me[b] if b == bits[s] else slice(None) for b in BITS)
            source, target = g_v.at[index], vec_inbox[s]
        elif s == 0:
            index = (slice(None),) * 4 + (1 - me["c"],)
            source = ready.at[(u,) + index] if u < READY else made.at[(u - READY,) + index]
            target = in0.at[u]
        else:
            index = tuple(me[b] if b in gone else 1 - me[b] if b == bits[s] else slice(None) for b in BITS[:4])
            source, target = held.at[(u,) + index], inbox[s].at[u]
        return pltpu.make_async_remote_copy(
            src_ref=source,
            dst_ref=target,
            send_sem=send.at[u, s],
            recv_sem=recv.at[u, s],
            device_id=partner(bits[s], d, f),
            device_id_type=MESH,
        )

    def own_half(u):
        index = (u,) + (slice(None),) * 4 + (me["c"],)
        return pltpu.make_async_copy(ready.at[index], held.at[u], keep.at[u])

    def add(u, s):
        gone = order(u)[: s + 1]
        if u == UNITS:
            index = tuple(me[b] if b in gone else slice(None) for b in BITS)
            g_v[index] = g_v[index] + vec_inbox[s][...]
        elif s == 0:
            if u < READY:
                own_half(u).wait()
                mine = held[u]
            else:
                mine = made[(u - READY,) + (slice(None),) * 4 + (me["c"],)]
            held[u] = mine + in0[u]
        else:
            index = (u,) + tuple(me[b] if b in gone else slice(None) for b in BITS[:4])
            if s == 4:
                sums[u] = held[index].astype(F32) + in4[u].astype(F32)
            else:
                held[index] = held[index] + inbox[s][u]

    def step(u, s):
        if s == 0 and u < READY:
            own_half(u).start()
        if s == 0 and u == UNITS:
            g_v[...] = pack_vectors(vec_grad[...], in_b_grad[...]).reshape(bits5 + (16, 128))
        if s > 0:
            copy(u, s - 1).wait_recv()
            add(u, s - 1)
        if s < 5:
            copy(u, s).start()

    def steps(u, start, each):
        return [(start + each * s, u, partial(step, u, s)) for s in range(6)]

    events = []
    for u in range(READY):
        events += steps(u, SCATTER_START * u, SCATTER_STEP)

    def put(index):
        each = SCATTER_LAST_STEP if index > 3 else SCATTER_MADE_STEP
        return steps(UNITS if index == MADE else READY + index, 0.0, each)

    merge(events, rear(inputs, r, vec, vec_grad, made, rest[count + 19 :], arrived, put, emit))
    for u in range(UNITS + 1):
        for s in range(5):
            copy(u, s).wait_send()
    vec_sums[...] = g_v[tuple(me[b] for b in BITS)]
    for item in emitted:
        item.wait()


def scatter_rear(inputs, small, vec, vec_grad, in_b_grad, ready, late):
    rows, width = inputs[0].shape
    bits = (2,) * 5
    unit = (16, 512)
    vec_unit = (16, 128)
    boxes = [(UNITS,) + (2,) * (4 - s) + unit for s in range(5)]
    return pl.pallas_call(
        scatter_kernel,
        out_shape=[jax.ShapeDtypeStruct((rows, width), BF16)] * 2
        + [
            jax.ShapeDtypeStruct((UNITS,) + unit, F32),
            jax.ShapeDtypeStruct(vec_unit, F32),
        ],
        in_specs=[whole(None)] * 12 + [any_space()] * (1 + len(late)),
        out_specs=[any_space()] * 2 + [whole(None)] * 2,
        scratch_shapes=[pltpu.VMEM(b.shape, b.dtype) for b in late]
        + [pltpu.VMEM((16, 512), F32)]
        + [pltpu.VMEM((MADE,) + bits + unit, BF16), pltpu.VMEM((UNITS,) + (2,) * 4 + unit, BF16)]
        + [pltpu.VMEM(b, BF16) for b in boxes]
        + [pltpu.VMEM(bits + vec_unit, F32)]
        + [pltpu.VMEM((2,) * (4 - s) + vec_unit, F32) for s in range(5)]
        + [
            pltpu.SemaphoreType.DMA((UNITS + 1, 5)),
            pltpu.SemaphoreType.DMA((UNITS + 1, 5)),
            pltpu.SemaphoreType.DMA((READY,)),
            pltpu.SemaphoreType.DMA((len(late),)),
            pltpu.SemaphoreType.DMA((2,)),
        ]
        + rear_scratch(rows, width),
        compiler_params=pltpu.CompilerParams(
            collective_id=2, has_side_effects=True, vmem_limit_bytes=VMEM_LIMIT
        ),
        name="scatter_rear",
    )(*inputs, *small, vec, vec_grad, in_b_grad, ready.reshape((READY,) + bits + unit), *late)


def rear_kernel(*refs):
    inputs, small, vec, vec_in = refs[:6], refs[6:9], refs[9], refs[10]
    count = len(REAR_IN)
    vec_grad, made = refs[13 + count : 15 + count]
    rest = refs[15 + count :]
    emit, emitted = emitter(refs[11 + count : 13 + count], rest[count + 1])
    r, arrived = rear_inputs(refs[11 : 11 + count], rest[:count], rest[count])
    r.update(zip(REAR_SMALL, small, strict=True))
    vec_grad[...] = vec_in[...]
    for kind, value in rear(inputs, r, vec, vec_grad, made, rest[count + 2 :], arrived, lambda i: None, emit):
        if kind == "need":
            value()
    for item in emitted:
        item.wait()


def rear_only(inputs, small, vec, vec_grad, late):
    rows, width = inputs[0].shape
    return pl.pallas_call(
        rear_kernel,
        out_shape=[jax.ShapeDtypeStruct((rows, width), BF16)] * 2
        + [
            jax.ShapeDtypeStruct((16, 512), F32),
            jax.ShapeDtypeStruct((MADE, 32, 16, 512), BF16),
        ],
        in_specs=[whole(None)] * 11 + [any_space()] * len(late),
        out_specs=[any_space()] * 2 + [whole(None)] * 2,
        scratch_shapes=[pltpu.VMEM(b.shape, b.dtype) for b in late]
        + [pltpu.SemaphoreType.DMA((len(late),)), pltpu.SemaphoreType.DMA((2,))]
        + rear_scratch(rows, width),
        compiler_params=pltpu.CompilerParams(vmem_limit_bytes=VMEM_LIMIT),
        name="rear",
    )(*inputs, *small, vec, vec_grad, *late)


def pack_vectors(vec_grad, in_b_grad):
    row = lax.broadcasted_iota(jnp.int32, (32, 16, 512), 0)
    col = lax.broadcasted_iota(jnp.int32, (32, 16, 512), 2)
    own = jnp.where(row == col // 16, jnp.broadcast_to(vec_grad[None], (32, 16, 512)), 0.0)
    column = lax.broadcasted_iota(jnp.int32, (512, 128), 0)
    lane = lax.broadcasted_iota(jnp.int32, (512, 128), 1)
    pick = jnp.where((lane == column % 16) & (lane < 16), 1.0, 0.0).astype(BF16)
    packed = dot(own.reshape(512, 512).astype(BF16), pick)
    row = lax.broadcasted_iota(jnp.int32, (32, 2048), 0)
    col = lax.broadcasted_iota(jnp.int32, (32, 2048), 1)
    own = jnp.where(row == col // 64, jnp.broadcast_to(in_b_grad, (32, 2048)), 0.0).astype(BF16)
    column = lax.broadcasted_iota(jnp.int32, (2048, 128), 0)
    lane = lax.broadcasted_iota(jnp.int32, (2048, 128), 1)
    pick = jnp.where((lane == column % 64) & (lane < 64), 1.0, 0.0).astype(BF16)
    wide = dot(own, pick).astype(BF16)
    target = lax.broadcasted_iota(jnp.int32, (512, 32), 0)
    device = lax.broadcasted_iota(jnp.int32, (512, 32), 1)
    choose = jnp.where(target == device * 16 + FFN_IN_B, 1.0, 0.0).astype(BF16)
    return packed + dot(choose, wide)


def unpack_kernel(sums, vec_sums, *refs):
    held, kept, outs = refs[:3], refs[3:6], refs[6:]
    matrices, vectors = outs[:10], outs[10:]
    for source, target in zip(held, kept, strict=True):
        target[...] = source[...]
    for i, u in enumerate((13, 14, 15, 12, 11, 9, 10, 8)):
        matrices[i][...] = sums[u]
    for u in range(4):
        matrices[8][:, 512 * u : 512 * u + 512] = sums[u]
        matrices[9][16 * u : 16 * u + 16, :] = sums[4 + u]
    for i in range(13):
        vectors[i][...] = vec_sums[i : i + 1, 0:16]
    vectors[13][...] = vec_sums[FFN_IN_B : FFN_IN_B + 1, 0:64]


def unpack(sums, vec_sums, held):
    shapes = [(16, 512)] * 8 + [(16, 2048), (64, 512)] + [(1, 16)] * 13 + [(1, 64)]
    return pl.pallas_call(
        unpack_kernel,
        out_shape=[jax.ShapeDtypeStruct(h.shape, h.dtype) for h in held]
        + [jax.ShapeDtypeStruct(s, F32) for s in shapes],
        in_specs=[whole(None)] * 5,
        out_specs=[whole(None)] * (3 + len(shapes)),
        name="unpack",
    )(sums, vec_sums, *held)


def local(
    tokens, memory, token_seg, token_pad, memory_seg, memory_pad, out_grad,
    self_q_w, self_q_b, self_k_w, self_v_w, self_v_b, self_o_w, self_o_b, norm1_gain, norm1_bias,
    cross_q_w, cross_q_b, cross_k_w, cross_v_w, cross_v_b, cross_o_w, cross_o_b, norm2_gain, norm2_bias,
    ffn_in_w, ffn_in_b, ffn_out_w, ffn_out_b, norm3_gain, norm3_bias, *, ring,
):
    vectors = (self_q_b, self_v_b, self_o_b, norm1_gain, norm1_bias, cross_q_b, cross_v_b, cross_o_b,
               norm2_gain, norm2_bias, ffn_out_b, norm3_gain, norm3_bias)
    shards = (self_q_w, self_k_w, self_v_w, self_o_w, cross_q_w, cross_k_w, cross_v_w, cross_o_w,
              ffn_in_w, ffn_out_w)
    inputs = (tokens, memory, token_seg, token_pad, memory_seg, memory_pad, out_grad)
    if ring:
        packed = jnp.pad(jnp.stack(vectors), ((0, 3), (0, 112)))
        w_s, w_c, vec, fronts = gather_front(inputs, packed, shards, ffn_in_b.reshape(1, 64))
    else:
        get = partial(lax.all_gather, axis_name=AXES, axis=0, tiled=True)
        full = [get(w) for w in shards]
        w_s, w_c = jnp.concatenate(full[:4], 1), jnp.concatenate(full[4:8], 1)
        vec = jnp.pad(jnp.stack([get(b) for b in vectors]).astype(F32), ((0, 3), (0, 0)))
        in_b = get(ffn_in_b).astype(F32).reshape(1, -1)
        fronts = front_only(inputs, vec, in_b, (w_s, w_c, full[8], full[9]))
    lse, clse, cdelta, layer_out, vec_grad, in_b_grad, ready = fronts[: N_SMALL + 1]
    a = dict(zip(FRONT + FRONT_WIDE, fronts[N_SMALL + 1 :], strict=True), w_s=w_s, w_c=w_c)
    late = [a[name] for name in REAR_IN]
    small = (lse, clse, cdelta)
    if ring:
        tokens_grad, memory_grad, sums, vec_sums = scatter_rear(
            inputs[:6], small, vec, vec_grad, in_b_grad, ready, late
        )
        results = unpack(sums, vec_sums, (layer_out, tokens_grad, memory_grad))
        layer_out, tokens_grad, memory_grad = results[:3]
        mats, vecs = results[3:13], [v.reshape(-1) for v in results[13:]]
    else:
        give = partial(lax.psum_scatter, axis_name=AXES, scatter_dimension=0, tiled=True)
        tokens_grad, memory_grad, vec_grad, made = rear_only(inputs[:6], small, vec, vec_grad, late)
        made = made.astype(F32).reshape(MADE, 512, 512)
        done = ready.astype(F32).reshape(9, 512, 512)
        in_w = done[:4].transpose(1, 0, 2).reshape(512, 2048)
        out_w = done[4:8].reshape(4, 32, 16, 512).transpose(1, 0, 2, 3).reshape(2048, 512)
        full = [made[4], made[5], made[6], made[3], made[2], made[0], made[1], done[8], in_w, out_w]
        mats = [give(g) for g in full]
        vecs = [give(vec_grad[i]) for i in range(13)] + [give(in_b_grad[0])]
    (g_sqw, g_skw, g_svw, g_sow, g_cqw, g_ckw, g_cvw, g_cow, g_iw, g_ow) = mats
    (g_sqb, g_svb, g_sob, g_n1g, g_n1b, g_cqb, g_cvb, g_cob, g_n2g, g_n2b, g_ob, g_n3g, g_n3b, g_ib) = vecs
    return (
        layer_out, tokens_grad, memory_grad,
        g_sqw, g_sqb, g_skw, g_svw, g_svb, g_sow, g_sob, g_n1g, g_n1b,
        g_cqw, g_cqb, g_ckw, g_cvw, g_cvb, g_cow, g_cob, g_n2g, g_n2b,
        g_iw, g_ib, g_ow, g_ob, g_n3g, g_n3b,
    )


def solution(mesh):
    ring = mesh.shape["dp"] == 8 and mesh.shape["fsdp"] == 4
    matrix, vector = P(AXES, None), P(AXES)
    return jax.shard_map(
        partial(local, ring=ring),
        mesh=mesh,
        in_specs=(
            (matrix,) * 7
            + (matrix, vector, matrix, matrix, vector, matrix, vector, vector, vector) * 2
            + (matrix, vector, matrix, vector, vector, vector)
        ),
        out_specs=(
            (matrix,) * 3
            + (matrix, vector, matrix, matrix, vector, matrix, vector, vector, vector) * 2
            + (matrix, vector, matrix, vector, vector, vector)
        ),
        check_vma=False,
    )
```
